32 devices in a mesh: dp: 16 (over z, x, core), head: 2 (over y).
Axes of the slice: x: 2, y: 2, z: 4, core: 2. Of those that a mesh axis runs over, the one named last changes fastest.
Arguments:
- layer_input: bfloat16 [16384, 1024], P('dp', 'head'), may hold values from -6 to 6
- ln_gain: bfloat16 [1024], P('head'), may hold values from 0.5 to 1.5
- up_x_weight: bfloat16 [1024, 2048], P(None, 'head'), may hold values from -0.1875 to 0.1875
- up_z_weight: bfloat16 [1024, 2048], P(None, 'head'), may hold values from -0.1875 to 0.1875
- conv_weight: bfloat16 [4, 2048], P(None, 'head'), may hold values from -3 to 3
- conv_bias: bfloat16 [2048], P('head'), may hold values from -3 to 3
- query_weight: bfloat16 [4, 2048], P(None, 'head'), may hold values from -3 to 3
- key_weight: bfloat16 [4, 2048], P(None, 'head'), may hold values from -3 to 3
- value_weight: bfloat16 [4, 2048], P(None, 'head'), may hold values from -3 to 3
- gate_weight: bfloat16 [3, 2048, 8], P(None, 'head'), may hold values from -0.078125 to 0.078125
- forget_bias: bfloat16 [4], replicated, may hold values from 3 to 6
- norm_gain: bfloat16 [2048], P('head'), may hold values from 0.5 to 1.5
- skip_gain: bfloat16 [2048], P('head'), may hold values from 0.25 to 1.75
- down_weight: bfloat16 [2048, 1024], P('head'), may hold values from -0.25 to 0.25
- cotangent: bfloat16 [16384, 1024], P('dp', 'head'), may hold values from -6 to 6
Outputs:
- layer_output: bfloat16 [16384, 1024], P('dp', 'head')
- input_grad: float32 [16384, 1024], P('dp', 'head')
- grad_ln_gain: float32 [1024], P('head')
- grad_up_x: float32 [1024, 2048], P(None, 'head')
- grad_up_z: float32 [1024, 2048], P(None, 'head')
- grad_conv_weight: float32 [4, 2048], P(None, 'head')
- grad_conv_bias: float32 [2048], P('head')
- grad_query_weight: float32 [4, 2048], P(None, 'head')
- grad_key_weight: float32 [4, 2048], P(None, 'head')
- grad_value_weight: float32 [4, 2048], P(None, 'head')
- grad_gate_weight: float32 [3, 2048, 8], P(None, 'head')
- grad_forget_bias: float32 [4], replicated
- grad_norm_gain: float32 [2048], P('head')
- grad_skip_gain: float32 [2048], P('head')
- grad_down: float32 [2048, 1024], P('head')
The draws below stay inside these ranges and needn't reach their ends.
All inputs are finite; a program needn't handle non-finite values.
Results may differ from the reference program's by a relative error of at most 0.019.
The reference program's roundings to bfloat16 on the way (of `normed` and `gated`) count: a program that leaves them out, or rounds other values in their place, can miss the bound.
Values may be sent and summed in bfloat16 or wider, within the bound.
No kernel may reach another device: no remote copies, remote signals or barrier semaphores. Data moves between devices by JAX's collectives and lax.ppermute only.
A program may use at most 384 MiB of HBM per device.

```python
import jax
import jax.numpy as jnp
from jax import lax

D = 1024
INNER = 2048
HEADS = 4
KERNEL = 4
BLOCKSIZE = 4
SEQ = 1024
TOKENS = 16384
N_DP = 16


def block_scale(own_key, dims, pieces, smallest, top_value):
    level = 1.0
    for position, parts in pieces:
        draws = jax.random.uniform(jax.random.fold_in(jax.random.fold_in(own_key, 6), position), (parts,), jnp.float32, smallest / len(pieces), top_value / len(pieces))
        level = level * jnp.repeat(jnp.exp(draws), dims[position] // parts).reshape((-1,) + (1,) * (len(dims) - 1 - position))
    return level


def scatter_about(key, dims, deviation, reach, split=(), held_as=jnp.bfloat16):
    drawn = deviation * jax.random.normal(key, dims, jnp.float32)
    if split:
        drawn = drawn * block_scale(key, dims, split, -0.22, 0.18)
    return jnp.clip(drawn, -reach, reach).astype(held_as)


def setup_inputs(seed: int = 0) -> dict:
    key_of = jax.random.split(jax.random.key(seed), 16)
    return {
        "layer_input": scatter_about(key_of[0], (TOKENS, D), 1.0, 6.0, ((0, 16), (1, 2))),
        "ln_gain": jnp.clip(1.0 + 0.1 * jax.random.normal(key_of[1], (D,), jnp.float32), 0.5, 1.5).astype(jnp.bfloat16),
        "up_x_weight": scatter_about(key_of[2], (D, INNER), D ** -0.5, 0.1875, ((1, 2),)),
        "up_z_weight": scatter_about(key_of[3], (D, INNER), D ** -0.5, 0.1875, ((1, 2),)),
        "conv_weight": scatter_about(key_of[4], (KERNEL, INNER), KERNEL ** -0.5, 3.0, ((1, 2),)),
        "conv_bias": scatter_about(key_of[5], (INNER,), 0.5, 3.0, ((0, 2),)),
        "query_weight": scatter_about(key_of[6], (BLOCKSIZE, INNER), BLOCKSIZE ** -0.5, 3.0, ((1, 2),)),
        "key_weight": scatter_about(key_of[7], (BLOCKSIZE, INNER), BLOCKSIZE ** -0.5, 3.0, ((1, 2),)),
        "value_weight": scatter_about(key_of[8], (BLOCKSIZE, INNER), BLOCKSIZE ** -0.5, 3.0, ((1, 2),)),
        "gate_weight": scatter_about(key_of[9], (3, INNER, 2 * HEADS), (3 * INNER) ** -0.5, 0.078125, ((1, 2),)),
        "forget_bias": jnp.clip(jax.random.uniform(key_of[10], (HEADS,), jnp.float32, 3.0, 6.0), 3.0, 6.0).astype(jnp.bfloat16),
        "norm_gain": jnp.clip(1.0 + 0.1 * jax.random.normal(key_of[11], (INNER,), jnp.float32), 0.5, 1.5).astype(jnp.bfloat16),
        "skip_gain": jnp.clip(1.0 + 0.15 * jax.random.normal(key_of[12], (INNER,), jnp.float32), 0.25, 1.75).astype(jnp.bfloat16),
        "down_weight": scatter_about(key_of[13], (INNER, D), (INNER // 4) ** -0.5, 0.25, ((0, 2),)),
        "cotangent": scatter_about(key_of[14], (TOKENS, D), 1.0, 6.0, ((0, 16), (1, 2))),
    }


eps_norm = 1e-05
block_rows = 512
neg_big = -1e+30

@jax.custom_vjp
def low(v):
    return lax.optimization_barrier(v.astype(jnp.bfloat16)).astype(jnp.float32)

@jax.custom_vjp
def low_back(v):
    return v

def low_keep(v):
    return (low(v), None)

def low_pass(kept, grad):
    return (grad,)

def back_keep(v):
    return (v, None)

def back_low(kept, grad):
    return (low(grad),)
low.defvjp(low_keep, low_pass)
low_back.defvjp(back_keep, back_low)

def matmul(first, second):
    return jnp.dot(first, second, precision=lax.Precision.HIGHEST, preferred_element_type=jnp.float32)

def layer_norm(rows, gain):
    center = lax.optimization_barrier(jnp.mean(rows, axis=1, keepdims=True))
    spread = lax.optimization_barrier(jnp.mean(rows * rows, axis=1, keepdims=True)) - center * center
    return (rows - center) * lax.rsqrt(spread + eps_norm) * gain

def causal_conv(inputs, taps, bias_row):
    tap_count = taps.shape[0]
    length = inputs.shape[0]
    padded = jnp.pad(inputs, ((tap_count - 1, 0), (0, 0)))
    running = jnp.zeros_like(inputs) + bias_row
    for tap_index in range(tap_count):
        running = running + taps[tap_index] * padded[tap_index:tap_index + length]
    return running

def blockwise(inputs, taps):
    length, channels = inputs.shape
    tap_count = taps.shape[0]
    grouped = inputs.reshape(length, channels // tap_count, tap_count)
    mixer = taps.reshape(tap_count, channels // tap_count, tap_count)
    return jnp.einsum('sgj,jgi->sgi', grouped, mixer, precision=lax.Precision.HIGHEST).reshape(length, channels)

def head_block(carried_state, block_item):
    memory, normal, stabilizer = carried_state
    queries, key_rows, value_rows, inlet_gate, log_forget = block_item
    block_len = queries.shape[0]
    cumulative = jnp.cumsum(log_forget)
    running = cumulative[-1]
    causal = jnp.arange(block_len)[:, None] >= jnp.arange(block_len)[None, :]
    decay_log = jnp.where(causal, cumulative[:, None] - cumulative[None, :] + inlet_gate[None, :], neg_big)
    carried = cumulative + stabilizer
    stable = jnp.maximum(carried, lax.optimization_barrier(jnp.max(decay_log, axis=1)))
    weights = jnp.exp(decay_log - stable[:, None])
    scores = matmul(queries, key_rows.T) * weights
    carry_weight = jnp.exp(carried - stable)
    numerator = matmul(scores, value_rows) + matmul(queries, memory) * carry_weight[:, None]
    denominator = lax.optimization_barrier(jnp.sum(scores, axis=1)) + matmul(queries, normal) * carry_weight
    hidden = numerator / jnp.maximum(jnp.abs(denominator), jnp.exp(-stable))[:, None]
    fresh_log = running - cumulative + inlet_gate
    stab_next = jnp.maximum(running + stabilizer, jnp.max(fresh_log))
    keep_weight = jnp.exp(fresh_log - stab_next)
    weighted = key_rows * keep_weight[:, None]
    fade_factor = jnp.exp(running + stabilizer - stab_next)
    memory_next = memory * fade_factor + matmul(weighted.T, value_rows)
    normal_next = normal * fade_factor + lax.optimization_barrier(jnp.sum(weighted, axis=0))
    return ((memory_next, normal_next, stab_next), hidden)

def one_head(queries, key_rows, value_rows, inlet_gate, forget_gate):
    length, channels = queries.shape
    block_len = min(block_rows, length)
    block_count = length // block_len
    log_forget = jax.nn.log_sigmoid(forget_gate)
    queries = queries * channels ** (-0.5)
    block_items = (queries.reshape(block_count, block_len, channels), key_rows.reshape(block_count, block_len, channels), value_rows.reshape(block_count, block_len, channels), inlet_gate.reshape(block_count, block_len), log_forget.reshape(block_count, block_len))
    initial = (jnp.zeros((channels, channels), jnp.float32), jnp.zeros((channels,), jnp.float32), jnp.zeros((), jnp.float32))
    last_state, hidden = lax.scan(jax.checkpoint(head_block), initial, block_items)
    return hidden.reshape(length, channels)

def mlstm_heads(queries, key_rows, value_rows, inlet_gate, forget_gate):
    length = queries.shape[0]
    head_count = inlet_gate.shape[1]
    channels = queries.shape[1] // head_count

    def to_heads(values):
        return values.reshape(length, head_count, channels).transpose(1, 0, 2)
    hidden = jax.vmap(one_head)(to_heads(queries), to_heads(key_rows), to_heads(value_rows), inlet_gate.T, forget_gate.T)
    return hidden.transpose(1, 0, 2).reshape(length, head_count * channels)

def group_norm(hidden, gain, head_count):
    length = hidden.shape[0]
    grouped = hidden.reshape(length, head_count, -1)
    center = grouped - lax.optimization_barrier(jnp.mean(grouped, axis=2, keepdims=True))
    scaled = center * lax.rsqrt(lax.optimization_barrier(jnp.mean(center * center, axis=2, keepdims=True)) + eps_norm)
    return scaled.reshape(length, -1) * gain

def layer(rows, params):
    gain_ln, weight_upx, weight_upz, conv_taps, conv_offset, query_taps, key_taps, value_taps, gate_table, forget_offset, gain_norm, gain_skip, weight_down = params
    normed = low(layer_norm(rows, gain_ln))
    up_x = low_back(matmul(normed, weight_upx))
    up_z = low_back(matmul(normed, weight_upz))
    conv_out = jax.nn.silu(causal_conv(up_x, conv_taps, conv_offset))
    queries = low(blockwise(conv_out, query_taps))
    key_rows = low(blockwise(conv_out, key_taps))
    value_rows = low(blockwise(up_x, value_taps))
    gates = matmul(queries, gate_table[0]) + matmul(key_rows, gate_table[1]) + matmul(value_rows, gate_table[2])
    hidden = mlstm_heads(queries, key_rows, value_rows, gates[:, :HEADS], gates[:, HEADS:] + forget_offset)
    gated = low((group_norm(hidden, gain_norm, HEADS) + gain_skip * conv_out) * jax.nn.silu(up_z))
    return rows + matmul(gated, weight_down)

def add_up(first, second):
    return first + second

def reference(layer_input, ln_gain, up_x_weight, up_z_weight, conv_weight, conv_bias, query_weight, key_weight, value_weight, gate_weight, forget_bias, norm_gain, skip_gain, down_weight, cotangent):
    params = tuple((p.astype(jnp.float32) for p in (ln_gain, up_x_weight, up_z_weight, conv_weight, conv_bias, query_weight, key_weight, value_weight, gate_weight, forget_bias, norm_gain, skip_gain, down_weight)))
    seqs_in = layer_input.astype(jnp.float32).reshape(N_DP, SEQ, D)
    seqs_grad = cotangent.astype(jnp.float32).reshape(N_DP, SEQ, D)

    def one_sequence(totals, paired):
        rows, grads = paired
        output, pullback = jax.vjp(layer, rows, params)
        grad_rows, grad_params = pullback(grads)
        totals = jax.tree.map(add_up, totals, grad_params)
        return (totals, (output.astype(jnp.bfloat16), grad_rows))
    zeros = tuple((jnp.zeros_like(p) for p in params))
    totals, (outputs, grad_inputs) = lax.scan(one_sequence, zeros, (seqs_in, seqs_grad))
    return (outputs.reshape(TOKENS, D), grad_inputs.reshape(TOKENS, D), totals[0], totals[1], totals[2], totals[3], totals[4], totals[5], totals[6], totals[7], totals[8], totals[9], totals[10], totals[11], totals[12])
```

```python
from functools import partial

import jax
import jax.numpy as jnp
from jax import lax
from jax.experimental import pallas as pl
from jax.experimental.pallas import tpu as pltpu
from jax.sharding import PartitionSpec as P

eps_norm = 1e-05
group = 256
block = 256
b16 = jnp.bfloat16
f32 = jnp.float32


def dot_nn(first, second):
    return lax.dot_general(first, second, (((1,), (0,)), ((), ())), preferred_element_type=f32)


def dot_nt(first, second):
    return lax.dot_general(first, second, (((1,), (1,)), ((), ())), preferred_element_type=f32)


def dot_tn(first, second):
    return lax.dot_general(first, second, (((0,), (0,)), ((), ())), preferred_element_type=f32)


def sigmoid(values):
    return 0.5 * jnp.tanh(0.5 * values) + 0.5


def spec(shape, index_map):
    return pl.BlockSpec(shape, index_map)


def whole(shape):
    return pl.BlockSpec(shape, lambda *_: (0,) * len(shape))


def smem():
    return pl.BlockSpec(memory_space=pltpu.SMEM)


def shape_of(shape, dtype):
    return jax.ShapeDtypeStruct(shape, dtype)


def settings(mebibytes):
    return pltpu.CompilerParams(
        dimension_semantics=("arbitrary",), vmem_limit_bytes=mebibytes * 2**20
    )


def cost(micros):
    return pl.CostEstimate(
        flops=int(micros * 1.1e9), bytes_accessed=int(micros * 3.6e6), transcendentals=0
    )


def side_cols(side, width):
    return pl.ds(pl.multiple_of(side * width, width), width)


def spread_taps(taps):
    tap_count, width = taps.shape
    rows = lax.broadcasted_iota(jnp.int32, (width, width), 0) // tap_count
    cols = lax.broadcasted_iota(jnp.int32, (width, width), 1) // tap_count
    pair = jnp.concatenate([taps.astype(f32)] * (8 // tap_count), axis=0)
    full = jnp.concatenate([pair] * (width // 8), axis=0)
    return jnp.where(rows == cols, full, 0.0).astype(b16)


def gather_taps(dense, tap_count):
    width = dense.shape[0]
    rows = lax.broadcasted_iota(jnp.int32, (width, width), 0) // tap_count
    cols = lax.broadcasted_iota(jnp.int32, (width, width), 1) // tap_count
    kept = jnp.where(rows == cols, dense, 0.0)
    folded = jnp.sum(kept.reshape(width // 8, 8, width), axis=0)
    total = folded[:tap_count]
    for part in range(1, 8 // tap_count):
        total = total + folded[part * tap_count : (part + 1) * tap_count]
    return total


def row_stats(own, other):
    width = own.shape[1] + other.shape[1]
    total = jnp.sum(own, axis=1, keepdims=True) + jnp.sum(other, axis=1, keepdims=True)
    square = jnp.sum(own * own, axis=1, keepdims=True) + jnp.sum(
        other * other, axis=1, keepdims=True
    )
    center = total / width
    return center, lax.rsqrt(square / width - center * center + eps_norm)


def seat_rows(values, seats_ref, out_ref):
    seats = seats_ref.shape[0]
    height = values.shape[0] // seats
    for piece in range(seats):
        out_ref[pl.ds(pl.multiple_of(seats_ref[piece] * height, height), height), :] = values[
            piece * height : (piece + 1) * height
        ]


def front_kernel(
    side_ref,
    seats_ref,
    own_ref,
    other_ref,
    gain_own_ref,
    gain_other_ref,
    wx_ref,
    wz_ref,
    conv_ref,
    bias_ref,
    qw_ref,
    kw_ref,
    vw_ref,
    gate_ref,
    normed_ref,
    flipped_ref,
    upx_ref,
    upz_ref,
    conv_out_ref,
    slope_ref,
    q_ref,
    k_ref,
    v_ref,
    gates_ref,
    padded_ref,
):
    step = pl.program_id(0)
    side = side_ref[0]
    length, part = own_ref.shape
    tap_count = conv_ref.shape[0]

    @pl.when(step == 0)
    def _():
        for start in range(0, length, block):
            rows = pl.ds(start, block)
            own = own_ref[rows, :].astype(f32)
            other = other_ref[rows, :].astype(f32)
            center, scale = row_stats(own, other)
            normed_ref[rows, side_cols(side, part)] = (
                (own - center) * scale * gain_own_ref[...].astype(f32)
            ).astype(b16)
            normed_ref[rows, side_cols(1 - side, part)] = (
                (other - center) * scale * gain_other_ref[...].astype(f32)
            ).astype(b16)
        gates_ref[...] = jnp.zeros_like(gates_ref)
        padded_ref[pl.ds(0, 8), :] = jnp.zeros((8, group), f32)

    flip_rows = flipped_ref.shape[1]
    flat = normed_ref[pl.ds(pl.multiple_of(step * flip_rows, flip_rows), flip_rows), :].T
    seat_rows(flat, seats_ref, flipped_ref)
    upz_ref[...] = dot_nn(normed_ref[...], wz_ref[...]).astype(b16)
    upx = dot_nn(normed_ref[...], wx_ref[...])
    upx_b = upx.astype(b16)
    upx_ref[...] = upx_b
    padded_ref[pl.ds(8, length), :] = upx
    taps = conv_ref[...].astype(f32)
    pre = bias_ref[...].astype(f32) + taps[tap_count - 1 : tap_count] * upx
    for tap in range(tap_count - 1):
        pre = pre + taps[tap : tap + 1] * padded_ref[pl.ds(8 - (tap_count - 1 - tap), length), :]
    gate = sigmoid(pre)
    conv_out = pre * gate
    conv_b = conv_out.astype(b16)
    conv_out_ref[...] = conv_b
    slope_ref[...] = (gate + conv_out * (1.0 - gate)).astype(b16)
    conv_low = (conv_out - conv_b.astype(f32)).astype(b16)
    upx_low = (upx - upx_b.astype(f32)).astype(b16)
    qd, kd, vd = spread_taps(qw_ref[...]), spread_taps(kw_ref[...]), spread_taps(vw_ref[...])
    q_b = (dot_nn(conv_b, qd) + dot_nn(conv_low, qd)).astype(b16)
    k_b = (dot_nn(conv_b, kd) + dot_nn(conv_low, kd)).astype(b16)
    v_b = (dot_nn(upx_b, vd) + dot_nn(upx_low, vd)).astype(b16)
    q_ref[...] = q_b
    k_ref[...] = k_b
    v_ref[...] = v_b
    gates_ref[...] += (
        dot_nt(gate_ref[0], q_b) + dot_nt(gate_ref[1], k_b) + dot_nt(gate_ref[2], v_b)
    )


def front(side, seats, own, other, gain_own, gain_other, wx, wz, conv, bias, qw, kw, vw, gate):
    length, part = own.shape
    width, channels = wx.shape
    steps = channels // group
    taps = conv.shape[0]
    gate_count = gate.shape[1]

    def columns(rows):
        return spec((rows, group), lambda c: (0, c))

    full = shape_of((length, channels), b16)
    return pl.pallas_call(
        front_kernel,
        grid=(steps,),
        in_specs=[
            smem(),
            smem(),
            whole((length, part)),
            whole((length, part)),
            whole((1, part)),
            whole((1, part)),
            columns(width),
            columns(width),
            columns(taps),
            columns(1),
            columns(taps),
            columns(taps),
            columns(taps),
            spec((3, gate_count, group), lambda c: (0, 0, c)),
        ],
        out_specs=[
            whole((length, width)),
            spec((width, length // steps), lambda c: (0, c)),
            columns(length),
            columns(length),
            columns(length),
            columns(length),
            columns(length),
            columns(length),
            columns(length),
            whole((gate_count, length)),
        ],
        out_shape=[
            shape_of((length, width), b16),
            shape_of((width, length), b16),
            full,
            full,
            full,
            full,
            full,
            full,
            full,
            shape_of((gate_count, length), f32),
        ],
        scratch_shapes=[pltpu.VMEM((length + 8, group), f32)],
        compiler_params=settings(56),
        cost_estimate=cost(19),
        name="front",
    )(side, seats, own, other, gain_own, gain_other, wx, wz, conv, bias, qw, kw, vw, gate)


def scan_lanes(values, combine, empty, reverse=False):
    length = values.shape[1]
    lane = lax.broadcasted_iota(jnp.int32, values.shape, 1)
    distance = 1
    while distance < length:
        if reverse:
            moved = pltpu.roll(values, length - distance, 1)
            inside = lane < length - distance
        else:
            moved = pltpu.roll(values, distance, 1)
            inside = lane >= distance
        values = combine(values, jnp.where(inside, moved, empty))
        distance *= 2
    return values


def pick(side, first, second):
    return jnp.where(side == 0, first, second)


def fold_rows(values):
    rows, lanes = values.shape
    return jnp.sum(values.reshape(rows // 8, 8, lanes), axis=0)


def cell_kernel(
    head_dim,
    side_ref,
    seats_ref,
    forget_ref,
    gates_own_ref,
    gates_other_ref,
    q_ref,
    k_ref,
    v_ref,
    conv_ref,
    upz_ref,
    cot_own_ref,
    cot_other_ref,
    wd_ref,
    gain_ref,
    skip_ref,
    flipped_ref,
    rows_ref,
    keep_ref,
    send_ref,
    dnum_ref,
    skip_grad_ref,
    upz_grad_ref,
    first_ref,
    second_ref,
    gains_ref,
    cols_ref,
    gated_t_ref,
    state_ref,
    gated_ref,
    num_ref,
    den_ref,
    slack_ref,
    sums_ref,
):
    step = pl.program_id(0)
    side = side_ref[0]
    length, channels = q_ref.shape
    heads = channels // head_dim
    gate_count = gates_own_ref.shape[0]
    all_heads = gate_count // 2
    part = cot_own_ref.shape[1]

    @pl.when(step == 0)
    def _():
        gates = gates_own_ref[...] + gates_other_ref[...]
        inlet = pick(side, gates[:heads], gates[heads : 2 * heads])
        forget = pick(
            side, gates[all_heads : all_heads + heads], gates[all_heads + heads : gate_count]
        )
        forget = forget + jnp.concatenate(
            [jnp.full((1, length), forget_ref[side * heads + h], f32) for h in range(heads)], axis=0
        )
        log_forget = jnp.minimum(forget, 0.0) - jnp.log1p(jnp.exp(-jnp.abs(forget)))
        total = scan_lanes(log_forget, jnp.add, 0.0)
        ahead = inlet - total
        top = scan_lanes(jnp.maximum(ahead, 0.0), jnp.maximum, 0.0)
        floor = jnp.exp(-(total + top))
        rows_ref[...] = jnp.concatenate(
            [ahead + jnp.log(f32(head_dim**-0.5)), top, forget, jnp.zeros_like(top)], axis=0
        )
        cols_ref[...] = jnp.concatenate([top, floor, top, floor], axis=0).T
        sums_ref[...] = jnp.zeros_like(sums_ref)

    here = pl.ds(pl.multiple_of(step * block, block), block)

    ones = jnp.ones((length, 128), b16)

    def attend(count):
        span = count * block
        here = pl.ds(span - block, block)
        pieces = []
        for h in range(heads):
            lanes = pl.ds(h * head_dim, head_dim)
            start = span - block
            top = cols_ref[pl.ds(start, block), h : h + 1]
            scores = dot_nt(q_ref[pl.ds(start, block), lanes], k_ref[pl.ds(0, span), lanes])
            done = []
            for piece in range(count):
                there = slice(piece * block, (piece + 1) * block)
                exponent = rows_ref[h : h + 1, there] - top
                if piece == count - 1:
                    row_ids = lax.broadcasted_iota(jnp.int32, (block, block), 0)
                    col_ids = lax.broadcasted_iota(jnp.int32, (block, block), 1)
                    exponent = jnp.where(row_ids >= col_ids, exponent, -jnp.inf)
                done.append((scores[:, there] * jnp.exp(exponent)).astype(b16))
            pieces.append(jnp.concatenate(done, axis=1))
        for h in range(heads):
            lanes = pl.ds(h * head_dim, head_dim)
            num_ref[:, lanes] = dot_nn(pieces[h], v_ref[pl.ds(0, span), lanes])
            den_ref[:, pl.ds(h * 128, 128)] = dot_nn(pieces[h], ones[:span])
        state_ref[...] = dot_nt(cot_own_ref[here, :], wd_ref[:, side_cols(side, part)]) + dot_nt(
            cot_other_ref[here, :], wd_ref[:, side_cols(1 - side, part)]
        )

        small = 64
        floors = cols_ref[here, heads : 2 * heads]

        def tiles():
            for h in range(heads):
                for start in range(0, block, small):
                    yield h, start, pl.ds(start, small), pl.ds(h * head_dim, head_dim)

        stats = {}
        for h, start, rows, lanes in tiles():
            denominator = den_ref[rows, h * 128 : h * 128 + 1]
            floor = floors[start : start + small, h : h + 1]
            inverse = 1.0 / jnp.maximum(jnp.abs(denominator), floor)
            hidden = num_ref[rows, lanes] * inverse
            num_ref[rows, lanes] = hidden
            stats[h, start] = [
                inverse,
                jnp.where(jnp.abs(denominator) >= floor, jnp.where(denominator >= 0.0, inverse, -inverse), 0.0),
                jnp.mean(hidden, axis=1, keepdims=True),
            ]
        for h, start, rows, lanes in tiles():
            centered = num_ref[rows, lanes] - stats[h, start][2]
            num_ref[rows, lanes] = centered
            stats[h, start].append(
                lax.rsqrt(jnp.mean(centered * centered, axis=1, keepdims=True) + eps_norm)
            )
        gain_sums = [jnp.zeros((8, head_dim), f32)] * heads
        skip_sums = [jnp.zeros((8, head_dim), f32)] * heads
        for h, start, rows, lanes in tiles():
            gain = gain_ref[:, lanes].astype(f32)
            skip = skip_ref[:, lanes].astype(f32)
            unit = num_ref[rows, lanes] * stats[h, start][3]
            num_ref[rows, lanes] = unit
            conv_out = conv_ref[rows, lanes].astype(f32)
            inner = unit * gain + skip * conv_out
            upz = upz_ref[rows, lanes].astype(f32)
            gate = sigmoid(upz)
            active = upz * gate
            gated_ref[rows, lanes] = (inner * active).astype(b16)
            grad_state = state_ref[rows, lanes]
            grad_inner = grad_state * active
            upz_grad_ref[pl.ds(span - block + start, small), lanes] = (
                grad_state * inner * (gate + active * (1.0 - gate))
            ).astype(b16)
            skip_grad_ref[rows, lanes] = (grad_inner * skip).astype(b16)
            along = grad_inner * unit
            gain_sums[h] = gain_sums[h] + fold_rows(along)
            skip_sums[h] = skip_sums[h] + fold_rows(grad_inner * conv_out)
            grad_unit = grad_inner * gain
            state_ref[rows, lanes] = grad_unit
            stats[h, start] += [
                jnp.mean(grad_unit, axis=1, keepdims=True),
                jnp.mean(along * gain, axis=1, keepdims=True),
            ]
        for h, start, rows, lanes in tiles():
            inverse, signed, _, scale, mean, moment = stats[h, start]
            dnum_ref[rows, lanes] = (
                (state_ref[rows, lanes] - mean - num_ref[rows, lanes] * moment) * (scale * inverse)
            ).astype(b16)
            slack = -signed * moment * (head_dim * eps_norm) * scale * scale
            slack_ref[rows, pl.ds(h * 128, 128)] = jnp.broadcast_to(slack, (small, 128))
        for h in range(heads):
            lanes = pl.ds(h * head_dim, head_dim)
            sums_ref[0:8, lanes] += gain_sums[h]
            sums_ref[8:16, lanes] += skip_sums[h]
        for h in range(heads):
            rows_ref[3 * heads + h : 3 * heads + h + 1, here] = slack_ref[:, pl.ds(h * 128, 128)].T[0:1]
        gated = gated_ref[...]
        keep_ref[...] = dot_nn(gated, wd_ref[:, side_cols(side, part)]).astype(b16)
        send_ref[...] = dot_nn(gated, wd_ref[:, side_cols(1 - side, part)]).astype(b16)
        seat_rows(gated.T, seats_ref, gated_t_ref.at[:, here])


    for count in range(1, length // block + 1):
        pl.when(step == count - 1)(partial(attend, count))

    @pl.when(step == pl.num_programs(0) - 1)
    def _():
        gains_ref[0:1, :] = jnp.sum(sums_ref[0:8, :], axis=0, keepdims=True)
        gains_ref[1:2, :] = jnp.sum(sums_ref[8:16, :], axis=0, keepdims=True)
        gains_ref[2:8, :] = jnp.zeros((6, channels), f32)
        half = first_ref.shape[0]
        width = 2 * part
        for start in range(0, 2 * half, block):
            out_ref = (first_ref if start < half else second_ref).at[pl.ds(start % half, block), :]
            rows = pl.ds(start, block)
            turned = gated_t_ref[rows, :]
            out_ref[:, side_cols(side, part)] = dot_nn(turned, cot_own_ref[...]).astype(b16)
            out_ref[:, side_cols(1 - side, part)] = dot_nn(turned, cot_other_ref[...]).astype(b16)
            out_ref[:, pl.ds(width, channels)] = dot_nn(
                flipped_ref[rows, :], upz_grad_ref[...]
            ).astype(b16)


def cell(
    side, seats, forget, gates_own, gates_other, q, k, v, conv, upz, cot_own, cot_other, wd, gain,
    skip, flipped, head_dim,
):
    length, channels = q.shape
    part = cot_own.shape[1]
    width = wd.shape[1]
    gate_count = gates_own.shape[0]
    heads = channels // head_dim

    def rows(cols):
        return spec((block, cols), lambda r: (r, 0))

    return pl.pallas_call(
        partial(cell_kernel, head_dim),
        grid=(length // block,),
        in_specs=[
            smem(),
            smem(),
            smem(),
            whole((gate_count, length)),
            whole((gate_count, length)),
            whole((length, channels)),
            whole((length, channels)),
            whole((length, channels)),
            rows(channels),
            rows(channels),
            whole((length, part)),
            whole((length, part)),
            whole((channels, width)),
            whole((1, channels)),
            whole((1, channels)),
            whole((width, length)),
        ],
        out_specs=[
            whole((8, length)),
            rows(part),
            rows(part),
            rows(channels),
            rows(channels),
            whole((length, channels)),
            whole((channels // 2, width + channels)),
            whole((channels // 2, width + channels)),
            whole((8, channels)),
        ],
        out_shape=[
            shape_of((8, length), f32),
            shape_of((length, part), b16),
            shape_of((length, part), b16),
            shape_of((length, channels), b16),
            shape_of((length, channels), b16),
            shape_of((length, channels), b16),
            shape_of((channels // 2, width + channels), b16),
            shape_of((channels // 2, width + channels), b16),
            shape_of((8, channels), f32),
        ],
        scratch_shapes=[
            pltpu.VMEM((length, 8), f32),
            pltpu.VMEM((channels, length), b16),
            pltpu.VMEM((block, channels), f32),
            pltpu.VMEM((block, channels), b16),
            pltpu.VMEM((block, channels), f32),
            pltpu.VMEM((block, heads * 128), f32),
            pltpu.VMEM((block, heads * 128), f32),
            pltpu.VMEM((16, channels), f32),
        ],
        compiler_params=settings(56),
        cost_estimate=cost(25),
        name="cell",
    )(side, seats, forget, gates_own, gates_other, q, k, v, conv, upz, cot_own, cot_other, wd,
      gain, skip, flipped)


def cell_back_kernel(
    h, heads, q_ref, k_ref, v_ref, dnum_ref, rows_ref, prior_ref, dq_ref, dk_ref, dv_ref, gates_ref, cols_ref,
    dk_acc, dv_acc, pair_ref,
):
    length, head_dim = q_ref.shape
    cols_ref[...] = rows_ref[...].T
    gates_ref[...] = prior_ref[...]
    ahead = cols_ref[:, h : h + 1]
    row_ids = lax.broadcasted_iota(jnp.int32, (block, block), 0)
    col_ids = lax.broadcasted_iota(jnp.int32, (block, block), 1)
    blocks = length // block
    for t in range(blocks):
        here = pl.ds(t * block, block)
        top = rows_ref[pl.ds(heads + h, 1), here]
        slack = rows_ref[pl.ds(3 * heads + h, 1), here]
        queries = q_ref[here, :]
        dnum = dnum_ref[here, :]
        for s in range(t + 1):
            there = pl.ds(s * block, block)
            keys = k_ref[there, :]
            exponent = ahead[s * block : (s + 1) * block] - top
            if s == t:
                exponent = jnp.where(row_ids <= col_ids, exponent, -jnp.inf)
            weight = jnp.exp(exponent)
            scores = dot_nt(keys, queries) * weight
            grads = (dot_nt(v_ref[there, :], dnum) + slack) * weight
            grads_b = grads.astype(b16)
            dv_part = dot_nn(scores.astype(b16), dnum)
            dk_part = dot_nn(grads_b, queries)
            dq_part = dot_tn(grads_b, keys)
            if s == t:
                dv_acc[there, :] = dv_part
                dk_acc[there, :] = dk_part
            else:
                dv_acc[there, :] += dv_part
                dk_acc[there, :] += dk_part
            dq = dq_part if s == 0 else dq + dq_part
        dq_ref[here, :] = dq.astype(b16)
        pair_ref[here, 0:128] = jnp.broadcast_to(
            jnp.sum(dq * queries.astype(f32), axis=1, keepdims=True), (block, 128)
        )
    for s in range(blocks):
        there = pl.ds(s * block, block)
        dk = dk_acc[there, :]
        dk_ref[there, :] = dk.astype(b16)
        dv_ref[there, :] = dv_acc[there, :].astype(b16)
        pair_ref[there, 128:256] = jnp.broadcast_to(
            jnp.sum(dk * k_ref[there, :].astype(f32), axis=1, keepdims=True), (block, 128)
        )
    outward = pair_ref[:, 0:128].T[0:1]
    inward = pair_ref[:, 128:256].T[0:1]
    forget = rows_ref[pl.ds(2 * heads + h, 1), :]
    grad_log = scan_lanes(jnp.broadcast_to(outward - inward, (8, length)), jnp.add, 0.0, True)[0:1]
    gates_ref[pl.ds(h, 1), :] = inward
    gates_ref[pl.ds(heads + h, 1), :] = grad_log * sigmoid(-forget)


def cell_back(q, k, v, dnum, rows, prior, h, head_dim):
    length, channels = q.shape
    heads = channels // head_dim
    per_head = spec((length, head_dim), lambda _: (0, h))
    result = whole((length, head_dim))
    full = shape_of((length, head_dim), b16)
    return pl.pallas_call(
        partial(cell_back_kernel, h, heads),
        grid=(1,),
        in_specs=[per_head] * 4 + [whole((8, length))] * 2,
        out_specs=[result, result, result, whole((8, length))],
        out_shape=[full, full, full, shape_of((8, length), f32)],
        scratch_shapes=[
            pltpu.VMEM((length, 8), f32),
            pltpu.VMEM((length, head_dim), f32),
            pltpu.VMEM((length, head_dim), f32),
            pltpu.VMEM((length, 256), f32),
        ],
        compiler_params=settings(56),
        cost_estimate=cost(8),
        name="cell_back",
    )(q, k, v, dnum, rows, prior)


def steps_width(ref):
    return ref.shape[1]


def front_back_kernel(
    heads,
    index,
    reseat,
    side_ref,
    table_ref,
    gates_own_ref,
    gates_other_ref,
    dq_ref,
    dk_ref,
    dv_ref,
    q_ref,
    k_ref,
    v_ref,
    conv_out_ref,
    slope_ref,
    upx_ref,
    skip_grad_ref,
    conv_ref,
    qw_ref,
    kw_ref,
    vw_ref,
    gate_ref,
    flipped_ref,
    *refs,
):
    last = index == heads - 1
    if last:
        gains_ref, *refs = refs
        prior_refs, refs = refs[:index], refs[index:]
    upx_grad_ref, first_ref, second_ref, small_ref, gates_ref, gates_t_ref, padded_ref = refs[:7]
    step = pl.program_id(0)
    side = side_ref[0]
    length = q_ref.shape[0]
    tap_count = conv_ref.shape[0]

    @pl.when(step == 0)
    def _():
        own = gates_own_ref[...]
        other = gates_other_ref[...]
        gates = jnp.concatenate(
            [
                pick(side, own[:heads], other[:heads]),
                pick(side, other[:heads], own[:heads]),
                pick(side, own[heads : 2 * heads], other[heads : 2 * heads]),
                pick(side, other[heads : 2 * heads], own[heads : 2 * heads]),
            ],
            axis=0,
        )
        gates_ref[...] = gates
        gates_t_ref[...] = gates.T
        padded_ref[pl.ds(length, 8), :] = jnp.zeros((8, group), f32)

    gates = gates_ref[...]
    gates_b = gates.astype(b16)
    gates_t = gates_t_ref[...].astype(b16)
    dq_b = (dq_ref[...].astype(f32) + dot_nn(gates_t, gate_ref[0])).astype(b16)
    dk_b = (dk_ref[...].astype(f32) + dot_nn(gates_t, gate_ref[1])).astype(b16)
    dv_b = (dv_ref[...].astype(f32) + dot_nn(gates_t, gate_ref[2])).astype(b16)
    conv_out = conv_out_ref[...]
    upx_b = upx_ref[...]
    grad_conv = (
        skip_grad_ref[...].astype(f32)
        + dot_nt(dq_b, spread_taps(qw_ref[...]))
        + dot_nt(dk_b, spread_taps(kw_ref[...]))
    )
    grad_pre = grad_conv * slope_ref[...].astype(f32)
    padded_ref[pl.ds(0, length), :] = grad_pre
    taps = conv_ref[...].astype(f32)
    upx = upx_b.astype(f32)
    grad_upx = dot_nt(dv_b, spread_taps(vw_ref[...])) + taps[tap_count - 1 : tap_count] * grad_pre
    tap_grads = [jnp.sum(upx * grad_pre, axis=0, keepdims=True)]
    for tap in range(tap_count - 2, -1, -1):
        moved = padded_ref[pl.ds(tap_count - 1 - tap, length), :]
        grad_upx = grad_upx + taps[tap : tap + 1] * moved
        tap_grads.insert(0, jnp.sum(upx * moved, axis=0, keepdims=True))
    grad_b = grad_upx.astype(b16)
    upx_grad_ref[...] = grad_b
    half = first_ref.shape[0]
    height = half // len(reseat)
    for start, out_ref in ((0, first_ref), (half, second_ref)):
        result = dot_nn(flipped_ref[pl.ds(start, half), :], grad_b).astype(b16)
        for seat, source in enumerate(reseat):
            out_ref[
                seat * height : (seat + 1) * height,
                pl.ds(pl.multiple_of(step * group, group), group),
            ] = result[source * height : (source + 1) * height]
    small_ref[:, pl.ds(pl.multiple_of(step * group, group), group)] = jnp.concatenate(
        tap_grads
        + [
            gather_taps(dot_tn(conv_out, dq_b), tap_count),
            gather_taps(dot_tn(conv_out, dk_b), tap_count),
            gather_taps(dot_tn(upx_b, dv_b), tap_count),
            dot_nn(gates_b, q_ref[...]),
            dot_nn(gates_b, k_ref[...]),
            dot_nn(gates_b, v_ref[...]),
            jnp.broadcast_to(jnp.sum(gates, axis=1, keepdims=True), (gates.shape[0], group)),
            jnp.sum(grad_pre, axis=0, keepdims=True),
            jnp.zeros((7, group), f32),
        ],
        axis=0,
    )
    if last:

        @pl.when(step == pl.num_programs(0) - 1)
        def _():
            turned_ref = refs[7]
            small = jnp.concatenate([ref[...] for ref in (*prior_refs, small_ref)], axis=1)
            split = 4 * tap_count + 3 * gates.shape[0]
            stacked = jnp.concatenate(
                [
                    small[:split],
                    small[split + gates.shape[0] : split + gates.shape[0] + 1],
                    gains_ref[0:2, :],
                    jnp.zeros((128 - split - 3, small.shape[1]), f32),
                ],
                axis=0,
            )
            turned_ref[...] = stacked.T
            span = steps_width(small_ref)
            for seat in range(2 * len(reseat)):
                out_ref = first_ref if seat < len(reseat) else second_ref
                start = seat % len(reseat) * height
                out_ref[start : start + height, span : span + 128] = turned_ref[
                    pl.ds(pl.multiple_of(table_ref[seat] * height, height), height), :
                ].astype(b16)


def front_back(
    side, table, gates_own, gates_other, dq, dk, dv, q, k, v, conv_out, slope, upx, skip_grad, conv,
    qw, kw, vw, gate, flipped, gains, priors, heads, index, reseat,
):
    length, channels = q.shape
    width = flipped.shape[0]
    taps = conv.shape[0]
    gate_count = gate.shape[1]
    parts = heads
    steps = channels // group // parts
    base = index * steps
    last = index == heads - 1
    out_width = channels // parts + (128 if last else 0)
    extra = [gains, *priors] if last else []
    scratch = [pltpu.VMEM((channels, 128), f32)] if last else []

    def columns(rows):
        return spec((rows, group), lambda c: (0, base + c))

    def results(rows):
        return spec((rows, group), lambda c: (0, c))

    return pl.pallas_call(
        partial(front_back_kernel, heads, index, reseat),
        grid=(steps,),
        in_specs=[smem(), smem(), whole((8, length)), whole((8, length))]
        + [results(length)] * 3
        + [columns(length)] * 7
        + [columns(taps)] * 4
        + [spec((3, gate_count, group), lambda c: (0, 0, base + c)), whole((width, length))]
        + [whole(value.shape) for value in extra],
        out_specs=[
            results(length),
            whole((width // 2, out_width)),
            whole((width // 2, out_width)),
            whole((56, channels // parts)),
        ],
        out_shape=[
            shape_of((length, channels // parts), b16),
            shape_of((width // 2, out_width), b16),
            shape_of((width // 2, out_width), b16),
            shape_of((56, channels // parts), f32),
        ],
        scratch_shapes=[
            pltpu.VMEM((gate_count, length), f32),
            pltpu.VMEM((length, gate_count), f32),
            pltpu.VMEM((length + 8, group), f32),
        ]
        + scratch,
        compiler_params=settings(56),
        cost_estimate=cost(8),
        name="front_back",
    )(side, table, gates_own, gates_other, dq, dk, dv, q, k, v, conv_out, slope, upx, skip_grad, conv,
      qw, kw, vw, gate, flipped, *extra)


def norm_back_kernel(
    parts,
    side_ref,
    *refs,
):
    upx_grad_refs = refs[:parts]
    norm_back_body(side_ref, upx_grad_refs, *refs[parts:])


def norm_back_body(
    side_ref,
    upx_grad_refs,
    upz_grad_ref,
    wx_ref,
    wz_ref,
    own_ref,
    other_ref,
    gain_own_ref,
    gain_other_ref,
    keep_ref,
    send_ref,
    stats_ref,
    gains_ref,
):
    step = pl.program_id(0)
    side = side_ref[0]
    part = own_ref.shape[1]

    @pl.when(step == 0)
    def _():
        gains_ref[...] = jnp.zeros_like(gains_ref)

    own = own_ref[...].astype(f32)
    other = other_ref[...].astype(f32)
    center, scale = row_stats(own, other)
    sums = []
    for index, (values, place, gain_ref, out_ref) in enumerate(
        [(own, side, gain_own_ref, keep_ref), (other, 1 - side, gain_other_ref, send_ref)]
    ):
        rows = side_cols(place, part)
        terms = dot_nt(upz_grad_ref[...], wz_ref[rows, :])
        for index_part, grad_ref in enumerate(upx_grad_refs):
            span = grad_ref.shape[1]
            lanes = pl.ds(index_part * span, span)
            terms = terms + dot_nt(grad_ref[...], wx_ref[rows, lanes])
        out_ref[...] = terms.astype(b16)
        unit = (values - center) * scale
        along = terms * unit
        gains_ref[index : index + 1, :] += jnp.sum(along, axis=0, keepdims=True)
        gain = gain_ref[...].astype(f32)
        sums.append(
            (
                jnp.sum(terms * gain, axis=1, keepdims=True),
                jnp.sum(along * gain, axis=1, keepdims=True),
            )
        )
    flat = jnp.concatenate(
        [
            jnp.broadcast_to(sums[0][0] + sums[1][0], (block, 128)).T[0:1],
            jnp.broadcast_to(sums[0][1] + sums[1][1], (block, 128)).T[0:1],
            jnp.zeros((6, block), f32),
        ],
        axis=0,
    )
    stats_ref[...] = flat


def norm_back(side, upx_grads, upz_grad, wx, wz, own, other, gain_own, gain_other):
    length, channels = upz_grad.shape
    parts = len(upx_grads)
    part = own.shape[1]
    width = wx.shape[0]

    def rows(cols):
        return spec((block, cols), lambda r: (r, 0))

    return pl.pallas_call(
        partial(norm_back_kernel, parts),
        grid=(length // block,),
        in_specs=[smem()]
        + [rows(channels // parts)] * parts
        + [
            rows(channels),
            whole((width, channels)),
            whole((width, channels)),
            rows(part),
            rows(part),
            whole((1, part)),
            whole((1, part)),
        ],
        out_specs=[rows(part), rows(part), spec((8, block), lambda r: (0, r)), whole((8, part))],
        out_shape=[
            shape_of((length, part), b16),
            shape_of((length, part), b16),
            shape_of((8, length), f32),
            shape_of((8, part), f32),
        ],
        compiler_params=settings(56),
        cost_estimate=cost(10),
        name="norm_back",
    )(side, *upx_grads, upz_grad, wx, wz, own, other, gain_own, gain_other)


def seat_back(table_ref, near_ref, far_ref, out_ref):
    pieces = table_ref.shape[0]
    height = out_ref.shape[0] // pieces
    for seat in range(pieces):
        source = near_ref if seat < pieces // 2 else far_ref
        start = seat % (pieces // 2) * height
        out_ref[pl.ds(pl.multiple_of(table_ref[seat] * height, height), height), :] = source[
            start : start + height, :
        ].astype(f32)


def place_rows(table, pair):
    near, far = pair
    half, width = near.shape
    source = spec((half, group), lambda c: (0, c))
    return pl.pallas_call(
        seat_back,
        grid=(width // group,),
        in_specs=[smem(), source, source],
        out_specs=spec((2 * half, group), lambda c: (0, c)),
        out_shape=shape_of((2 * half, width), f32),
        compiler_params=settings(24),
        cost_estimate=cost(3),
        name="place_rows",
    )(table, near, far)


def place_last_kernel(
    taps, gate_count, mixed_ref, far_table_ref, near_ref, far_ref, near_two_ref, far_two_ref,
    near_small_ref, far_small_ref, out_ref, conv_ref, q_ref, k_ref, v_ref, bias_ref, gain_ref,
    skip_ref, gate_ref, turned_ref,
):
    step = pl.program_id(0)
    middle = pl.num_programs(0) // 2

    @pl.when(step == 0)
    def _():
        seat_back(far_table_ref, near_small_ref, far_small_ref, turned_ref)
        flat = turned_ref[...].T
        for at, ref in enumerate((conv_ref, q_ref, k_ref, v_ref)):
            ref[...] = flat[at * taps : (at + 1) * taps]
        start = 4 * taps
        for part in range(3):
            gate_ref[part, :, :] = turned_ref[
                :, start + part * gate_count : start + (part + 1) * gate_count
            ]
        start += 3 * gate_count
        for at, ref in enumerate((bias_ref, gain_ref, skip_ref)):
            ref[...] = flat[start + at : start + at + 1]

    @pl.when(step < middle)
    def _():
        seat_back(mixed_ref, near_ref, far_ref, out_ref)

    @pl.when(step >= middle)
    def _():
        seat_back(far_table_ref, near_two_ref, far_two_ref, out_ref)


def place_last(mixed_table, far_table, pair, pair_two, taps, gate_count):
    half, width = pair[0].shape
    steps = width // group
    channels = 2 * half

    def source(first):
        return spec((half, group), lambda c: (0, jnp.clip(c - first, 0, steps - 1)))

    small = spec((half, 128), lambda c: (0, width // 128))
    row = shape_of((1, channels), f32)
    tap_rows = shape_of((taps, channels), f32)
    shapes = [tap_rows] * 4 + [row] * 3 + [shape_of((3, channels, gate_count), f32)]
    return pl.pallas_call(
        partial(place_last_kernel, taps, gate_count),
        grid=(2 * steps,),
        in_specs=[smem(), smem(), source(0), source(0), source(steps), source(steps), small, small],
        out_specs=[spec((2 * half, group), lambda c: (0, c))] + [whole(v.shape) for v in shapes],
        out_shape=[shape_of((2 * half, 2 * width), f32)] + shapes,
        scratch_shapes=[pltpu.VMEM((channels, 128), f32)],
        compiler_params=settings(32),
        cost_estimate=cost(5),
        name="place_last",
    )(mixed_table, far_table, *pair, *pair_two, *pair_two)


def finish_kernel(
    own_ref, other_ref, gain_ref, keep_ref, recv_ref, stats_own_ref, stats_other_ref, cot_ref,
    out_ref,
):
    own = own_ref[...].astype(f32)
    center, scale = row_stats(own, other_ref[...].astype(f32))
    stats = (stats_own_ref[...] + stats_other_ref[...]).T
    width = own.shape[1] + other_ref.shape[1]
    terms = keep_ref[...].astype(f32) + recv_ref[...].astype(f32)
    unit = (own - center) * scale
    pulled = terms * gain_ref[...].astype(f32) - (stats[:, 0:1] + unit * stats[:, 1:2]) / width
    out_ref[...] = cot_ref[...].astype(f32) + pulled * scale


def finish(own, other, gain, keep, recv, stats_own, stats_other, cot):
    length, part = own.shape
    rows = spec((block, part), lambda r: (r, 0))
    stats = spec((8, block), lambda r: (0, r))
    return pl.pallas_call(
        finish_kernel,
        grid=(length // block,),
        in_specs=[rows, rows, whole((1, part)), rows, rows, stats, stats, rows],
        out_specs=rows,
        out_shape=shape_of((length, part), f32),
        compiler_params=settings(32),
        cost_estimate=cost(4),
        name="finish",
    )(own, other, gain, keep, recv, stats_own, stats_other, cot)


def swap(values):
    return lax.ppermute(values, "head", [(0, 1), (1, 0)])


def across(values, bit, count):
    return lax.ppermute(values, "dp", [(i, i ^ (1 << bit)) for i in range(count)])


def add_halves(first, second):
    return (first.astype(f32) + second.astype(f32)).astype(first.dtype)


class Reduction:
    def __init__(self, keep, out, order, bits, count, step=0):
        self.keep, self.out, self.count = keep, out, count
        self.plan = (
            [("half", bit) for bit in order]
            + [("full", bit) for bit in range(len(order), bits)]
            + [("copy", bit) for bit in reversed(order)]
        )
        self.step = step

    def send(self):
        if not self.more():
            return None
        self.got = across(self.keep if self.out is None else self.out, self.plan[self.step][1], self.count)
        return self.got

    def take(self, got=None):
        if not self.more():
            return
        got = self.got if got is None else got
        kind, bit = self.plan[self.step]
        self.step += 1
        after = self.plan[self.step][0] if self.step < len(self.plan) else "end"
        if kind == "copy":
            if after == "end":
                self.result = (self.keep, got)
            else:
                self.keep = jnp.concatenate([self.keep, got], axis=0)
                self.out = None
        elif after == "half":
            half = self.keep.shape[0] // 2
            self.out = add_halves(self.keep[half:], got[half:])
            self.keep = add_halves(self.keep[:half], got[:half])
        else:
            self.keep = add_halves(self.keep, got)
            self.out = None

    def more(self):
        return self.step < len(self.plan)


def arrange(order, place):
    levels = len(order)
    return sum((((place >> bit) & 1) << (levels - 1 - at)) for at, bit in enumerate(order))


def settle(value, *flows):
    flows = [flow for flow in flows if flow.more()]
    value, gots = lax.optimization_barrier((value, [flow.got for flow in flows]))
    for flow, got in zip(flows, gots):
        flow.take(got)
    flows = [flow for flow in flows if flow.more()]
    held = [(flow.keep, flow.out) for flow in flows]
    value, held = lax.optimization_barrier((value, held))
    for flow, (keep, out) in zip(flows, held):
        flow.keep, flow.out = keep, out
    return value


def send_all(flows):
    for flow in flows:
        flow.send()


def on_device(
    layer_input,
    ln_gain,
    up_x_weight,
    up_z_weight,
    conv_weight,
    conv_bias,
    query_weight,
    key_weight,
    value_weight,
    gate_weight,
    forget_bias,
    norm_gain,
    skip_gain,
    down_weight,
    cotangent,
):
    head_index = lax.axis_index("head")
    place = lax.axis_index("dp")
    count = lax.axis_size("dp")
    side = head_index.astype(jnp.int32).reshape(1)
    part = layer_input.shape[1]
    channels = up_x_weight.shape[1]
    all_heads = gate_weight.shape[2] // 2
    heads = all_heads // lax.axis_size("head")
    head_dim = channels // heads
    taps = conv_weight.shape[0]
    bits = count.bit_length() - 1
    levels = min(bits, 3)
    near_order = list(range(levels))
    far_order = near_order[:1] + near_order[2:3] + near_order[1:2] + near_order[3:]
    pieces = 2**levels
    turned = [0] * pieces
    for relative in range(pieces):
        turned[arrange(near_order, relative)] = arrange(far_order, relative)
    seats = jnp.arange(pieces, dtype=jnp.int32)
    near_table = (seats ^ arrange(near_order, place)).astype(jnp.int32)
    far_table = (seats ^ arrange(far_order, place)).astype(jnp.int32)
    mixed_table = (jnp.array(turned, jnp.int32) ^ arrange(far_order, place)).astype(jnp.int32)
    middle = max(pieces // 2, 1)
    straight = list(range(middle))
    mixed = [turned[seat] for seat in range(middle)]

    gain_own = ln_gain.reshape(1, part)
    gain_other = swap(gain_own)
    input_other = swap(layer_input)
    cot_start, input_other, gain_other = lax.optimization_barrier(
        (cotangent, input_other, gain_other)
    )
    cot_other = swap(cot_start)
    gate_t = gate_weight.transpose(0, 2, 1)
    normed, flipped, upx, upz, conv_out, slope, q, k, v, gates = front(
        side, far_table, layer_input, input_other, gain_own, gain_other, up_x_weight, up_z_weight,
        conv_weight, conv_bias.reshape(1, channels), query_weight, key_weight, value_weight, gate_t,
    )
    gates_other = swap(gates)
    rows, keep, send, dnum, skip_grad, upz_grad, early_keep, early_send, gains = cell(
        side, near_table, forget_bias.astype(f32), gates, gates_other, q, k, v, conv_out, upz,
        cotangent, cot_other, down_weight, norm_gain.reshape(1, channels),
        skip_gain.reshape(1, channels), flipped, head_dim,
    )
    width = down_weight.shape[1]
    down_other = swap(send)
    got = across(early_send, near_order[0], count)
    grads = [cell_back(q, k, v, dnum, rows, rows, 0, head_dim)]
    prior, got = lax.optimization_barrier((grads[0][3], got))
    first = Reduction(early_keep[:, :width], None, near_order, bits, count)
    second = Reduction(early_keep[:, width:], None, far_order, bits, count)
    first.got, second.got = got[:, :width], got[:, width:]
    prior = settle(prior, first, second)
    first.send()
    second.send()
    gate_grads = cell_back(q, k, v, dnum, rows, prior, 1, head_dim)
    grads.append(gate_grads)
    gate_grads = settle(gate_grads[3], first, second)
    gate_grads_other = swap(gate_grads)
    first.send()
    second.send()
    late = []
    upx_grads = []
    smalls = []

    def back(index, order, reseat):
        dq, dk, dv, _ = grads[index]
        upx_grad, late_keep, late_send, small = front_back(
            side, far_table, gate_grads, gate_grads_other, dq, dk, dv, q, k, v, conv_out, slope,
            upx, skip_grad, conv_weight, query_weight, key_weight, value_weight, gate_t, flipped,
            gains, list(smalls), heads, index, reseat,
        )
        upx_grads.append(upx_grad)
        smalls.append(small)
        late.append(Reduction(late_keep, late_send, order, bits, count))
        late[-1].send()

    back(0, near_order, mixed)
    layer_output = (
        layer_input.astype(f32) + keep.astype(f32) + down_other.astype(f32)
    ).astype(b16)
    gate_grads_other, layer_output = settle((gate_grads_other, layer_output), first, second)
    send_all([first, second])
    back(1, far_order, straight)
    upx_grads[1] = settle(upx_grads[1], *late)
    send_all(late)
    terms = norm_back(
        side, upx_grads, upz_grad, up_x_weight, up_z_weight, layer_input, input_other, gain_own,
        gain_other,
    )
    flows = [first, second, *late]
    terms_keep, terms_send, stats, ln_parts = settle(terms, *flows)
    stats_other = swap(stats)
    ln_other = swap(ln_parts[1:2])
    terms_other = swap(terms_send)
    send_all(flows)
    stats_other, ln_other = settle((stats_other, ln_other), *flows)
    sums = smalls[0][-12:-8, 0]
    tiny = jnp.concatenate([(ln_parts[0] + ln_other[0]), sums, jnp.zeros((124,), f32)])
    flows.append(Reduction(tiny.reshape(-1, 128), None, [], bits, count))
    send_all(flows)
    settle((), *flows)
    send_all(flows)
    terms_other = settle(terms_other, *flows)
    send_all(flows)
    input_grad = finish(
        layer_input, input_other, gain_own, terms_keep, terms_other, stats, stats_other, cotangent
    )
    input_grad = settle(input_grad, *flows)
    while any(flow.more() for flow in flows):
        send_all(flows)
        settle((), *flows)
    grad_down = place_rows(near_table, first.result)
    grad_upz = place_rows(far_table, second.result)
    grad_upx, conv_grad, q_grad, k_grad, v_grad, bias_grad, gain_grad, skip_sum, gate_grad = (
        place_last(mixed_table, far_table, late[0].result, late[1].result, taps, 2 * all_heads)
    )
    tiny = flows[-1].keep.reshape(-1)
    return (
        layer_output,
        input_grad,
        tiny[:part],
        grad_upx,
        grad_upz,
        conv_grad,
        bias_grad.reshape(-1),
        q_grad,
        k_grad,
        v_grad,
        gate_grad,
        tiny[part : part + all_heads],
        gain_grad.reshape(-1),
        skip_sum.reshape(-1),
        grad_down,
    )


def solution(mesh):
    in_specs = (
        P("dp", "head"),
        P("head"),
        P(None, "head"),
        P(None, "head"),
        P(None, "head"),
        P("head"),
        P(None, "head"),
        P(None, "head"),
        P(None, "head"),
        P(None, "head", None),
        P(),
        P("head"),
        P("head"),
        P("head", None),
        P("dp", "head"),
    )
    out_specs = (
        P("dp", "head"),
        P("dp", "head"),
        P("head"),
        P(None, "head"),
        P(None, "head"),
        P(None, "head"),
        P("head"),
        P(None, "head"),
        P(None, "head"),
        P(None, "head"),
        P(None, "head", None),
        P(),
        P("head"),
        P("head"),
        P("head", None),
    )
    return jax.shard_map(
        on_device, mesh=mesh, in_specs=in_specs, out_specs=out_specs, check_vma=False
    )
```

```python
from functools import partial

import jax
import jax.numpy as jnp
from jax import lax
from jax.experimental import pallas as pl
from jax.experimental.pallas import tpu as pltpu
from jax.sharding import PartitionSpec as P

eps_norm = 1e-05
group = 256
block = 256
b16 = jnp.bfloat16
f32 = jnp.float32


def dot_nn(first, second):
    return lax.dot_general(first, second, (((1,), (0,)), ((), ())), preferred_element_type=f32)


def dot_nt(first, second):
    return lax.dot_general(first, second, (((1,), (1,)), ((), ())), preferred_element_type=f32)


def dot_tn(first, second):
    return lax.dot_general(first, second, (((0,), (0,)), ((), ())), preferred_element_type=f32)


def sigmoid(values):
    return 0.5 * jnp.tanh(0.5 * values) + 0.5


def spec(shape, index_map):
    return pl.BlockSpec(shape, index_map)


def whole(shape):
    return pl.BlockSpec(shape, lambda *_: (0,) * len(shape))


def smem():
    return pl.BlockSpec(memory_space=pltpu.SMEM)


def shape_of(shape, dtype):
    return jax.ShapeDtypeStruct(shape, dtype)


def vmem():
    return pl.BlockSpec(memory_space=pltpu.VMEM)


def hbm():
    return pl.BlockSpec(memory_space=pltpu.HBM)


def roomy(mebibytes):
    return pltpu.CompilerParams(vmem_limit_bytes=mebibytes * 2**20)


def settings(mebibytes):
    return pltpu.CompilerParams(
        dimension_semantics=("arbitrary",), vmem_limit_bytes=mebibytes * 2**20
    )


def cost(micros):
    return pl.CostEstimate(
        flops=int(micros * 1.1e9), bytes_accessed=int(micros * 3.6e6), transcendentals=0
    )


def side_cols(side, width):
    return pl.ds(pl.multiple_of(side * width, width), width)


def spread_taps(taps):
    tap_count, width = taps.shape
    rows = lax.broadcasted_iota(jnp.int32, (width, width), 0) // tap_count
    cols = lax.broadcasted_iota(jnp.int32, (width, width), 1) // tap_count
    pair = jnp.concatenate([taps.astype(f32)] * (8 // tap_count), axis=0)
    full = jnp.concatenate([pair] * (width // 8), axis=0)
    return jnp.where(rows == cols, full, 0.0).astype(b16)


def gather_taps(dense, tap_count):
    width = dense.shape[0]
    rows = lax.broadcasted_iota(jnp.int32, (width, width), 0) // tap_count
    cols = lax.broadcasted_iota(jnp.int32, (width, width), 1) // tap_count
    kept = jnp.where(rows == cols, dense, 0.0)
    folded = jnp.sum(kept.reshape(width // 8, 8, width), axis=0)
    total = folded[:tap_count]
    for part in range(1, 8 // tap_count):
        total = total + folded[part * tap_count : (part + 1) * tap_count]
    return total


def row_stats(own, other):
    width = own.shape[1] + other.shape[1]
    total = jnp.sum(own, axis=1, keepdims=True) + jnp.sum(other, axis=1, keepdims=True)
    square = jnp.sum(own * own, axis=1, keepdims=True) + jnp.sum(
        other * other, axis=1, keepdims=True
    )
    center = total / width
    return center, lax.rsqrt(square / width - center * center + eps_norm)


def seat_rows(values, seats_ref, out_ref):
    seats = seats_ref.shape[0]
    height = values.shape[0] // seats
    for piece in range(seats):
        out_ref[pl.ds(pl.multiple_of(seats_ref[piece] * height, height), height), :] = values[
            piece * height : (piece + 1) * height
        ]


class Fetch:
    def __init__(self, sems):
        self.sems, self.copies = sems, []

    def __call__(self, source, target):
        copy = pltpu.make_async_copy(source, target, self.sems.at[len(self.copies)])
        copy.start()
        self.copies.append(copy)
        return copy


def buffers(*operands):
    return [pltpu.VMEM(value.shape, value.dtype) for value in operands]


def in_hbm(values):
    return pltpu.with_memory_space_constraint(values, pltpu.HBM)


def stage_kernel(count, taps_count, *refs):
    sources, smalls, targets = refs[:count], refs[count : count + 7], refs[count + 7 : 2 * count + 7]
    params_ref, sems = refs[2 * count + 7 :]
    fetch = Fetch(sems)
    for source, target in zip(sources, targets):
        fetch(source, target)
    rows = [ref[...].astype(f32) for ref in smalls]
    filled = sum(row.shape[0] for row in rows)
    rows.append(jnp.zeros((params_ref.shape[0] - filled, params_ref.shape[1]), f32))
    params_ref[...] = jnp.concatenate(rows, axis=0).astype(b16)
    for copy in fetch.copies:
        copy.wait()


def stage(arrays, smalls):
    count = len(arrays)
    params = shape_of((32, smalls[0].shape[1]), b16)
    return pl.pallas_call(
        partial(stage_kernel, count, smalls[0].shape[0]),
        in_specs=[hbm()] * count + [vmem()] * len(smalls),
        out_specs=[vmem()] * (count + 1),
        out_shape=[shape_of(value.shape, value.dtype) for value in arrays] + [params],
        scratch_shapes=[pltpu.SemaphoreType.DMA((count,))],
        compiler_params=roomy(16),
        cost_estimate=cost(4),
        name="stage",
    )(*[in_hbm(value) for value in arrays], *smalls)


def norm_kernel(
    side_ref, own_ref, gain_own_ref, gain_other_ref, other_hbm, normed_ref, unit_own_ref,
    unit_other_ref, scales_ref, other_ref, sems,
):
    side = side_ref[0]
    length, part = own_ref.shape
    fetch = Fetch(sems)
    blocks = length // block
    for at in range(blocks):
        rows = pl.ds(at * block, block)
        fetch(other_hbm.at[rows, :], other_ref.at[rows, :])
    for at in range(blocks):
        rows = pl.ds(at * block, block)
        fetch.copies[at].wait()
        own = own_ref[rows, :].astype(f32)
        other = other_ref[rows, :].astype(f32)
        center, scale = row_stats(own, other)
        unit_own = (own - center) * scale
        unit_other = (other - center) * scale
        unit_own_ref[rows, :] = unit_own.astype(b16)
        unit_other_ref[rows, :] = unit_other.astype(b16)
        normed_ref[rows, side_cols(side, part)] = (
            unit_own * gain_own_ref[...].astype(f32)
        ).astype(b16)
        normed_ref[rows, side_cols(1 - side, part)] = (
            unit_other * gain_other_ref[...].astype(f32)
        ).astype(b16)
        scales_ref[:, rows] = jnp.broadcast_to(scale, (block, 128)).T[0:8]


def norm(side, own, gain_own, gain_other, other):
    length, part = own.shape
    half = shape_of((length, part), b16)
    return pl.pallas_call(
        norm_kernel,
        in_specs=[smem()] + [vmem()] * 3 + [hbm()],
        out_specs=[vmem()] * 4,
        out_shape=[shape_of((length, 2 * part), b16), half, half, shape_of((8, length), f32)],
        scratch_shapes=buffers(other) + [pltpu.SemaphoreType.DMA((length // block,))],
        compiler_params=roomy(16),
        cost_estimate=cost(4),
        name="norm",
    )(side, own, gain_own, gain_other, in_hbm(other))


def front_kernel(
    taps_count,
    side_ref,
    seats_ref,
    normed_ref,
    wx_ref,
    wz_ref,
    params_ref,
    gate_ref,
    flipped_ref,
    upx_ref,
    upz_ref,
    conv_out_ref,
    slope_ref,
    q_ref,
    k_ref,
    v_ref,
    gates_ref,
    padded_ref,
):
    side = side_ref[0]
    length = normed_ref.shape[0]
    channels = wx_ref.shape[1]
    tap_count = taps_count
    steps = channels // group
    padded_ref[0:8, :] = jnp.zeros((8, group), f32)
    flip_rows = length // steps
    gates_ref[...] = jnp.zeros_like(gates_ref)

    @pl.loop(0, steps)
    def _(step):
        lanes = pl.ds(pl.multiple_of(step * group, group), group)
        upx = dot_nn(normed_ref[...], wx_ref[:, lanes])
        upx_b = upx.astype(b16)
        upx_ref[:, lanes] = upx_b
        padded_ref[pl.ds(8, length), :] = upx
        upz_ref[:, lanes] = dot_nn(normed_ref[...], wz_ref[:, lanes]).astype(b16)
        params = params_ref[:, lanes]
        taps = params[0:tap_count].astype(f32)
        bias = params[4 * tap_count : 4 * tap_count + 1].astype(f32)
        pre = bias + taps[tap_count - 1 : tap_count] * upx
        for tap in range(tap_count - 1):
            pre = pre + taps[tap : tap + 1] * padded_ref[pl.ds(8 - (tap_count - 1 - tap), length), :]
        gate = sigmoid(pre)
        conv_out = pre * gate
        conv_b = conv_out.astype(b16)
        conv_out_ref[:, lanes] = conv_b
        slope_ref[:, lanes] = (gate + conv_out * (1.0 - gate)).astype(b16)
        conv_low = (conv_out - conv_b.astype(f32)).astype(b16)
        upx_low = (upx - upx_b.astype(f32)).astype(b16)
        qd, kd, vd = (
            spread_taps(params[at * tap_count : (at + 1) * tap_count]) for at in range(1, 4)
        )
        q_b = (dot_nn(conv_b, qd) + dot_nn(conv_low, qd)).astype(b16)
        k_b = (dot_nn(conv_b, kd) + dot_nn(conv_low, kd)).astype(b16)
        v_b = (dot_nn(upx_b, vd) + dot_nn(upx_low, vd)).astype(b16)
        q_ref[:, lanes] = q_b
        k_ref[:, lanes] = k_b
        v_ref[:, lanes] = v_b
        gates_ref[...] += (
            dot_nt(gate_ref[0, :, lanes], q_b)
            + dot_nt(gate_ref[1, :, lanes], k_b)
            + dot_nt(gate_ref[2, :, lanes], v_b)
        )
        rows = pl.ds(pl.multiple_of(step * flip_rows, flip_rows), flip_rows)
        seat_rows(normed_ref[rows, :].T, seats_ref, flipped_ref.at[:, rows])


def front(side, seats, normed, wx, wz, params, gate, taps_count):
    length = normed.shape[0]
    width, channels = wx.shape
    full = shape_of((length, channels), b16)
    return pl.pallas_call(
        partial(front_kernel, taps_count),
        in_specs=[smem(), smem()] + [vmem()] * 5,
        out_specs=[vmem()] * 9,
        out_shape=[shape_of((width, length), b16)]
        + [full] * 7
        + [shape_of((gate.shape[1], length), f32)],
        scratch_shapes=[pltpu.VMEM((length + 8, group), f32)],
        compiler_params=roomy(16),
        cost_estimate=cost(14),
        name="front",
    )(side, seats, normed, wx, wz, params, gate)


def scan_lanes(values, combine, empty, reverse=False):
    length = values.shape[1]
    lane = lax.broadcasted_iota(jnp.int32, values.shape, 1)
    distance = 1
    while distance < length:
        if reverse:
            moved = pltpu.roll(values, length - distance, 1)
            inside = lane < length - distance
        else:
            moved = pltpu.roll(values, distance, 1)
            inside = lane >= distance
        values = combine(values, jnp.where(inside, moved, empty))
        distance *= 2
    return values


def pick(side, first, second):
    return jnp.where(side == 0, first, second)


def fold_rows(values):
    rows, lanes = values.shape
    return jnp.sum(values.reshape(rows // 8, 8, lanes), axis=0)


def cell_kernel(
    head_dim,
    side_ref,
    seats_ref,
    forget_ref,
    gates_own_ref,
    gates_other_ref,
    q_ref,
    k_ref,
    v_ref,
    conv_ref,
    upz_ref,
    flipped_ref,
    cot_own_ref,
    wd_ref,
    params_ref,
    cot_other_hbm,
    rows_ref,
    keep_ref,
    send_ref,
    dnum_ref,
    skip_grad_ref,
    upz_grad_ref,
    first_ref,
    second_ref,
    gains_ref,
    cols_ref,
    gated_t_ref,
    states_ref,
    gateds_ref,
    nums_ref,
    dens_ref,
    slacks_ref,
    sums_ref,
    cot_other_ref,
    sems,
):
    side = side_ref[0]
    length, channels = q_ref.shape
    heads = channels // head_dim
    gate_count = gates_own_ref.shape[0]
    all_heads = gate_count // 2
    part = cot_own_ref.shape[1]
    fetch = Fetch(sems)
    fetch(cot_other_hbm, cot_other_ref)

    gates = gates_own_ref[...] + gates_other_ref[...]
    inlet = pick(side, gates[:heads], gates[heads : 2 * heads])
    forget = pick(
        side, gates[all_heads : all_heads + heads], gates[all_heads + heads : gate_count]
    )
    forget = forget + jnp.concatenate(
        [jnp.full((1, length), forget_ref[side * heads + h], f32) for h in range(heads)], axis=0
    )
    log_forget = jnp.minimum(forget, 0.0) - jnp.log1p(jnp.exp(-jnp.abs(forget)))
    total = scan_lanes(log_forget, jnp.add, 0.0)
    ahead = inlet - total
    top = scan_lanes(jnp.maximum(ahead, 0.0), jnp.maximum, 0.0)
    floor = jnp.exp(-(total + top))
    rows_ref[...] = jnp.concatenate(
        [ahead + jnp.log(f32(head_dim**-0.5)), top, forget, jnp.zeros_like(top)], axis=0
    )
    cols_ref[...] = jnp.concatenate([top, floor, top, floor], axis=0).T
    sums_ref[...] = jnp.zeros_like(sums_ref)

    ones = jnp.ones((length, 128), b16)

    def attend(count):
        span = count * block
        here = pl.ds(span - block, block)
        slot = count % 2
        num_ref, den_ref, state_ref, gated_ref, slack_ref = (
            ref.at[slot] for ref in (nums_ref, dens_ref, states_ref, gateds_ref, slacks_ref)
        )
        pieces = []
        for h in range(heads):
            lanes = pl.ds(h * head_dim, head_dim)
            start = span - block
            top = cols_ref[pl.ds(start, block), h : h + 1]
            scores = dot_nt(q_ref[pl.ds(start, block), lanes], k_ref[pl.ds(0, span), lanes])
            done = []
            for piece in range(count):
                there = slice(piece * block, (piece + 1) * block)
                exponent = rows_ref[h : h + 1, there] - top
                if piece == count - 1:
                    row_ids = lax.broadcasted_iota(jnp.int32, (block, block), 0)
                    col_ids = lax.broadcasted_iota(jnp.int32, (block, block), 1)
                    exponent = jnp.where(row_ids >= col_ids, exponent, -jnp.inf)
                done.append((scores[:, there] * jnp.exp(exponent)).astype(b16))
            pieces.append(jnp.concatenate(done, axis=1))
        for h in range(heads):
            lanes = pl.ds(h * head_dim, head_dim)
            num_ref[:, lanes] = dot_nn(pieces[h], v_ref[pl.ds(0, span), lanes])
            den_ref[:, pl.ds(h * 128, 128)] = dot_nn(pieces[h], ones[:span])
        if count == 1:
            for copy in fetch.copies:
                copy.wait()
        state_ref[...] = dot_nt(cot_own_ref[here, :], wd_ref[:, side_cols(side, part)]) + dot_nt(
            cot_other_ref[here, :], wd_ref[:, side_cols(1 - side, part)]
        )

        small = 64
        floors = cols_ref[here, heads : 2 * heads]

        def tiles():
            for h in range(heads):
                for start in range(0, block, small):
                    yield h, start, pl.ds(start, small), pl.ds(h * head_dim, head_dim)

        stats = {}
        for h, start, rows, lanes in tiles():
            denominator = den_ref[rows, h * 128 : h * 128 + 1]
            floor = floors[start : start + small, h : h + 1]
            inverse = 1.0 / jnp.maximum(jnp.abs(denominator), floor)
            hidden = num_ref[rows, lanes] * inverse
            num_ref[rows, lanes] = hidden
            stats[h, start] = [
                inverse,
                jnp.where(jnp.abs(denominator) >= floor, jnp.where(denominator >= 0.0, inverse, -inverse), 0.0),
                jnp.mean(hidden, axis=1, keepdims=True),
            ]
        for h, start, rows, lanes in tiles():
            centered = num_ref[rows, lanes] - stats[h, start][2]
            num_ref[rows, lanes] = centered
            stats[h, start].append(
                lax.rsqrt(jnp.mean(centered * centered, axis=1, keepdims=True) + eps_norm)
            )
        gain_sums = [jnp.zeros((8, head_dim), f32)] * heads
        skip_sums = [jnp.zeros((8, head_dim), f32)] * heads
        for h, start, rows, lanes in tiles():
            gain = params_ref[17:18, lanes].astype(f32)
            skip = params_ref[18:19, lanes].astype(f32)
            unit = num_ref[rows, lanes] * stats[h, start][3]
            num_ref[rows, lanes] = unit
            conv_out = conv_ref[pl.ds(span - block + start, small), lanes].astype(f32)
            inner = unit * gain + skip * conv_out
            upz = upz_ref[pl.ds(span - block + start, small), lanes].astype(f32)
            gate = sigmoid(upz)
            active = upz * gate
            gated_ref[rows, lanes] = (inner * active).astype(b16)
            grad_state = state_ref[rows, lanes]
            grad_inner = grad_state * active
            upz_grad_ref[pl.ds(span - block + start, small), lanes] = (
                grad_state * inner * (gate + active * (1.0 - gate))
            ).astype(b16)
            skip_grad_ref[pl.ds(span - block + start, small), lanes] = (grad_inner * skip).astype(b16)
            along = grad_inner * unit
            gain_sums[h] = gain_sums[h] + fold_rows(along)
            skip_sums[h] = skip_sums[h] + fold_rows(grad_inner * conv_out)
            grad_unit = grad_inner * gain
            state_ref[rows, lanes] = grad_unit
            stats[h, start] += [
                jnp.mean(grad_unit, axis=1, keepdims=True),
                jnp.mean(along * gain, axis=1, keepdims=True),
            ]
        for h, start, rows, lanes in tiles():
            inverse, signed, _, scale, mean, moment = stats[h, start]
            dnum_ref[pl.ds(span - block + start, small), lanes] = (
                (state_ref[rows, lanes] - mean - num_ref[rows, lanes] * moment) * (scale * inverse)
            ).astype(b16)
            slack = -signed * moment * (head_dim * eps_norm) * scale * scale
            slack_ref[rows, pl.ds(h * 128, 128)] = jnp.broadcast_to(slack, (small, 128))
        for h in range(heads):
            lanes = pl.ds(h * head_dim, head_dim)
            sums_ref[0:8, lanes] += gain_sums[h]
            sums_ref[8:16, lanes] += skip_sums[h]
        for h in range(heads):
            rows_ref[3 * heads + h : 3 * heads + h + 1, here] = slack_ref[:, pl.ds(h * 128, 128)].T[0:1]
        gated = gated_ref[...]
        keep_ref[here, :] = dot_nn(gated, wd_ref[:, side_cols(side, part)]).astype(b16)
        send_ref[here, :] = dot_nn(gated, wd_ref[:, side_cols(1 - side, part)]).astype(b16)
        seat_rows(gated.T, seats_ref, gated_t_ref.at[:, here])


    for count in range(1, length // block + 1):
        pl.when(side >= 0)(partial(attend, count))
    gains_ref[0:1, :] = jnp.sum(sums_ref[0:8, :], axis=0, keepdims=True)
    gains_ref[1:2, :] = jnp.sum(sums_ref[8:16, :], axis=0, keepdims=True)
    gains_ref[2:8, :] = jnp.zeros((6, channels), f32)
    half = first_ref.shape[0]
    width = 2 * part
    for start in range(0, 2 * half, block):
        out_ref = (first_ref if start < half else second_ref).at[pl.ds(start % half, block), :]
        rows = pl.ds(start, block)
        turned = gated_t_ref[rows, :]
        out_ref[:, side_cols(side, part)] = dot_nn(turned, cot_own_ref[...]).astype(b16)
        out_ref[:, side_cols(1 - side, part)] = dot_nn(turned, cot_other_ref[...]).astype(b16)
        out_ref[:, pl.ds(width, channels)] = dot_nn(
            flipped_ref[rows, :], upz_grad_ref[...]
        ).astype(b16)


def cell(
    side, seats, forget, gates_own, gates_other, q, k, v, conv, upz, flipped, cot_own, cot_other, wd,
    params, head_dim,
):
    length, channels = q.shape
    part = cot_own.shape[1]
    width = wd.shape[1]
    gate_count = gates_own.shape[0]
    heads = channels // head_dim

    return pl.pallas_call(
        partial(cell_kernel, head_dim),
        in_specs=[smem()] * 3 + [vmem()] * 11 + [hbm()],
        out_specs=[vmem()] * 9,
        out_shape=[
            shape_of((8, length), f32),
            shape_of((length, part), b16),
            shape_of((length, part), b16),
            shape_of((length, channels), b16),
            shape_of((length, channels), b16),
            shape_of((length, channels), b16),
            shape_of((channels // 2, width + channels), b16),
            shape_of((channels // 2, width + channels), b16),
            shape_of((8, channels), f32),
        ],
        scratch_shapes=[
            pltpu.VMEM((length, 8), f32),
            pltpu.VMEM((channels, length), b16),
            pltpu.VMEM((2, block, channels), f32),
            pltpu.VMEM((2, block, channels), b16),
            pltpu.VMEM((2, block, channels), f32),
            pltpu.VMEM((2, block, heads * 128), f32),
            pltpu.VMEM((2, block, heads * 128), f32),
            pltpu.VMEM((16, channels), f32),
        ]
        + buffers(cot_other)
        + [pltpu.SemaphoreType.DMA((1,))],
        compiler_params=roomy(16),
        cost_estimate=cost(25),
        name="cell",
    )(side, seats, forget, gates_own, gates_other, q, k, v, conv, upz, flipped, cot_own, wd,
      params, in_hbm(cot_other))


def cell_back_kernel(
    h, heads, q_ref, k_ref, v_ref, dnum_ref, rows_ref, prior_ref, dq_ref, dk_ref, dv_ref, gates_ref,
    grads_ref, pair_ref,
):
    length, head_dim = dq_ref.shape
    lanes = pl.ds(h * head_dim, head_dim)
    gates_ref[...] = prior_ref[...]
    ahead = rows_ref[...].T[:, h : h + 1]
    row_ids = lax.broadcasted_iota(jnp.int32, (block, block), 0)
    col_ids = lax.broadcasted_iota(jnp.int32, (block, block), 1)
    blocks = length // block
    for s in range(blocks):
        there = pl.ds(s * block, block)
        span = length - s * block
        after = pl.ds(s * block, span)
        keys = k_ref[there, lanes]
        scores = dot_nt(keys, q_ref[after, lanes])
        grads = dot_nt(v_ref[there, lanes], dnum_ref[after, lanes])
        scored, graded = [], []
        for t in range(s, blocks):
            here = pl.ds(t * block, block)
            at = slice((t - s) * block, (t - s + 1) * block)
            exponent = ahead[s * block : (s + 1) * block] - rows_ref[heads + h : heads + h + 1, here]
            if s == t:
                exponent = jnp.where(row_ids <= col_ids, exponent, -jnp.inf)
            weight = jnp.exp(exponent)
            slack = rows_ref[3 * heads + h : 3 * heads + h + 1, here]
            scored.append((scores[:, at] * weight).astype(b16))
            graded.append(((grads[:, at] + slack) * weight).astype(b16))
            grads_ref[there, here] = graded[-1]
        dv_ref[there, :] = dot_nn(
            jnp.concatenate(scored, axis=1), dnum_ref[after, lanes]
        ).astype(b16)
        dk = dot_nn(jnp.concatenate(graded, axis=1), q_ref[after, lanes])
        dk_ref[there, :] = dk.astype(b16)
        pair_ref[there, 128:256] = jnp.broadcast_to(
            jnp.sum(dk * keys.astype(f32), axis=1, keepdims=True), (block, 128)
        )
    for t in range(blocks):
        here = pl.ds(t * block, block)
        before = pl.ds(0, (t + 1) * block)
        dq = dot_tn(grads_ref[before, here], k_ref[before, lanes])
        dq_ref[here, :] = dq.astype(b16)
        pair_ref[here, 0:128] = jnp.broadcast_to(
            jnp.sum(dq * q_ref[here, lanes].astype(f32), axis=1, keepdims=True), (block, 128)
        )
    outward = pair_ref[:, 0:128].T[0:1]
    inward = pair_ref[:, 128:256].T[0:1]
    forget = rows_ref[2 * heads + h : 2 * heads + h + 1, :]
    grad_log = scan_lanes(jnp.broadcast_to(outward - inward, (8, length)), jnp.add, 0.0, True)[0:1]
    gates_ref[h : h + 1, :] = inward
    gates_ref[heads + h : heads + h + 1, :] = grad_log * sigmoid(-forget)


def cell_back(q, k, v, dnum, rows, prior, h, head_dim):
    length, channels = q.shape
    heads = channels // head_dim
    full = shape_of((length, head_dim), b16)
    return pl.pallas_call(
        partial(cell_back_kernel, h, heads),
        in_specs=[vmem()] * 6,
        out_specs=[vmem()] * 4,
        out_shape=[full, full, full, shape_of((8, length), f32)],
        scratch_shapes=[pltpu.VMEM((length, length), b16), pltpu.VMEM((length, 256), f32)],
        compiler_params=roomy(16),
        cost_estimate=cost(7),
        name="cell_back",
    )(q, k, v, dnum, rows, prior)


def front_back_kernel(
    tap_count,
    heads,
    index,
    reseat,
    side_ref,
    table_ref,
    gates_own_ref,
    gates_other_ref,
    dq_ref,
    dk_ref,
    dv_ref,
    q_ref,
    k_ref,
    v_ref,
    conv_out_ref,
    slope_ref,
    upx_ref,
    skip_grad_ref,
    flipped_ref,
    params_ref,
    gate_ref,
    *refs,
):
    last = index == heads - 1
    if last:
        gains_ref, *refs = refs
        prior_refs, refs = refs[:index], refs[index:]
    upx_grad_ref, first_ref, second_ref, small_ref, padded_refs, turned_ref = refs
    side = side_ref[0]
    length, span = upx_grad_ref.shape
    own = gates_own_ref[...]
    other = gates_other_ref[...]
    gates = jnp.concatenate(
        [
            pick(side, own[:heads], other[:heads]),
            pick(side, other[:heads], own[:heads]),
            pick(side, own[heads : 2 * heads], other[heads : 2 * heads]),
            pick(side, other[heads : 2 * heads], own[heads : 2 * heads]),
        ],
        axis=0,
    )
    gates_t = gates.T.astype(b16)
    gates_b = gates.astype(b16)
    padded_refs[:, length : length + 8, :] = jnp.zeros((2, 8, group), f32)
    half = first_ref.shape[0]
    height = half // len(reseat)
    for step in range(span // group):
        padded_ref = padded_refs.at[step % 2]
        near = pl.ds(step * group, group)
        lanes = pl.ds(index * span + step * group, group)
        dq_b = (dq_ref[:, near].astype(f32) + dot_nn(gates_t, gate_ref[0, :, lanes])).astype(b16)
        dk_b = (dk_ref[:, near].astype(f32) + dot_nn(gates_t, gate_ref[1, :, lanes])).astype(b16)
        dv_b = (dv_ref[:, near].astype(f32) + dot_nn(gates_t, gate_ref[2, :, lanes])).astype(b16)
        conv_out = conv_out_ref[:, lanes]
        params = params_ref[:, lanes]
        upx_b = upx_ref[:, lanes]
        grad_conv = (
            skip_grad_ref[:, lanes].astype(f32)
            + dot_nt(dq_b, spread_taps(params[tap_count : 2 * tap_count]))
            + dot_nt(dk_b, spread_taps(params[2 * tap_count : 3 * tap_count]))
        )
        grad_pre = grad_conv * slope_ref[:, lanes].astype(f32)
        padded_ref[0:length, :] = grad_pre
        taps = params[0:tap_count].astype(f32)
        upx = upx_b.astype(f32)
        grad_upx = (
            dot_nt(dv_b, spread_taps(params[3 * tap_count : 4 * tap_count]))
            + taps[tap_count - 1 : tap_count] * grad_pre
        )
        tap_grads = [jnp.sum(upx * grad_pre, axis=0, keepdims=True)]
        for tap in range(tap_count - 2, -1, -1):
            moved = padded_ref[tap_count - 1 - tap : tap_count - 1 - tap + length, :]
            grad_upx = grad_upx + taps[tap : tap + 1] * moved
            tap_grads.insert(0, jnp.sum(upx * moved, axis=0, keepdims=True))
        grad_b = grad_upx.astype(b16)
        upx_grad_ref[:, near] = grad_b
        for start, out_ref in ((0, first_ref), (half, second_ref)):
            result = dot_nn(flipped_ref[start : start + half, :], grad_b).astype(b16)
            for seat, source in enumerate(reseat):
                out_ref[seat * height : (seat + 1) * height, near] = result[
                    source * height : (source + 1) * height
                ]
        small_ref[:, near] = jnp.concatenate(
            tap_grads
            + [
                gather_taps(dot_tn(conv_out, dq_b), tap_count),
                gather_taps(dot_tn(conv_out, dk_b), tap_count),
                gather_taps(dot_tn(upx_b, dv_b), tap_count),
                dot_nn(gates_b, q_ref[:, lanes]),
                dot_nn(gates_b, k_ref[:, lanes]),
                dot_nn(gates_b, v_ref[:, lanes]),
                jnp.broadcast_to(jnp.sum(gates, axis=1, keepdims=True), (gates.shape[0], group)),
                jnp.sum(grad_pre, axis=0, keepdims=True),
                jnp.zeros((7, group), f32),
            ],
            axis=0,
        )
    if last:
        small = jnp.concatenate([ref[...] for ref in (*prior_refs, small_ref)], axis=1)
        split = 4 * tap_count + 3 * gates.shape[0]
        stacked = jnp.concatenate(
            [
                small[:split],
                small[split + gates.shape[0] : split + gates.shape[0] + 1],
                gains_ref[0:2, :],
                jnp.zeros((128 - split - 3, small.shape[1]), f32),
            ],
            axis=0,
        )
        turned_ref[...] = stacked.T
        for seat in range(2 * len(reseat)):
            out_ref = first_ref if seat < len(reseat) else second_ref
            start = seat % len(reseat) * height
            out_ref[start : start + height, span : span + 128] = turned_ref[
                pl.ds(pl.multiple_of(table_ref[seat] * height, height), height), :
            ].astype(b16)


def front_back(
    side, table, gates_own, gates_other, dq, dk, dv, q, k, v, conv_out, slope, upx, skip_grad, flipped,
    params, gate, gains, priors, tap_count, heads, index, reseat,
):
    length, channels = q.shape
    width = flipped.shape[0]
    last = index == heads - 1
    span = channels // heads
    out_width = span + (128 if last else 0)
    extra = [gains, *priors] if last else []
    return pl.pallas_call(
        partial(front_back_kernel, tap_count, heads, index, reseat),
        in_specs=[smem(), smem()] + [vmem()] * (15 + len(extra)),
        out_specs=[vmem()] * 4,
        out_shape=[
            shape_of((length, span), b16),
            shape_of((width // 2, out_width), b16),
            shape_of((width // 2, out_width), b16),
            shape_of((56, span), f32),
        ],
        scratch_shapes=[
            pltpu.VMEM((2, length + 8, group), f32),
            pltpu.VMEM((channels, 128), f32),
        ],
        compiler_params=roomy(16),
        cost_estimate=cost(8),
        name="front_back",
    )(side, table, gates_own, gates_other, dq, dk, dv, q, k, v, conv_out, slope, upx, skip_grad,
      flipped, params, gate, *extra)


def norm_back_kernel(
    parts, side_ref, upz_grad_ref, wx_ref, wz_ref, unit_own_ref, unit_other_ref, gain_own_ref,
    gain_other_ref, *refs,
):
    upx_grad_refs = refs[:parts]
    keep_ref, send_ref, stats_ref = refs[parts:]
    side = side_ref[0]
    length, part = unit_own_ref.shape
    gain_sums = [jnp.zeros((8, part), f32)] * 2
    for start in range(0, length, block):
        here = pl.ds(start, block)
        sums = []
        for index, (unit_ref, place, gain_ref, out_ref) in enumerate(
            [
                (unit_own_ref, side, gain_own_ref, keep_ref),
                (unit_other_ref, 1 - side, gain_other_ref, send_ref),
            ]
        ):
            rows = side_cols(place, part)
            terms = dot_nt(upz_grad_ref[here, :], wz_ref[rows, :])
            for index_part, grad_ref in enumerate(upx_grad_refs):
                span = grad_ref.shape[1]
                lanes = pl.ds(index_part * span, span)
                terms = terms + dot_nt(grad_ref[here, :], wx_ref[rows, lanes])
            out_ref[here, :] = terms.astype(b16)
            along = terms * unit_ref[here, :].astype(f32)
            gain_sums[index] = gain_sums[index] + fold_rows(along)
            gain = gain_ref[...].astype(f32)
            sums.append(
                (
                    jnp.sum(terms * gain, axis=1, keepdims=True),
                    jnp.sum(along * gain, axis=1, keepdims=True),
                )
            )
        for row in range(2):
            stats_ref[row : row + 1, here] = jnp.broadcast_to(
                sums[0][row] + sums[1][row], (block, 128)
            ).T[0:1]
    stats_ref[2:8, :] = jnp.zeros((6, length), f32)
    for row, total in ((2, gain_sums[1]), (3, gain_sums[0])):
        stats_ref[row : row + 1, 0:part] = jnp.sum(total, axis=0, keepdims=True)


def norm_back(side, upx_grads, upz_grad, wx, wz, own, other, gain_own, gain_other):
    length, channels = upz_grad.shape
    parts = len(upx_grads)
    part = own.shape[1]
    return pl.pallas_call(
        partial(norm_back_kernel, parts),
        in_specs=[smem()] + [vmem()] * (7 + parts),
        out_specs=[vmem()] * 3,
        out_shape=[
            shape_of((length, part), b16),
            shape_of((length, part), b16),
            shape_of((8, max(length, part)), f32),
        ],
        compiler_params=roomy(16),
        cost_estimate=cost(9),
        name="norm_back",
    )(side, upz_grad, wx, wz, own, other, gain_own, gain_other, *upx_grads)


def seat_back(table_ref, near_ref, far_ref, out_ref):
    pieces = table_ref.shape[0]
    height = out_ref.shape[0] // pieces
    for seat in range(pieces):
        source = near_ref if seat < pieces // 2 else far_ref
        start = seat % (pieces // 2) * height
        out_ref[pl.ds(pl.multiple_of(table_ref[seat] * height, height), height), :] = source[
            start : start + height, :
        ].astype(f32)


def place_rows(table, pair):
    near, far = pair
    half, width = near.shape
    source = spec((half, group), lambda c: (0, c))
    return pl.pallas_call(
        seat_back,
        grid=(width // group,),
        in_specs=[smem(), source, source],
        out_specs=spec((2 * half, group), lambda c: (0, c)),
        out_shape=shape_of((2 * half, width), f32),
        compiler_params=settings(16),
        cost_estimate=cost(3),
        name="place_rows",
    )(table, near, far)


def place_last_kernel(
    taps, gate_count, mixed_ref, far_table_ref, near_ref, far_ref, near_two_ref, far_two_ref,
    near_small_ref, far_small_ref, out_ref, conv_ref, q_ref, k_ref, v_ref, bias_ref, gain_ref,
    skip_ref, gate_ref, turned_ref,
):
    step = pl.program_id(0)
    middle = pl.num_programs(0) // 2

    @pl.when(step == 0)
    def _():
        seat_back(far_table_ref, near_small_ref, far_small_ref, turned_ref)
        flat = turned_ref[...].T
        for at, ref in enumerate((conv_ref, q_ref, k_ref, v_ref)):
            ref[...] = flat[at * taps : (at + 1) * taps]
        start = 4 * taps
        for part in range(3):
            gate_ref[part, :, :] = turned_ref[
                :, start + part * gate_count : start + (part + 1) * gate_count
            ]
        start += 3 * gate_count
        for at, ref in enumerate((bias_ref, gain_ref, skip_ref)):
            ref[...] = flat[start + at : start + at + 1]

    @pl.when(step < middle)
    def _():
        seat_back(mixed_ref, near_ref, far_ref, out_ref)

    @pl.when(step >= middle)
    def _():
        seat_back(far_table_ref, near_two_ref, far_two_ref, out_ref)


def place_last(mixed_table, far_table, pair, pair_two, taps, gate_count):
    half, width = pair[0].shape
    steps = width // group
    channels = 2 * half

    def source(first):
        return spec((half, group), lambda c: (0, jnp.clip(c - first, 0, steps - 1)))

    small = spec((half, 128), lambda c: (0, width // 128))
    row = shape_of((1, channels), f32)
    tap_rows = shape_of((taps, channels), f32)
    shapes = [tap_rows] * 4 + [row] * 3 + [shape_of((3, channels, gate_count), f32)]
    return pl.pallas_call(
        partial(place_last_kernel, taps, gate_count),
        grid=(2 * steps,),
        in_specs=[smem(), smem(), source(0), source(0), source(steps), source(steps), small, small],
        out_specs=[spec((2 * half, group), lambda c: (0, c))] + [whole(v.shape) for v in shapes],
        out_shape=[shape_of((2 * half, 2 * width), f32)] + shapes,
        scratch_shapes=[pltpu.VMEM((channels, 128), f32)],
        compiler_params=settings(16),
        cost_estimate=cost(5),
        name="place_last",
    )(mixed_table, far_table, *pair, *pair_two, *pair_two)


def finish_kernel(
    unit_ref, scales_ref, gain_ref, keep_ref, recv_ref, stats_own_ref, stats_other_ref,
    cot_ref, out_ref,
):
    length, part = unit_ref.shape
    width = 2 * part
    gain = gain_ref[...].astype(f32)
    for start in range(0, length, block):
        here = pl.ds(start, block)
        unit = unit_ref[here, :].astype(f32)
        scale = scales_ref[:, here].T[:, 0:1]
        stats = (stats_own_ref[:, here] + stats_other_ref[:, here]).T
        terms = keep_ref[here, :].astype(f32) + recv_ref[here, :].astype(f32)
        pulled = terms * gain - (stats[:, 0:1] + unit * stats[:, 1:2]) / width
        out_ref[here, :] = cot_ref[here, :].astype(f32) + pulled * scale


def finish(unit, scales, gain, keep, recv, stats_own, stats_other, cot):
    return pl.pallas_call(
        finish_kernel,
        in_specs=[vmem()] * 8,
        out_specs=vmem(),
        out_shape=shape_of(unit.shape, f32),
        compiler_params=roomy(16),
        cost_estimate=cost(4),
        name="finish",
    )(unit, scales, gain, keep, recv, stats_own, stats_other, cot)


def swap(values):
    return lax.ppermute(values, "head", [(0, 1), (1, 0)])


def across(values, bit, count):
    return lax.ppermute(values, "dp", [(i, i ^ (1 << bit)) for i in range(count)])


def add_halves(first, second):
    return (first.astype(f32) + second.astype(f32)).astype(first.dtype)


class Reduction:
    def __init__(self, keep, out, order, bits, count, step=0):
        self.keep, self.out, self.count = keep, out, count
        self.plan = (
            [("half", bit) for bit in order]
            + [("full", bit) for bit in range(len(order), bits)]
            + [("copy", bit) for bit in reversed(order)]
        )
        self.step = step

    def send(self):
        if not self.more():
            return None
        self.got = across(self.keep if self.out is None else self.out, self.plan[self.step][1], self.count)
        return self.got

    def take(self, got=None):
        if not self.more():
            return
        got = self.got if got is None else got
        kind, bit = self.plan[self.step]
        self.step += 1
        after = self.plan[self.step][0] if self.step < len(self.plan) else "end"
        if kind == "copy":
            if after == "end":
                self.result = (self.keep, got)
            else:
                self.keep = jnp.concatenate([self.keep, got], axis=0)
                self.out = None
        elif after == "half":
            half = self.keep.shape[0] // 2
            self.out = add_halves(self.keep[half:], got[half:])
            self.keep = add_halves(self.keep[:half], got[:half])
        else:
            self.keep = add_halves(self.keep, got)
            self.out = None

    def more(self):
        return self.step < len(self.plan)


def arrange(order, place):
    levels = len(order)
    return sum((((place >> bit) & 1) << (levels - 1 - at)) for at, bit in enumerate(order))


def settle(value, *flows):
    flows = [flow for flow in flows if flow.more()]
    value, gots = lax.optimization_barrier((value, [flow.got for flow in flows]))
    for flow, got in zip(flows, gots):
        flow.take(got)
    flows = [flow for flow in flows if flow.more()]
    held = [(flow.keep, flow.out) for flow in flows]
    value, held = lax.optimization_barrier((value, held))
    for flow, (keep, out) in zip(flows, held):
        flow.keep, flow.out = keep, out
    return value


def send_all(flows):
    for flow in flows:
        flow.send()


def on_device(
    layer_input,
    ln_gain,
    up_x_weight,
    up_z_weight,
    conv_weight,
    conv_bias,
    query_weight,
    key_weight,
    value_weight,
    gate_weight,
    forget_bias,
    norm_gain,
    skip_gain,
    down_weight,
    cotangent,
):
    head_index = lax.axis_index("head")
    place = lax.axis_index("dp")
    count = lax.axis_size("dp")
    side = head_index.astype(jnp.int32).reshape(1)
    part = layer_input.shape[1]
    channels = up_x_weight.shape[1]
    all_heads = gate_weight.shape[2] // 2
    heads = all_heads // lax.axis_size("head")
    head_dim = channels // heads
    taps = conv_weight.shape[0]
    bits = count.bit_length() - 1
    levels = min(bits, 3)
    near_order = list(range(levels))
    far_order = near_order[:1] + near_order[2:3] + near_order[1:2] + near_order[3:]
    pieces = 2**levels
    turned = [0] * pieces
    for relative in range(pieces):
        turned[arrange(near_order, relative)] = arrange(far_order, relative)
    seats = jnp.arange(pieces, dtype=jnp.int32)
    near_table = (seats ^ arrange(near_order, place)).astype(jnp.int32)
    far_table = (seats ^ arrange(far_order, place)).astype(jnp.int32)
    mixed_table = (jnp.array(turned, jnp.int32) ^ arrange(far_order, place)).astype(jnp.int32)
    middle = max(pieces // 2, 1)
    straight = list(range(middle))
    mixed = [turned[seat] for seat in range(middle)]

    gain_own = ln_gain.reshape(1, part)
    gain_other = swap(gain_own)
    input_other = swap(layer_input)
    gate_t = gate_weight.transpose(0, 2, 1)
    input_v, wx_v, wz_v, wd_v, cot_v, params = stage(
        [layer_input, up_x_weight, up_z_weight, down_weight, cotangent],
        [conv_weight, query_weight, key_weight, value_weight]
        + [values.reshape(1, channels) for values in (conv_bias, norm_gain, skip_gain)],
    )
    normed, unit_own, unit_other, scales = norm(side, input_v, gain_own, gain_other, input_other)
    cot_start, normed = lax.optimization_barrier((cotangent, normed))
    cot_other = swap(cot_start)
    flipped, upx, upz, conv_out, slope, q, k, v, gates = front(
        side, far_table, normed, wx_v, wz_v, params, gate_t, taps
    )
    gates_other = swap(gates)
    rows, keep, send, dnum, skip_grad, upz_grad, early_keep, early_send, gains = cell(
        side, near_table, forget_bias.astype(f32), gates, gates_other, q, k, v, conv_out, upz,
        flipped, cot_v, cot_other, wd_v, params, head_dim,
    )
    width = down_weight.shape[1]
    down_other = swap(send)
    got = across(early_send, near_order[0], count)
    grads = [cell_back(q, k, v, dnum, rows, rows, 0, head_dim)]
    prior, got = lax.optimization_barrier((grads[0][3], got))
    first = Reduction(early_keep[:, :width], None, near_order, bits, count)
    second = Reduction(early_keep[:, width:], None, far_order, bits, count)
    first.got, second.got = got[:, :width], got[:, width:]
    prior = settle(prior, first, second)
    first.send()
    second.send()
    gate_grads = cell_back(q, k, v, dnum, rows, prior, 1, head_dim)
    grads.append(gate_grads)
    gate_grads = settle(gate_grads[3], first, second)
    gate_grads_other = swap(gate_grads)
    first.send()
    second.send()
    late = []
    upx_grads = []
    smalls = []

    def back(index, order, reseat):
        dq, dk, dv, _ = grads[index]
        upx_grad, late_keep, late_send, small = front_back(
            side, far_table, gate_grads, gate_grads_other, dq, dk, dv, q, k, v, conv_out, slope,
            upx, skip_grad, flipped, params, gate_t, gains, list(smalls), taps, heads, index, reseat,
        )
        upx_grads.append(upx_grad)
        smalls.append(small)
        late.append(Reduction(late_keep, late_send, order, bits, count))
        late[-1].send()

    back(0, near_order, mixed)
    layer_output = (
        layer_input.astype(f32) + keep.astype(f32) + down_other.astype(f32)
    ).astype(b16)
    gate_grads_other, layer_output = settle((gate_grads_other, layer_output), first, second)
    send_all([first, second])
    back(1, far_order, straight)
    upx_grads[1] = settle(upx_grads[1], *late)
    send_all(late)
    terms = norm_back(
        side, upx_grads, upz_grad, up_x_weight, up_z_weight, unit_own, unit_other, gain_own,
        gain_other,
    )
    flows = [first, second, *late]
    terms_keep, terms_send, stats = settle(terms, *flows)
    stats_other = swap(stats)
    terms_other = swap(terms_send)
    send_all(flows)
    stats_other = settle(stats_other, *flows)
    sums = smalls[0][-12:-8, 0]
    tiny = jnp.concatenate([stats[3, :part] + stats_other[2, :part], sums, jnp.zeros((124,), f32)])
    flows.append(Reduction(tiny.reshape(-1, 128), None, [], bits, count))
    send_all(flows)
    settle((), *flows)
    send_all(flows)
    terms_other = settle(terms_other, *flows)
    send_all(flows)
    input_grad = finish(
        unit_own, scales, gain_own, terms_keep, terms_other, stats, stats_other, cotangent
    )
    input_grad = settle(input_grad, *flows)
    while any(flow.more() for flow in flows):
        send_all(flows)
        settle((), *flows)
    grad_down = place_rows(near_table, first.result)
    grad_upz = place_rows(far_table, second.result)
    grad_upx, conv_grad, q_grad, k_grad, v_grad, bias_grad, gain_grad, skip_sum, gate_grad = (
        place_last(mixed_table, far_table, late[0].result, late[1].result, taps, 2 * all_heads)
    )
    tiny = flows[-1].keep.reshape(-1)
    return (
        layer_output,
        input_grad,
        tiny[:part],
        grad_upx,
        grad_upz,
        conv_grad,
        bias_grad.reshape(-1),
        q_grad,
        k_grad,
        v_grad,
        gate_grad,
        tiny[part : part + all_heads],
        gain_grad.reshape(-1),
        skip_sum.reshape(-1),
        grad_down,
    )


def solution(mesh):
    in_specs = (
        P("dp", "head"),
        P("head"),
        P(None, "head"),
        P(None, "head"),
        P(None, "head"),
        P("head"),
        P(None, "head"),
        P(None, "head"),
        P(None, "head"),
        P(None, "head", None),
        P(),
        P("head"),
        P("head"),
        P("head", None),
        P("dp", "head"),
    )
    out_specs = (
        P("dp", "head"),
        P("dp", "head"),
        P("head"),
        P(None, "head"),
        P(None, "head"),
        P(None, "head"),
        P("head"),
        P(None, "head"),
        P(None, "head"),
        P(None, "head"),
        P(None, "head", None),
        P(),
        P("head"),
        P("head"),
        P("head", None),
    )
    return jax.shard_map(
        on_device, mesh=mesh, in_specs=in_specs, out_specs=out_specs, check_vma=False
    )
```

```python
from functools import partial

import jax
import jax.numpy as jnp
from jax import lax
from jax.experimental import pallas as pl
from jax.experimental.pallas import tpu as pltpu
from jax.sharding import PartitionSpec as P

eps_norm = 1e-05
group = 256
block = 256
b16 = jnp.bfloat16
f32 = jnp.float32


def dot_nn(first, second):
    return lax.dot_general(first, second, (((1,), (0,)), ((), ())), preferred_element_type=f32)


def dot_nt(first, second):
    return lax.dot_general(first, second, (((1,), (1,)), ((), ())), preferred_element_type=f32)


def dot_tn(first, second):
    return lax.dot_general(first, second, (((0,), (0,)), ((), ())), preferred_element_type=f32)


def sigmoid(values):
    return 0.5 * jnp.tanh(0.5 * values) + 0.5


def spec(shape, index_map):
    return pl.BlockSpec(shape, index_map)


def whole(shape):
    return pl.BlockSpec(shape, lambda *_: (0,) * len(shape))


def smem():
    return pl.BlockSpec(memory_space=pltpu.SMEM)


def shape_of(shape, dtype):
    return jax.ShapeDtypeStruct(shape, dtype)


def vmem():
    return pl.BlockSpec(memory_space=pltpu.VMEM)


def hbm():
    return pl.BlockSpec(memory_space=pltpu.HBM)


def roomy(mebibytes):
    return pltpu.CompilerParams(vmem_limit_bytes=mebibytes * 2**20)


def settings(mebibytes):
    return pltpu.CompilerParams(
        dimension_semantics=("arbitrary",), vmem_limit_bytes=mebibytes * 2**20
    )


def cost(micros):
    return pl.CostEstimate(
        flops=int(micros * 1.1e9), bytes_accessed=int(micros * 3.6e6), transcendentals=0
    )


def side_cols(side, width):
    return pl.ds(pl.multiple_of(side * width, width), width)


def spread_taps(taps):
    tap_count, width = taps.shape
    rows = lax.broadcasted_iota(jnp.int32, (width, width), 0) // tap_count
    cols = lax.broadcasted_iota(jnp.int32, (width, width), 1) // tap_count
    pair = jnp.concatenate([taps.astype(f32)] * (8 // tap_count), axis=0)
    full = jnp.concatenate([pair] * (width // 8), axis=0)
    return jnp.where(rows == cols, full, 0.0).astype(b16)


def gather_taps(dense, tap_count):
    width = dense.shape[0]
    rows = lax.broadcasted_iota(jnp.int32, (width, width), 0) // tap_count
    cols = lax.broadcasted_iota(jnp.int32, (width, width), 1) // tap_count
    kept = jnp.where(rows == cols, dense, 0.0)
    folded = jnp.sum(kept.reshape(width // 8, 8, width), axis=0)
    total = folded[:tap_count]
    for part in range(1, 8 // tap_count):
        total = total + folded[part * tap_count : (part + 1) * tap_count]
    return total


def row_stats(own, other):
    width = own.shape[1] + other.shape[1]
    total = jnp.sum(own, axis=1, keepdims=True) + jnp.sum(other, axis=1, keepdims=True)
    square = jnp.sum(own * own, axis=1, keepdims=True) + jnp.sum(
        other * other, axis=1, keepdims=True
    )
    center = total / width
    return center, lax.rsqrt(square / width - center * center + eps_norm)


def seat_rows(values, seats_ref, out_ref):
    seats = seats_ref.shape[0]
    height = values.shape[0] // seats
    for piece in range(seats):
        out_ref[pl.ds(pl.multiple_of(seats_ref[piece] * height, height), height), :] = values[
            piece * height : (piece + 1) * height
        ]


class Fetch:
    def __init__(self, sems):
        self.sems, self.copies = sems, []

    def __call__(self, source, target):
        copy = pltpu.make_async_copy(source, target, self.sems.at[len(self.copies)])
        copy.start()
        self.copies.append(copy)
        return copy


def buffers(*operands):
    return [pltpu.VMEM(value.shape, value.dtype) for value in operands]


def in_hbm(values):
    return pltpu.with_memory_space_constraint(values, pltpu.HBM)


def stage_kernel(count, taps_count, *refs):
    sources, smalls, targets = refs[:count], refs[count : count + 7], refs[count + 7 : 2 * count + 7]
    params_ref, sems = refs[2 * count + 7 :]
    fetch = Fetch(sems)
    for source, target in zip(sources, targets):
        fetch(source, target)
    rows = [ref[...].astype(f32) for ref in smalls]
    filled = sum(row.shape[0] for row in rows)
    rows.append(jnp.zeros((params_ref.shape[0] - filled, params_ref.shape[1]), f32))
    params_ref[...] = jnp.concatenate(rows, axis=0).astype(b16)
    for copy in fetch.copies:
        copy.wait()


def stage(arrays, smalls):
    count = len(arrays)
    params = shape_of((32, smalls[0].shape[1]), b16)
    return pl.pallas_call(
        partial(stage_kernel, count, smalls[0].shape[0]),
        in_specs=[hbm()] * count + [vmem()] * len(smalls),
        out_specs=[vmem()] * (count + 1),
        out_shape=[shape_of(value.shape, value.dtype) for value in arrays] + [params],
        scratch_shapes=[pltpu.SemaphoreType.DMA((count,))],
        compiler_params=roomy(16),
        cost_estimate=cost(4),
        name="stage",
    )(*[in_hbm(value) for value in arrays], *smalls)


def norm_kernel(
    side_ref, own_ref, gain_own_ref, gain_other_ref, other_ref, normed_ref, unit_own_ref,
    unit_other_ref, scales_ref,
):
    side = side_ref[0]
    length, part = own_ref.shape
    for start in range(0, length, block):
        rows = pl.ds(start, block)
        own = own_ref[rows, :].astype(f32)
        other = other_ref[rows, :].astype(f32)
        center, scale = row_stats(own, other)
        unit_own = (own - center) * scale
        unit_other = (other - center) * scale
        unit_own_ref[rows, :] = unit_own.astype(b16)
        unit_other_ref[rows, :] = unit_other.astype(b16)
        normed_ref[rows, side_cols(side, part)] = (
            unit_own * gain_own_ref[...].astype(f32)
        ).astype(b16)
        normed_ref[rows, side_cols(1 - side, part)] = (
            unit_other * gain_other_ref[...].astype(f32)
        ).astype(b16)
        scales_ref[:, rows] = jnp.broadcast_to(scale, (block, 128)).T[0:8]


def norm(side, own, gain_own, gain_other, other):
    length, part = own.shape
    half = shape_of((length, part), b16)
    return pl.pallas_call(
        norm_kernel,
        in_specs=[smem()] + [vmem()] * 4,
        out_specs=[vmem()] * 4,
        out_shape=[shape_of((length, 2 * part), b16), half, half, shape_of((8, length), f32)],
        compiler_params=roomy(16),
        cost_estimate=cost(4),
        name="norm",
    )(side, own, gain_own, gain_other, other)


def front_kernel(
    taps_count,
    side_ref,
    seats_ref,
    normed_ref,
    wx_ref,
    wz_ref,
    params_ref,
    gate_ref,
    flipped_ref,
    upx_ref,
    upz_ref,
    conv_out_ref,
    slope_ref,
    q_ref,
    k_ref,
    v_ref,
    gates_ref,
    padded_ref,
):
    side = side_ref[0]
    length = normed_ref.shape[0]
    channels = wx_ref.shape[1]
    tap_count = taps_count
    steps = channels // group
    padded_ref[0:8, :] = jnp.zeros((8, group), f32)
    flip_rows = length // steps
    gates_ref[...] = jnp.zeros_like(gates_ref)

    @pl.loop(0, steps)
    def _(step):
        lanes = pl.ds(pl.multiple_of(step * group, group), group)
        upx = dot_nn(normed_ref[...], wx_ref[:, lanes])
        upx_b = upx.astype(b16)
        upx_ref[:, lanes] = upx_b
        padded_ref[pl.ds(8, length), :] = upx
        upz_ref[:, lanes] = dot_nn(normed_ref[...], wz_ref[:, lanes]).astype(b16)
        params = params_ref[:, lanes]
        taps = params[0:tap_count].astype(f32)
        bias = params[4 * tap_count : 4 * tap_count + 1].astype(f32)
        pre = bias + taps[tap_count - 1 : tap_count] * upx
        for tap in range(tap_count - 1):
            pre = pre + taps[tap : tap + 1] * padded_ref[pl.ds(8 - (tap_count - 1 - tap), length), :]
        gate = sigmoid(pre)
        conv_out = pre * gate
        conv_b = conv_out.astype(b16)
        conv_out_ref[:, lanes] = conv_b
        slope_ref[:, lanes] = (gate + conv_out * (1.0 - gate)).astype(b16)
        conv_low = (conv_out - conv_b.astype(f32)).astype(b16)
        upx_low = (upx - upx_b.astype(f32)).astype(b16)
        qd, kd, vd = (
            spread_taps(params[at * tap_count : (at + 1) * tap_count]) for at in range(1, 4)
        )
        q_b = (dot_nn(conv_b, qd) + dot_nn(conv_low, qd)).astype(b16)
        k_b = (dot_nn(conv_b, kd) + dot_nn(conv_low, kd)).astype(b16)
        v_b = (dot_nn(upx_b, vd) + dot_nn(upx_low, vd)).astype(b16)
        q_ref[:, lanes] = q_b
        k_ref[:, lanes] = k_b
        v_ref[:, lanes] = v_b
        gates_ref[...] += (
            dot_nt(gate_ref[0, :, lanes], q_b)
            + dot_nt(gate_ref[1, :, lanes], k_b)
            + dot_nt(gate_ref[2, :, lanes], v_b)
        )
        rows = pl.ds(pl.multiple_of(step * flip_rows, flip_rows), flip_rows)
        seat_rows(normed_ref[rows, :].T, seats_ref, flipped_ref.at[:, rows])


def front(side, seats, normed, wx, wz, params, gate, taps_count):
    length = normed.shape[0]
    width, channels = wx.shape
    full = shape_of((length, channels), b16)
    return pl.pallas_call(
        partial(front_kernel, taps_count),
        in_specs=[smem(), smem()] + [vmem()] * 5,
        out_specs=[vmem()] * 9,
        out_shape=[shape_of((width, length), b16)]
        + [full] * 7
        + [shape_of((gate.shape[1], length), f32)],
        scratch_shapes=[pltpu.VMEM((length + 8, group), f32)],
        compiler_params=roomy(16),
        cost_estimate=cost(14),
        name="front",
    )(side, seats, normed, wx, wz, params, gate)


def scan_lanes(values, combine, empty, reverse=False):
    length = values.shape[1]
    lane = lax.broadcasted_iota(jnp.int32, values.shape, 1)
    distance = 1
    while distance < length:
        if reverse:
            moved = pltpu.roll(values, length - distance, 1)
            inside = lane < length - distance
        else:
            moved = pltpu.roll(values, distance, 1)
            inside = lane >= distance
        values = combine(values, jnp.where(inside, moved, empty))
        distance *= 2
    return values


def pick(side, first, second):
    return jnp.where(side == 0, first, second)


def fold_rows(values):
    rows, lanes = values.shape
    return jnp.sum(values.reshape(rows // 8, 8, lanes), axis=0)


def cell_kernel(
    head_dim,
    begin,
    end,
    side_ref,
    seats_ref,
    forget_ref,
    gates_own_ref,
    gates_other_ref,
    q_ref,
    k_ref,
    v_ref,
    conv_ref,
    upz_ref,
    flipped_ref,
    cot_own_ref,
    wd_ref,
    params_ref,
    *refs,
):
    length = q_ref.shape[0]
    final = end == length // block
    shares = 2 if begin else 1
    cot_other_refs, refs = refs[:shares], refs[shares:]
    if begin:
        refs = refs[9:]
    rows_ref, cols_ref, keep_ref, send_ref, dnum_ref, skip_grad_ref = refs[:6]
    upz_grad_ref, gated_t_ref, sums_ref, *refs = refs[6:]
    if final:
        first_ref, second_ref, gains_ref, *refs = refs
    states_ref, gateds_ref, nums_ref, dens_ref, slacks_ref = refs
    side = side_ref[0]
    length, channels = q_ref.shape
    heads = channels // head_dim
    gate_count = gates_own_ref.shape[0]
    all_heads = gate_count // 2
    part = cot_own_ref.shape[1]
    cot_rows = cot_other_refs[0].shape[0]
    if begin == 0:
        gates = gates_own_ref[...] + gates_other_ref[...]
        inlet = pick(side, gates[:heads], gates[heads : 2 * heads])
        forget = pick(
            side, gates[all_heads : all_heads + heads], gates[all_heads + heads : gate_count]
        )
        forget = forget + jnp.concatenate(
            [jnp.full((1, length), forget_ref[side * heads + h], f32) for h in range(heads)], axis=0
        )
        log_forget = jnp.minimum(forget, 0.0) - jnp.log1p(jnp.exp(-jnp.abs(forget)))
        total = scan_lanes(log_forget, jnp.add, 0.0)
        ahead = inlet - total
        top = scan_lanes(jnp.maximum(ahead, 0.0), jnp.maximum, 0.0)
        floor = jnp.exp(-(total + top))
        rows_ref[...] = jnp.concatenate(
            [ahead + jnp.log(f32(head_dim**-0.5)), top, forget, jnp.zeros_like(top)], axis=0
        )
        cols_ref[...] = jnp.concatenate([top, floor, top, floor], axis=0).T
        sums_ref[...] = jnp.zeros_like(sums_ref)

    ones = jnp.ones((length, 128), b16)

    def attend(count):
        span = count * block
        here = pl.ds(span - block, block)
        slot = count % 2
        start = span - block
        if start < cot_rows:
            other_rows = cot_other_refs[0][start : start + block, :]
        else:
            other_rows = cot_other_refs[1][start - cot_rows : start - cot_rows + block, :]
        num_ref, den_ref, state_ref, gated_ref, slack_ref = (
            ref.at[slot] for ref in (nums_ref, dens_ref, states_ref, gateds_ref, slacks_ref)
        )
        pieces = []
        for h in range(heads):
            lanes = pl.ds(h * head_dim, head_dim)
            start = span - block
            top = cols_ref[pl.ds(start, block), h : h + 1]
            scores = dot_nt(q_ref[pl.ds(start, block), lanes], k_ref[pl.ds(0, span), lanes])
            done = []
            for piece in range(count):
                there = slice(piece * block, (piece + 1) * block)
                exponent = rows_ref[h : h + 1, there] - top
                if piece == count - 1:
                    row_ids = lax.broadcasted_iota(jnp.int32, (block, block), 0)
                    col_ids = lax.broadcasted_iota(jnp.int32, (block, block), 1)
                    exponent = jnp.where(row_ids >= col_ids, exponent, -jnp.inf)
                done.append((scores[:, there] * jnp.exp(exponent)).astype(b16))
            pieces.append(jnp.concatenate(done, axis=1))
        for h in range(heads):
            lanes = pl.ds(h * head_dim, head_dim)
            num_ref[:, lanes] = dot_nn(pieces[h], v_ref[pl.ds(0, span), lanes])
            den_ref[:, pl.ds(h * 128, 128)] = dot_nn(pieces[h], ones[:span])
        state_ref[...] = dot_nt(cot_own_ref[here, :], wd_ref[:, side_cols(side, part)]) + dot_nt(
            other_rows, wd_ref[:, side_cols(1 - side, part)]
        )

        small = 64
        floors = cols_ref[here, heads : 2 * heads]

        def tiles():
            for h in range(heads):
                for start in range(0, block, small):
                    yield h, start, pl.ds(start, small), pl.ds(h * head_dim, head_dim)

        stats = {}
        for h, start, rows, lanes in tiles():
            denominator = den_ref[rows, h * 128 : h * 128 + 1]
            floor = floors[start : start + small, h : h + 1]
            inverse = 1.0 / jnp.maximum(jnp.abs(denominator), floor)
            hidden = num_ref[rows, lanes] * inverse
            num_ref[rows, lanes] = hidden
            stats[h, start] = [
                inverse,
                jnp.where(jnp.abs(denominator) >= floor, jnp.where(denominator >= 0.0, inverse, -inverse), 0.0),
                jnp.mean(hidden, axis=1, keepdims=True),
            ]
        for h, start, rows, lanes in tiles():
            centered = num_ref[rows, lanes] - stats[h, start][2]
            num_ref[rows, lanes] = centered
            stats[h, start].append(
                lax.rsqrt(jnp.mean(centered * centered, axis=1, keepdims=True) + eps_norm)
            )
        gain_sums = [jnp.zeros((8, head_dim), f32)] * heads
        skip_sums = [jnp.zeros((8, head_dim), f32)] * heads
        for h, start, rows, lanes in tiles():
            gain = params_ref[17:18, lanes].astype(f32)
            skip = params_ref[18:19, lanes].astype(f32)
            unit = num_ref[rows, lanes] * stats[h, start][3]
            num_ref[rows, lanes] = unit
            conv_out = conv_ref[pl.ds(span - block + start, small), lanes].astype(f32)
            inner = unit * gain + skip * conv_out
            upz = upz_ref[pl.ds(span - block + start, small), lanes].astype(f32)
            gate = sigmoid(upz)
            active = upz * gate
            gated_ref[rows, lanes] = (inner * active).astype(b16)
            grad_state = state_ref[rows, lanes]
            grad_inner = grad_state * active
            upz_grad_ref[pl.ds(span - block + start, small), lanes] = (
                grad_state * inner * (gate + active * (1.0 - gate))
            ).astype(b16)
            skip_grad_ref[pl.ds(span - block + start, small), lanes] = (grad_inner * skip).astype(b16)
            along = grad_inner * unit
            gain_sums[h] = gain_sums[h] + fold_rows(along)
            skip_sums[h] = skip_sums[h] + fold_rows(grad_inner * conv_out)
            grad_unit = grad_inner * gain
            state_ref[rows, lanes] = grad_unit
            stats[h, start] += [
                jnp.mean(grad_unit, axis=1, keepdims=True),
                jnp.mean(along * gain, axis=1, keepdims=True),
            ]
        for h, start, rows, lanes in tiles():
            inverse, signed, _, scale, mean, moment = stats[h, start]
            dnum_ref[pl.ds(span - block + start, small), lanes] = (
                (state_ref[rows, lanes] - mean - num_ref[rows, lanes] * moment) * (scale * inverse)
            ).astype(b16)
            slack = -signed * moment * (head_dim * eps_norm) * scale * scale
            slack_ref[rows, pl.ds(h * 128, 128)] = jnp.broadcast_to(slack, (small, 128))
        for h in range(heads):
            lanes = pl.ds(h * head_dim, head_dim)
            sums_ref[0:8, lanes] += gain_sums[h]
            sums_ref[8:16, lanes] += skip_sums[h]
        for h in range(heads):
            rows_ref[3 * heads + h : 3 * heads + h + 1, here] = slack_ref[:, pl.ds(h * 128, 128)].T[0:1]
        gated = gated_ref[...]
        keep_ref[here, :] = dot_nn(gated, wd_ref[:, side_cols(side, part)]).astype(b16)
        send_ref[here, :] = dot_nn(gated, wd_ref[:, side_cols(1 - side, part)]).astype(b16)
        seat_rows(gated.T, seats_ref, gated_t_ref.at[:, here])


    for count in range(begin + 1, end + 1):
        pl.when(side >= 0)(partial(attend, count))
    if not final:
        return
    gains_ref[0:1, :] = jnp.sum(sums_ref[0:8, :], axis=0, keepdims=True)
    gains_ref[1:2, :] = jnp.sum(sums_ref[8:16, :], axis=0, keepdims=True)
    gains_ref[2:8, :] = jnp.zeros((6, channels), f32)
    half = first_ref.shape[0]
    width = 2 * part
    for start in range(0, 2 * half, block):
        out_ref = (first_ref if start < half else second_ref).at[pl.ds(start % half, block), :]
        rows = pl.ds(start, block)
        turned = gated_t_ref[rows, :]
        out_ref[:, side_cols(side, part)] = dot_nn(turned, cot_own_ref[...]).astype(b16)
        out_ref[:, side_cols(1 - side, part)] = sum(
                dot_nn(gated_t_ref[rows, at : at + ref.shape[0]], ref[...])
                for at, ref in zip((0, cot_rows), cot_other_refs)
            ).astype(b16)
        out_ref[:, pl.ds(width, channels)] = dot_nn(
            flipped_ref[rows, :], upz_grad_ref[...]
        ).astype(b16)


def cell(
    side, seats, forget, gates_own, gates_other, q, k, v, conv, upz, flipped, cot_own, wd, params,
    cots_other, carried, head_dim, begin, end,
):
    length, channels = q.shape
    part = cot_own.shape[1]
    width = wd.shape[1]
    heads = channels // head_dim
    half = shape_of((length, part), b16)
    full = shape_of((length, channels), b16)
    shapes = [shape_of((8, length), f32), shape_of((length, 8), f32), half, half, full, full, full]
    shapes += [shape_of((channels, length), b16), shape_of((16, channels), f32)]
    aliases = {14 + len(cots_other) + at: at for at in range(len(carried))}
    if end == length // block:
        shapes += [shape_of((channels // 2, width + channels), b16)] * 2
        shapes += [shape_of((8, channels), f32)]
    return pl.pallas_call(
        partial(cell_kernel, head_dim, begin, end),
        in_specs=[smem()] * 3 + [vmem()] * (11 + len(cots_other) + len(carried)),
        out_specs=[vmem()] * len(shapes),
        out_shape=shapes,
        input_output_aliases=aliases,
        scratch_shapes=[
            pltpu.VMEM((2, block, channels), f32),
            pltpu.VMEM((2, block, channels), b16),
            pltpu.VMEM((2, block, channels), f32),
            pltpu.VMEM((2, block, heads * 128), f32),
            pltpu.VMEM((2, block, heads * 128), f32),
        ],
        compiler_params=roomy(16),
        cost_estimate=cost(10),
        name="cell",
    )(side, seats, forget, gates_own, gates_other, q, k, v, conv, upz, flipped, cot_own, wd, params,
      *cots_other, *carried)


def cell_back_kernel(
    h, heads, q_ref, k_ref, v_ref, dnum_ref, rows_ref, prior_ref, dq_ref, dk_ref, dv_ref, gates_ref,
    grads_ref, pair_ref,
):
    length, head_dim = dq_ref.shape
    lanes = pl.ds(h * head_dim, head_dim)
    gates_ref[...] = prior_ref[...]
    ahead = rows_ref[...].T[:, h : h + 1]
    row_ids = lax.broadcasted_iota(jnp.int32, (block, block), 0)
    col_ids = lax.broadcasted_iota(jnp.int32, (block, block), 1)
    blocks = length // block
    for s in range(blocks):
        there = pl.ds(s * block, block)
        span = length - s * block
        after = pl.ds(s * block, span)
        keys = k_ref[there, lanes]
        scores = dot_nt(keys, q_ref[after, lanes])
        grads = dot_nt(v_ref[there, lanes], dnum_ref[after, lanes])
        scored, graded = [], []
        for t in range(s, blocks):
            here = pl.ds(t * block, block)
            at = slice((t - s) * block, (t - s + 1) * block)
            exponent = ahead[s * block : (s + 1) * block] - rows_ref[heads + h : heads + h + 1, here]
            if s == t:
                exponent = jnp.where(row_ids <= col_ids, exponent, -jnp.inf)
            weight = jnp.exp(exponent)
            slack = rows_ref[3 * heads + h : 3 * heads + h + 1, here]
            scored.append((scores[:, at] * weight).astype(b16))
            graded.append(((grads[:, at] + slack) * weight).astype(b16))
            grads_ref[there, here] = graded[-1]
        dv_ref[there, :] = dot_nn(
            jnp.concatenate(scored, axis=1), dnum_ref[after, lanes]
        ).astype(b16)
        dk = dot_nn(jnp.concatenate(graded, axis=1), q_ref[after, lanes])
        dk_ref[there, :] = dk.astype(b16)
        pair_ref[there, 128:256] = jnp.broadcast_to(
            jnp.sum(dk * keys.astype(f32), axis=1, keepdims=True), (block, 128)
        )
    for t in range(blocks):
        here = pl.ds(t * block, block)
        before = pl.ds(0, (t + 1) * block)
        dq = dot_tn(grads_ref[before, here], k_ref[before, lanes])
        dq_ref[here, :] = dq.astype(b16)
        pair_ref[here, 0:128] = jnp.broadcast_to(
            jnp.sum(dq * q_ref[here, lanes].astype(f32), axis=1, keepdims=True), (block, 128)
        )
    outward = pair_ref[:, 0:128].T[0:1]
    inward = pair_ref[:, 128:256].T[0:1]
    forget = rows_ref[2 * heads + h : 2 * heads + h + 1, :]
    grad_log = scan_lanes(jnp.broadcast_to(outward - inward, (8, length)), jnp.add, 0.0, True)[0:1]
    gates_ref[h : h + 1, :] = inward
    gates_ref[heads + h : heads + h + 1, :] = grad_log * sigmoid(-forget)


def cell_back(q, k, v, dnum, rows, prior, h, head_dim):
    length, channels = q.shape
    heads = channels // head_dim
    full = shape_of((length, head_dim), b16)
    return pl.pallas_call(
        partial(cell_back_kernel, h, heads),
        in_specs=[vmem()] * 6,
        out_specs=[vmem()] * 4,
        out_shape=[full, full, full, shape_of((8, length), f32)],
        scratch_shapes=[pltpu.VMEM((length, length), b16), pltpu.VMEM((length, 256), f32)],
        compiler_params=roomy(16),
        cost_estimate=cost(7),
        name="cell_back",
    )(q, k, v, dnum, rows, prior)


def front_back_kernel(
    tap_count,
    heads,
    index,
    reseat,
    side_ref,
    table_ref,
    gates_own_ref,
    gates_other_ref,
    dq_ref,
    dk_ref,
    dv_ref,
    q_ref,
    k_ref,
    v_ref,
    conv_out_ref,
    slope_ref,
    upx_ref,
    skip_grad_ref,
    flipped_ref,
    params_ref,
    gate_ref,
    *refs,
):
    last = index == heads - 1
    if last:
        gains_ref, *refs = refs
        prior_refs, refs = refs[:index], refs[index:]
    upx_grad_ref, first_ref, second_ref, small_ref, padded_refs, turned_ref = refs
    side = side_ref[0]
    length, span = upx_grad_ref.shape
    own = gates_own_ref[...]
    other = gates_other_ref[...]
    gates = jnp.concatenate(
        [
            pick(side, own[:heads], other[:heads]),
            pick(side, other[:heads], own[:heads]),
            pick(side, own[heads : 2 * heads], other[heads : 2 * heads]),
            pick(side, other[heads : 2 * heads], own[heads : 2 * heads]),
        ],
        axis=0,
    )
    gates_t = gates.T.astype(b16)
    gates_b = gates.astype(b16)
    padded_refs[:, length : length + 8, :] = jnp.zeros((2, 8, group), f32)
    half = first_ref.shape[0]
    height = half // len(reseat)
    @pl.loop(0, span // group)
    def _(step):
        padded_ref = padded_refs.at[0]
        near = pl.ds(pl.multiple_of(step * group, group), group)
        lanes = pl.ds(pl.multiple_of(index * span + step * group, group), group)
        dq_b = (dq_ref[:, near].astype(f32) + dot_nn(gates_t, gate_ref[0, :, lanes])).astype(b16)
        dk_b = (dk_ref[:, near].astype(f32) + dot_nn(gates_t, gate_ref[1, :, lanes])).astype(b16)
        dv_b = (dv_ref[:, near].astype(f32) + dot_nn(gates_t, gate_ref[2, :, lanes])).astype(b16)
        conv_out = conv_out_ref[:, lanes]
        params = params_ref[:, lanes]
        upx_b = upx_ref[:, lanes]
        grad_conv = (
            skip_grad_ref[:, lanes].astype(f32)
            + dot_nt(dq_b, spread_taps(params[tap_count : 2 * tap_count]))
            + dot_nt(dk_b, spread_taps(params[2 * tap_count : 3 * tap_count]))
        )
        grad_pre = grad_conv * slope_ref[:, lanes].astype(f32)
        padded_ref[0:length, :] = grad_pre
        taps = params[0:tap_count].astype(f32)
        upx = upx_b.astype(f32)
        grad_upx = (
            dot_nt(dv_b, spread_taps(params[3 * tap_count : 4 * tap_count]))
            + taps[tap_count - 1 : tap_count] * grad_pre
        )
        tap_grads = [jnp.sum(upx * grad_pre, axis=0, keepdims=True)]
        for tap in range(tap_count - 2, -1, -1):
            moved = padded_ref[tap_count - 1 - tap : tap_count - 1 - tap + length, :]
            grad_upx = grad_upx + taps[tap : tap + 1] * moved
            tap_grads.insert(0, jnp.sum(upx * moved, axis=0, keepdims=True))
        grad_b = grad_upx.astype(b16)
        upx_grad_ref[:, near] = grad_b
        for start, out_ref in ((0, first_ref), (half, second_ref)):
            result = dot_nn(flipped_ref[start : start + half, :], grad_b).astype(b16)
            for seat, source in enumerate(reseat):
                out_ref[seat * height : (seat + 1) * height, near] = result[
                    source * height : (source + 1) * height
                ]
        small_ref[:, near] = jnp.concatenate(
            tap_grads
            + [
                gather_taps(dot_tn(conv_out, dq_b), tap_count),
                gather_taps(dot_tn(conv_out, dk_b), tap_count),
                gather_taps(dot_tn(upx_b, dv_b), tap_count),
                dot_nn(gates_b, q_ref[:, lanes]),
                dot_nn(gates_b, k_ref[:, lanes]),
                dot_nn(gates_b, v_ref[:, lanes]),
                jnp.broadcast_to(jnp.sum(gates, axis=1, keepdims=True), (gates.shape[0], group)),
                jnp.sum(grad_pre, axis=0, keepdims=True),
                jnp.zeros((7, group), f32),
            ],
            axis=0,
        )
    if last:
        small = jnp.concatenate([ref[...] for ref in (*prior_refs, small_ref)], axis=1)
        split = 4 * tap_count + 3 * gates.shape[0]
        stacked = jnp.concatenate(
            [
                small[:split],
                small[split + gates.shape[0] : split + gates.shape[0] + 1],
                gains_ref[0:2, :],
                jnp.zeros((128 - split - 3, small.shape[1]), f32),
            ],
            axis=0,
        )
        turned_ref[...] = stacked.T
        for seat in range(2 * len(reseat)):
            out_ref = first_ref if seat < len(reseat) else second_ref
            start = seat % len(reseat) * height
            out_ref[start : start + height, span : span + 128] = turned_ref[
                pl.ds(pl.multiple_of(table_ref[seat] * height, height), height), :
            ].astype(b16)


def front_back(
    side, table, gates_own, gates_other, dq, dk, dv, q, k, v, conv_out, slope, upx, skip_grad, flipped,
    params, gate, gains, priors, tap_count, heads, index, reseat,
):
    length, channels = q.shape
    width = flipped.shape[0]
    last = index == heads - 1
    span = channels // heads
    out_width = span + (128 if last else 0)
    extra = [gains, *priors] if last else []
    return pl.pallas_call(
        partial(front_back_kernel, tap_count, heads, index, reseat),
        in_specs=[smem(), smem()] + [vmem()] * (15 + len(extra)),
        out_specs=[vmem()] * 4,
        out_shape=[
            shape_of((length, span), b16),
            shape_of((width // 2, out_width), b16),
            shape_of((width // 2, out_width), b16),
            shape_of((56, span), f32),
        ],
        scratch_shapes=[
            pltpu.VMEM((2, length + 8, group), f32),
            pltpu.VMEM((channels, 128), f32),
        ],
        compiler_params=roomy(16),
        cost_estimate=cost(8),
        name="front_back",
    )(side, table, gates_own, gates_other, dq, dk, dv, q, k, v, conv_out, slope, upx, skip_grad,
      flipped, params, gate, *extra)


def norm_back_kernel(
    parts, side_ref, upz_grad_ref, wx_ref, wz_ref, unit_own_ref, unit_other_ref, gain_own_ref,
    gain_other_ref, *refs,
):
    upx_grad_refs = refs[:parts]
    keep_ref, send_ref, stats_ref = refs[parts:]
    side = side_ref[0]
    length, part = unit_own_ref.shape
    gain_sums = [jnp.zeros((8, part), f32)] * 2
    for start in range(0, length, block):
        here = pl.ds(start, block)
        sums = []
        for index, (unit_ref, place, gain_ref, out_ref) in enumerate(
            [
                (unit_own_ref, side, gain_own_ref, keep_ref),
                (unit_other_ref, 1 - side, gain_other_ref, send_ref),
            ]
        ):
            rows = side_cols(place, part)
            terms = dot_nt(upz_grad_ref[here, :], wz_ref[rows, :])
            for index_part, grad_ref in enumerate(upx_grad_refs):
                span = grad_ref.shape[1]
                lanes = pl.ds(index_part * span, span)
                terms = terms + dot_nt(grad_ref[here, :], wx_ref[rows, lanes])
            out_ref[here, :] = terms.astype(b16)
            along = terms * unit_ref[here, :].astype(f32)
            gain_sums[index] = gain_sums[index] + fold_rows(along)
            gain = gain_ref[...].astype(f32)
            sums.append(
                (
                    jnp.sum(terms * gain, axis=1, keepdims=True),
                    jnp.sum(along * gain, axis=1, keepdims=True),
                )
            )
        for row in range(2):
            stats_ref[row : row + 1, here] = jnp.broadcast_to(
                sums[0][row] + sums[1][row], (block, 128)
            ).T[0:1]
    stats_ref[2:8, :] = jnp.zeros((6, length), f32)
    for row, total in ((2, gain_sums[1]), (3, gain_sums[0])):
        stats_ref[row : row + 1, 0:part] = jnp.sum(total, axis=0, keepdims=True)


def norm_back(side, upx_grads, upz_grad, wx, wz, own, other, gain_own, gain_other):
    length, channels = upz_grad.shape
    parts = len(upx_grads)
    part = own.shape[1]
    return pl.pallas_call(
        partial(norm_back_kernel, parts),
        in_specs=[smem()] + [vmem()] * (7 + parts),
        out_specs=[vmem()] * 3,
        out_shape=[
            shape_of((length, part), b16),
            shape_of((length, part), b16),
            shape_of((8, max(length, part)), f32),
        ],
        compiler_params=roomy(16),
        cost_estimate=cost(9),
        name="norm_back",
    )(side, upz_grad, wx, wz, own, other, gain_own, gain_other, *upx_grads)


def seat_back(table_ref, near_ref, far_ref, out_ref):
    pieces = table_ref.shape[0]
    height = out_ref.shape[0] // pieces
    for seat in range(pieces):
        source = near_ref if seat < pieces // 2 else far_ref
        start = seat % (pieces // 2) * height
        out_ref[pl.ds(pl.multiple_of(table_ref[seat] * height, height), height), :] = source[
            start : start + height, :
        ].astype(f32)


def place_rows(table, pair):
    near, far = pair
    half, width = near.shape
    source = spec((half, group), lambda c: (0, c))
    return pl.pallas_call(
        seat_back,
        grid=(width // group,),
        in_specs=[smem(), source, source],
        out_specs=spec((2 * half, group), lambda c: (0, c)),
        out_shape=shape_of((2 * half, width), f32),
        compiler_params=settings(16),
        cost_estimate=cost(3),
        name="place_rows",
    )(table, near, far)


def place_last_kernel(
    taps, gate_count, mixed_ref, far_table_ref, near_ref, far_ref, near_two_ref, far_two_ref,
    near_small_ref, far_small_ref, out_ref, conv_ref, q_ref, k_ref, v_ref, bias_ref, gain_ref,
    skip_ref, gate_ref, turned_ref,
):
    step = pl.program_id(0)
    middle = pl.num_programs(0) // 2

    @pl.when(step == 0)
    def _():
        seat_back(far_table_ref, near_small_ref, far_small_ref, turned_ref)
        flat = turned_ref[...].T
        for at, ref in enumerate((conv_ref, q_ref, k_ref, v_ref)):
            ref[...] = flat[at * taps : (at + 1) * taps]
        start = 4 * taps
        for part in range(3):
            gate_ref[part, :, :] = flat[start + part * gate_count : start + (part + 1) * gate_count]
        start += 3 * gate_count
        for at, ref in enumerate((bias_ref, gain_ref, skip_ref)):
            ref[...] = flat[start + at : start + at + 1]

    @pl.when(step < middle)
    def _():
        seat_back(mixed_ref, near_ref, far_ref, out_ref)

    @pl.when(step >= middle)
    def _():
        seat_back(far_table_ref, near_two_ref, far_two_ref, out_ref)


def place_last(mixed_table, far_table, pair, pair_two, taps, gate_count):
    half, width = pair[0].shape
    steps = width // group
    channels = 2 * half

    def source(first):
        return spec((half, group), lambda c: (0, jnp.clip(c - first, 0, steps - 1)))

    small = spec((half, 128), lambda c: (0, width // 128))
    row = shape_of((1, channels), f32)
    tap_rows = shape_of((taps, channels), f32)
    shapes = [tap_rows] * 4 + [row] * 3 + [shape_of((3, gate_count, channels), f32)]
    return pl.pallas_call(
        partial(place_last_kernel, taps, gate_count),
        grid=(2 * steps,),
        in_specs=[smem(), smem(), source(0), source(0), source(steps), source(steps), small, small],
        out_specs=[spec((2 * half, group), lambda c: (0, c))] + [whole(v.shape) for v in shapes],
        out_shape=[shape_of((2 * half, 2 * width), f32)] + shapes,
        scratch_shapes=[pltpu.VMEM((channels, 128), f32)],
        compiler_params=settings(16),
        cost_estimate=cost(5),
        name="place_last",
    )(mixed_table, far_table, *pair, *pair_two, *pair_two)


def finish_kernel(
    unit_ref, scales_ref, gain_ref, keep_ref, recv_ref, stats_own_ref, stats_other_ref,
    cot_ref, out_ref,
):
    length, part = unit_ref.shape
    width = 2 * part
    gain = gain_ref[...].astype(f32)
    for start in range(0, length, block):
        here = pl.ds(start, block)
        unit = unit_ref[here, :].astype(f32)
        scale = scales_ref[:, here].T[:, 0:1]
        stats = (stats_own_ref[:, here] + stats_other_ref[:, here]).T
        terms = keep_ref[here, :].astype(f32) + recv_ref[here, :].astype(f32)
        pulled = terms * gain - (stats[:, 0:1] + unit * stats[:, 1:2]) / width
        out_ref[here, :] = cot_ref[here, :].astype(f32) + pulled * scale


def finish(unit, scales, gain, keep, recv, stats_own, stats_other, cot):
    return pl.pallas_call(
        finish_kernel,
        in_specs=[vmem()] * 8,
        out_specs=vmem(),
        out_shape=shape_of(unit.shape, f32),
        compiler_params=roomy(16),
        cost_estimate=cost(4),
        name="finish",
    )(unit, scales, gain, keep, recv, stats_own, stats_other, cot)


def swap(values):
    return lax.ppermute(values, "head", [(0, 1), (1, 0)])


def across(values, bit, count):
    return lax.ppermute(values, "dp", [(i, i ^ (1 << bit)) for i in range(count)])


def add_halves(first, second):
    return (first.astype(f32) + second.astype(f32)).astype(first.dtype)


class Reduction:
    def __init__(self, keep, out, order, bits, count, step=0):
        self.keep, self.out, self.count = keep, out, count
        self.plan = (
            [("half", bit) for bit in order]
            + [("full", bit) for bit in range(len(order), bits)]
            + [("copy", bit) for bit in reversed(order)]
        )
        self.step = step

    def send(self):
        if not self.more():
            return None
        self.got = across(self.keep if self.out is None else self.out, self.plan[self.step][1], self.count)
        return self.got

    def take(self, got=None):
        if not self.more():
            return
        got = self.got if got is None else got
        kind, bit = self.plan[self.step]
        self.step += 1
        after = self.plan[self.step][0] if self.step < len(self.plan) else "end"
        if kind == "copy":
            if after == "end":
                self.result = (self.keep, got)
            else:
                self.keep = jnp.concatenate([self.keep, got], axis=0)
                self.out = None
        elif after == "half":
            half = self.keep.shape[0] // 2
            self.out = add_halves(self.keep[half:], got[half:])
            self.keep = add_halves(self.keep[:half], got[:half])
        else:
            self.keep = add_halves(self.keep, got)
            self.out = None

    def more(self):
        return self.step < len(self.plan)


def arrange(order, place):
    levels = len(order)
    return sum((((place >> bit) & 1) << (levels - 1 - at)) for at, bit in enumerate(order))


def settle(value, *flows):
    flows = [flow for flow in flows if flow.more()]
    value, gots = lax.optimization_barrier((value, [flow.got for flow in flows]))
    for flow, got in zip(flows, gots):
        flow.take(got)
    flows = [flow for flow in flows if flow.more()]
    held = [(flow.keep, flow.out) for flow in flows]
    value, held = lax.optimization_barrier((value, held))
    for flow, (keep, out) in zip(flows, held):
        flow.keep, flow.out = keep, out
    return value


def send_all(flows):
    for flow in flows:
        flow.send()


def on_device(
    layer_input,
    ln_gain,
    up_x_weight,
    up_z_weight,
    conv_weight,
    conv_bias,
    query_weight,
    key_weight,
    value_weight,
    gate_weight,
    forget_bias,
    norm_gain,
    skip_gain,
    down_weight,
    cotangent,
):
    head_index = lax.axis_index("head")
    place = lax.axis_index("dp")
    count = lax.axis_size("dp")
    side = head_index.astype(jnp.int32).reshape(1)
    length, part = layer_input.shape
    channels = up_x_weight.shape[1]
    all_heads = gate_weight.shape[2] // 2
    heads = all_heads // lax.axis_size("head")
    head_dim = channels // heads
    taps = conv_weight.shape[0]
    bits = count.bit_length() - 1
    levels = min(bits, 4)
    near_order = list(range(levels))
    far_order = near_order[:1] + near_order[2:3] + near_order[1:2] + near_order[3:]
    pieces = 2**levels
    turned = [0] * pieces
    for relative in range(pieces):
        turned[arrange(near_order, relative)] = arrange(far_order, relative)
    seats = jnp.arange(pieces, dtype=jnp.int32)
    near_table = (seats ^ arrange(near_order, place)).astype(jnp.int32)
    far_table = (seats ^ arrange(far_order, place)).astype(jnp.int32)
    mixed_table = (jnp.array(turned, jnp.int32) ^ arrange(far_order, place)).astype(jnp.int32)
    middle = max(pieces // 2, 1)
    straight = list(range(middle))
    mixed = [turned[seat] for seat in range(middle)]

    gain_own = ln_gain.reshape(1, part)
    gain_other = swap(gain_own)
    input_other = swap(layer_input)
    gate_t = gate_weight.transpose(0, 2, 1)
    input_v, wx_v, wz_v, wd_v, cot_v, params = stage(
        [layer_input, up_x_weight, up_z_weight, down_weight, cotangent],
        [conv_weight, query_weight, key_weight, value_weight]
        + [values.reshape(1, channels) for values in (conv_bias, norm_gain, skip_gain)],
    )
    blocks = length // block
    early_rows = (blocks - 1) * block if blocks > 1 else length
    cot_start, input_other, gain_other = lax.optimization_barrier(
        (cotangent[:early_rows], input_other, gain_other)
    )
    cots_other = [swap(cot_start)]
    normed, unit_own, unit_other, scales = norm(side, input_v, gain_own, gain_other, input_other)
    flipped, upx, upz, conv_out, slope, q, k, v, gates = front(
        side, far_table, normed, wx_v, wz_v, params, gate_t, taps
    )
    gates_other = swap(gates)
    cot_start, gates_own = lax.optimization_barrier((cotangent[early_rows:], gates))
    cot_late = swap(cot_start)
    carried = []
    for begin, end in ((0, blocks - 1), (blocks - 1, blocks)) if blocks > 1 else ((0, 1),):
        if begin:
            cots_other.append(cot_late)
        carried = cell(
            side, near_table, forget_bias.astype(f32), gates, gates_other, q, k, v, conv_out, upz,
            flipped, cot_v, wd_v, params, cots_other, carried, head_dim, begin, end,
        )
    rows, _, keep, send, dnum, skip_grad, upz_grad, _, _, early_keep, early_send, gains = carried
    width = down_weight.shape[1]
    done = dict(
        rows=rows, keep=keep, send=send, gains=gains, skip_grad=skip_grad, upz_grad=upz_grad
    )
    flows = {
        "a": Reduction(early_keep[:, :width], early_send[:, :width], near_order, bits, count),
        "b": Reduction(early_keep[:, width:], early_send[:, width:], far_order, bits, count),
    }
    grads, upx_grads, smalls = [], [], []

    def back_cell(index):
        prior = done["gate_grads"] if index else rows
        grads.append(cell_back(q, k, v, dnum, rows, prior, index, head_dim))
        done["gate_grads"] = grads[-1][3]
        return ["gate_grads"]

    def back_front(index, order, reseat):
        dq, dk, dv, _ = grads[index]
        upx_grad, late_keep, late_send, small = front_back(
            side, far_table, done["gate_grads"], done["gate_grads_other"], dq, dk, dv, q, k, v,
            conv_out, slope, upx, skip_grad, flipped, params, gate_t, gains, list(smalls), taps,
            heads, index, reseat,
        )
        smalls.append(small)
        flows["cd"[index]] = Reduction(late_keep, late_send, order, bits, count)
        done["upx_grad", index] = upx_grad
        return [("upx_grad", index)]

    def swap_gates():
        done["gate_grads_other"] = swap(done["gate_grads"])
        return ["gate_grads_other"]

    def add_output():
        done["layer_output"] = (
            layer_input.astype(f32) + keep.astype(f32) + done["down_other"].astype(f32)
        ).astype(b16)
        return ["layer_output"]

    def back_norm():
        done["terms"], done["terms_send"], done["stats"] = norm_back(
            side, [done["upx_grad", index] for index in range(heads)], upz_grad, up_x_weight,
            up_z_weight, unit_own, unit_other, gain_own, gain_other,
        )
        return ["terms", "terms_send", "stats"]

    def swap_stats():
        done["stats_other"] = swap(done["stats"])
        done["terms_other"] = swap(done["terms_send"])
        return ["stats_other"]

    def start_tiny():
        line = done["stats"][3, :part] + done["stats_other"][2, :part]
        tiny = jnp.concatenate([line, smalls[0][-12:-8, 0], jnp.zeros((124,), f32)])
        flows["t"] = Reduction(tiny.reshape(-1, 128), None, [], bits, count)
        return []

    def end_norm():
        done["input_grad"] = finish(
            unit_own, scales, gain_own, done["terms"], done["terms_other"], done["stats"],
            done["stats_other"], cotangent,
        )
        return ["input_grad"]

    def place_down():
        if hasattr(flows["a"], "result"):
            done["grad_down"] = place_rows(near_table, flows["a"].result)
            return ["grad_down"]
        return []

    def place_upz():
        if hasattr(flows["b"], "result"):
            done["grad_upz"] = place_rows(far_table, flows["b"].result)
            return ["grad_upz"]
        return []

    works = dict(
        cell0=partial(back_cell, 0),
        cell1=partial(back_cell, 1),
        gates=swap_gates,
        front0=partial(back_front, 0, near_order, mixed),
        front1=partial(back_front, 1, far_order, straight),
        output=add_output,
        norm=back_norm,
        stats=swap_stats,
        tiny=start_tiny,
        terms=lambda: ["terms_other"],
        finish=end_norm,
        down=place_down,
        upz=place_upz,
        none=lambda: [],
    )
    plan = [
        ("ab", "cell0", "ab"),
        ("ab", "cell1", "ab"),
        ("", "gates", ""),
        ("ab", "front0+output", "ab"),
        ("abc", "front1", "c"),
        ("d", "none", "d"),
        ("cd", "norm", "abcd"),
        ("cdab", "stats+tiny", "cdab"),
        ("cdabt", "none", "cdabt"),
        ("cdabt", "terms", "cdabt"),
        ("cdabt", "finish", "cdabt"),
        ("cdt", "down+upz", "cdt"),
    ]
    done["down_other"] = swap(send)
    sending = set()

    def run(sends, work, waits):
        for name in sends:
            if name in flows and flows[name].more() and name not in sending:
                flows[name].send()
                sending.add(name)
        names = []
        for one in work.split("+"):
            names += works[one]()
        ready = [name for name in waits if name in sending]
        held = settle([done[name] for name in names], *[flows[name] for name in ready])
        done.update(zip(names, held))
        sending.difference_update(ready)

    for step in plan:
        run(*step)
    while any(flow.more() for flow in flows.values()):
        run("cdabt", "none", "cdabt")
    for name, place_one in (("grad_down", place_down), ("grad_upz", place_upz)):
        if name not in done:
            place_one()
    grad_upx, conv_grad, q_grad, k_grad, v_grad, bias_grad, gain_grad, skip_sum, gate_grad = (
        place_last(
            mixed_table, far_table, flows["c"].result, flows["d"].result, taps, 2 * all_heads
        )
    )
    tiny = flows["t"].keep.reshape(-1)
    return (
        done["layer_output"],
        done["input_grad"],
        tiny[:part],
        grad_upx,
        done["grad_upz"],
        conv_grad,
        bias_grad.reshape(-1),
        q_grad,
        k_grad,
        v_grad,
        gate_grad.transpose(0, 2, 1),
        tiny[part : part + all_heads],
        gain_grad.reshape(-1),
        skip_sum.reshape(-1),
        done["grad_down"],
    )


def solution(mesh):
    in_specs = (
        P("dp", "head"),
        P("head"),
        P(None, "head"),
        P(None, "head"),
        P(None, "head"),
        P("head"),
        P(None, "head"),
        P(None, "head"),
        P(None, "head"),
        P(None, "head", None),
        P(),
        P("head"),
        P("head"),
        P("head", None),
        P("dp", "head"),
    )
    out_specs = (
        P("dp", "head"),
        P("dp", "head"),
        P("head"),
        P(None, "head"),
        P(None, "head"),
        P(None, "head"),
        P("head"),
        P(None, "head"),
        P(None, "head"),
        P(None, "head"),
        P(None, "head", None),
        P(),
        P("head"),
        P("head"),
        P("head", None),
    )
    return jax.shard_map(
        on_device, mesh=mesh, in_specs=in_specs, out_specs=out_specs, check_vma=False
    )
```

```python
from functools import partial

import jax
import jax.numpy as jnp
from jax import lax
from jax.experimental import pallas as pl
from jax.experimental.pallas import tpu as pltpu
from jax.sharding import PartitionSpec as P

eps_norm = 1e-05
group = 256
block = 256
b16 = jnp.bfloat16
f32 = jnp.float32


def dot_nn(first, second):
    return lax.dot_general(first, second, (((1,), (0,)), ((), ())), preferred_element_type=f32)


def dot_nt(first, second):
    return lax.dot_general(first, second, (((1,), (1,)), ((), ())), preferred_element_type=f32)


def dot_tn(first, second):
    return lax.dot_general(first, second, (((0,), (0,)), ((), ())), preferred_element_type=f32)


def sigmoid(values):
    return 0.5 * jnp.tanh(0.5 * values) + 0.5


def spec(shape, index_map):
    return pl.BlockSpec(shape, index_map)


def whole(shape):
    return pl.BlockSpec(shape, lambda *_: (0,) * len(shape))


def smem():
    return pl.BlockSpec(memory_space=pltpu.SMEM)


def shape_of(shape, dtype):
    return jax.ShapeDtypeStruct(shape, dtype)


def vmem():
    return pl.BlockSpec(memory_space=pltpu.VMEM)


def hbm():
    return pl.BlockSpec(memory_space=pltpu.HBM)


def roomy(mebibytes):
    return pltpu.CompilerParams(vmem_limit_bytes=mebibytes * 2**20)


def settings(mebibytes):
    return pltpu.CompilerParams(
        dimension_semantics=("arbitrary",), vmem_limit_bytes=mebibytes * 2**20
    )


def cost(micros):
    return pl.CostEstimate(
        flops=int(micros * 1.1e9), bytes_accessed=int(micros * 3.6e6), transcendentals=0
    )


def side_cols(side, width):
    return pl.ds(pl.multiple_of(side * width, width), width)


def spread_taps(taps):
    tap_count, width = taps.shape
    rows = lax.broadcasted_iota(jnp.int32, (width, width), 0) // tap_count
    cols = lax.broadcasted_iota(jnp.int32, (width, width), 1) // tap_count
    pair = jnp.concatenate([taps.astype(f32)] * (8 // tap_count), axis=0)
    full = jnp.concatenate([pair] * (width // 8), axis=0)
    return jnp.where(rows == cols, full, 0.0).astype(b16)


def gather_taps(dense, tap_count):
    width = dense.shape[0]
    rows = lax.broadcasted_iota(jnp.int32, (width, width), 0) // tap_count
    cols = lax.broadcasted_iota(jnp.int32, (width, width), 1) // tap_count
    kept = jnp.where(rows == cols, dense, 0.0)
    folded = jnp.sum(kept.reshape(width // 8, 8, width), axis=0)
    total = folded[:tap_count]
    for part in range(1, 8 // tap_count):
        total = total + folded[part * tap_count : (part + 1) * tap_count]
    return total


def row_stats(own, other):
    width = own.shape[1] + other.shape[1]
    total = jnp.sum(own, axis=1, keepdims=True) + jnp.sum(other, axis=1, keepdims=True)
    square = jnp.sum(own * own, axis=1, keepdims=True) + jnp.sum(
        other * other, axis=1, keepdims=True
    )
    center = total / width
    return center, lax.rsqrt(square / width - center * center + eps_norm)


def seat_rows(values, seats_ref, out_ref):
    seats = seats_ref.shape[0]
    height = values.shape[0] // seats
    for piece in range(seats):
        out_ref[pl.ds(pl.multiple_of(seats_ref[piece] * height, height), height), :] = values[
            piece * height : (piece + 1) * height
        ]


class Fetch:
    def __init__(self, sems):
        self.sems, self.copies = sems, []

    def __call__(self, source, target):
        copy = pltpu.make_async_copy(source, target, self.sems.at[len(self.copies)])
        copy.start()
        self.copies.append(copy)
        return copy


def buffers(*operands):
    return [pltpu.VMEM(value.shape, value.dtype) for value in operands]


def in_hbm(values):
    return pltpu.with_memory_space_constraint(values, pltpu.HBM)


def stage_kernel(count, taps_count, *refs):
    sources, smalls, targets = refs[:count], refs[count : count + 7], refs[count + 7 : 2 * count + 7]
    params_ref, sems = refs[2 * count + 7 :]
    fetch = Fetch(sems)
    for source, target in zip(sources, targets):
        fetch(source, target)
    rows = [ref[...].astype(f32) for ref in smalls]
    filled = sum(row.shape[0] for row in rows)
    rows.append(jnp.zeros((params_ref.shape[0] - filled, params_ref.shape[1]), f32))
    params_ref[...] = jnp.concatenate(rows, axis=0).astype(b16)
    for copy in fetch.copies:
        copy.wait()


def stage(arrays, smalls):
    count = len(arrays)
    params = shape_of((32, smalls[0].shape[1]), b16)
    return pl.pallas_call(
        partial(stage_kernel, count, smalls[0].shape[0]),
        in_specs=[hbm()] * count + [vmem()] * len(smalls),
        out_specs=[vmem()] * (count + 1),
        out_shape=[shape_of(value.shape, value.dtype) for value in arrays] + [params],
        scratch_shapes=[pltpu.SemaphoreType.DMA((count,))],
        compiler_params=roomy(16),
        cost_estimate=cost(4),
        name="stage",
    )(*[in_hbm(value) for value in arrays], *smalls)


def norm_kernel(
    side_ref, own_ref, gain_own_ref, gain_other_ref, other_ref, normed_ref, unit_own_ref,
    unit_other_ref, scales_ref,
):
    side = side_ref[0]
    length, part = own_ref.shape
    for start in range(0, length, block):
        rows = pl.ds(start, block)
        own = own_ref[rows, :].astype(f32)
        other = other_ref[rows, :].astype(f32)
        center, scale = row_stats(own, other)
        unit_own = (own - center) * scale
        unit_other = (other - center) * scale
        unit_own_ref[rows, :] = unit_own.astype(b16)
        unit_other_ref[rows, :] = unit_other.astype(b16)
        normed_ref[rows, side_cols(side, part)] = (
            unit_own * gain_own_ref[...].astype(f32)
        ).astype(b16)
        normed_ref[rows, side_cols(1 - side, part)] = (
            unit_other * gain_other_ref[...].astype(f32)
        ).astype(b16)
        scales_ref[:, rows] = jnp.broadcast_to(scale, (block, 128)).T[0:8]


def norm(side, own, gain_own, gain_other, other):
    length, part = own.shape
    half = shape_of((length, part), b16)
    return pl.pallas_call(
        norm_kernel,
        in_specs=[smem()] + [vmem()] * 4,
        out_specs=[vmem()] * 4,
        out_shape=[shape_of((length, 2 * part), b16), half, half, shape_of((8, length), f32)],
        compiler_params=roomy(16),
        cost_estimate=cost(4),
        name="norm",
    )(side, own, gain_own, gain_other, other)


def front_kernel(
    taps_count,
    side_ref,
    seats_ref,
    normed_ref,
    wx_ref,
    wz_ref,
    params_ref,
    gate_ref,
    flipped_ref,
    upx_ref,
    upz_ref,
    conv_out_ref,
    slope_ref,
    q_ref,
    k_ref,
    v_ref,
    gates_ref,
    padded_ref,
):
    side = side_ref[0]
    length = normed_ref.shape[0]
    channels = wx_ref.shape[1]
    tap_count = taps_count
    steps = channels // group
    padded_ref[0:8, :] = jnp.zeros((8, group), f32)
    flip_rows = length // steps
    gates_ref[...] = jnp.zeros_like(gates_ref)

    @pl.loop(0, steps)
    def _(step):
        lanes = pl.ds(pl.multiple_of(step * group, group), group)
        upx = dot_nn(normed_ref[...], wx_ref[:, lanes])
        upx_b = upx.astype(b16)
        upx_ref[:, lanes] = upx_b
        padded_ref[pl.ds(8, length), :] = upx
        upz_ref[:, lanes] = dot_nn(normed_ref[...], wz_ref[:, lanes]).astype(b16)
        params = params_ref[:, lanes]
        taps = params[0:tap_count].astype(f32)
        bias = params[4 * tap_count : 4 * tap_count + 1].astype(f32)
        pre = bias + taps[tap_count - 1 : tap_count] * upx
        for tap in range(tap_count - 1):
            pre = pre + taps[tap : tap + 1] * padded_ref[pl.ds(8 - (tap_count - 1 - tap), length), :]
        gate = sigmoid(pre)
        conv_out = pre * gate
        conv_b = conv_out.astype(b16)
        conv_out_ref[:, lanes] = conv_b
        slope_ref[:, lanes] = (gate + conv_out * (1.0 - gate)).astype(b16)
        conv_low = (conv_out - conv_b.astype(f32)).astype(b16)
        upx_low = (upx - upx_b.astype(f32)).astype(b16)
        qd, kd, vd = (
            spread_taps(params[at * tap_count : (at + 1) * tap_count]) for at in range(1, 4)
        )
        q_b = (dot_nn(conv_b, qd) + dot_nn(conv_low, qd)).astype(b16)
        k_b = (dot_nn(conv_b, kd) + dot_nn(conv_low, kd)).astype(b16)
        v_b = (dot_nn(upx_b, vd) + dot_nn(upx_low, vd)).astype(b16)
        q_ref[:, lanes] = q_b
        k_ref[:, lanes] = k_b
        v_ref[:, lanes] = v_b
        gates_ref[...] += (
            dot_nt(gate_ref[0, :, lanes], q_b)
            + dot_nt(gate_ref[1, :, lanes], k_b)
            + dot_nt(gate_ref[2, :, lanes], v_b)
        )
        rows = pl.ds(pl.multiple_of(step * flip_rows, flip_rows), flip_rows)
        seat_rows(normed_ref[rows, :].T, seats_ref, flipped_ref.at[:, rows])


def front(side, seats, normed, wx, wz, params, gate, taps_count):
    length = normed.shape[0]
    width, channels = wx.shape
    full = shape_of((length, channels), b16)
    return pl.pallas_call(
        partial(front_kernel, taps_count),
        in_specs=[smem(), smem()] + [vmem()] * 5,
        out_specs=[vmem()] * 9,
        out_shape=[shape_of((width, length), b16)]
        + [full] * 7
        + [shape_of((gate.shape[1], length), f32)],
        scratch_shapes=[pltpu.VMEM((length + 8, group), f32)],
        compiler_params=roomy(16),
        cost_estimate=cost(14),
        name="front",
    )(side, seats, normed, wx, wz, params, gate)


def scan_lanes(values, combine, empty, reverse=False):
    length = values.shape[1]
    lane = lax.broadcasted_iota(jnp.int32, values.shape, 1)
    distance = 1
    while distance < length:
        if reverse:
            moved = pltpu.roll(values, length - distance, 1)
            inside = lane < length - distance
        else:
            moved = pltpu.roll(values, distance, 1)
            inside = lane >= distance
        values = combine(values, jnp.where(inside, moved, empty))
        distance *= 2
    return values


def pick(side, first, second):
    return jnp.where(side == 0, first, second)


def fold_rows(values):
    rows, lanes = values.shape
    return jnp.sum(values.reshape(rows // 8, 8, lanes), axis=0)


def cell_kernel(
    head_dim,
    begin,
    end,
    side_ref,
    seats_ref,
    forget_ref,
    gates_own_ref,
    gates_other_ref,
    q_ref,
    k_ref,
    v_ref,
    conv_ref,
    upz_ref,
    flipped_ref,
    cot_own_ref,
    wd_ref,
    params_ref,
    *refs,
):
    length = q_ref.shape[0]
    final = end == length // block
    shares = 2 if begin else 1
    cot_other_refs, refs = refs[:shares], refs[shares:]
    if begin:
        refs = refs[9:]
    rows_ref, cols_ref, keep_ref, send_ref, dnum_ref, skip_grad_ref = refs[:6]
    upz_grad_ref, gated_t_ref, sums_ref, *refs = refs[6:]
    if final:
        first_ref, second_ref, gains_ref, *refs = refs
    states_ref, gateds_ref, nums_ref, dens_ref, slacks_ref = refs
    side = side_ref[0]
    length, channels = q_ref.shape
    heads = channels // head_dim
    gate_count = gates_own_ref.shape[0]
    all_heads = gate_count // 2
    part = cot_own_ref.shape[1]
    cot_rows = cot_other_refs[0].shape[0]
    if begin == 0:
        gates = gates_own_ref[...] + gates_other_ref[...]
        inlet = pick(side, gates[:heads], gates[heads : 2 * heads])
        forget = pick(
            side, gates[all_heads : all_heads + heads], gates[all_heads + heads : gate_count]
        )
        forget = forget + jnp.concatenate(
            [jnp.full((1, length), forget_ref[side * heads + h], f32) for h in range(heads)], axis=0
        )
        log_forget = jnp.minimum(forget, 0.0) - jnp.log1p(jnp.exp(-jnp.abs(forget)))
        total = scan_lanes(log_forget, jnp.add, 0.0)
        ahead = inlet - total
        top = scan_lanes(jnp.maximum(ahead, 0.0), jnp.maximum, 0.0)
        floor = jnp.exp(-(total + top))
        rows_ref[...] = jnp.concatenate(
            [ahead + jnp.log(f32(head_dim**-0.5)), top, forget, jnp.zeros_like(top)], axis=0
        )
        cols_ref[...] = jnp.concatenate([top, floor, top, floor], axis=0).T
        sums_ref[...] = jnp.zeros_like(sums_ref)

    ones = jnp.ones((length, 128), b16)

    def attend(count):
        span = count * block
        here = pl.ds(span - block, block)
        slot = count % 2
        start = span - block
        if start < cot_rows:
            other_rows = cot_other_refs[0][start : start + block, :]
        else:
            other_rows = cot_other_refs[1][start - cot_rows : start - cot_rows + block, :]
        num_ref, den_ref, state_ref, gated_ref, slack_ref = (
            ref.at[slot] for ref in (nums_ref, dens_ref, states_ref, gateds_ref, slacks_ref)
        )
        pieces = []
        for h in range(heads):
            lanes = pl.ds(h * head_dim, head_dim)
            start = span - block
            top = cols_ref[pl.ds(start, block), h : h + 1]
            scores = dot_nt(q_ref[pl.ds(start, block), lanes], k_ref[pl.ds(0, span), lanes])
            done = []
            for piece in range(count):
                there = slice(piece * block, (piece + 1) * block)
                exponent = rows_ref[h : h + 1, there] - top
                if piece == count - 1:
                    row_ids = lax.broadcasted_iota(jnp.int32, (block, block), 0)
                    col_ids = lax.broadcasted_iota(jnp.int32, (block, block), 1)
                    exponent = jnp.where(row_ids >= col_ids, exponent, -jnp.inf)
                done.append((scores[:, there] * jnp.exp(exponent)).astype(b16))
            pieces.append(jnp.concatenate(done, axis=1))
        for h in range(heads):
            lanes = pl.ds(h * head_dim, head_dim)
            num_ref[:, lanes] = dot_nn(pieces[h], v_ref[pl.ds(0, span), lanes])
            den_ref[:, pl.ds(h * 128, 128)] = dot_nn(pieces[h], ones[:span])
        state_ref[...] = dot_nt(cot_own_ref[here, :], wd_ref[:, side_cols(side, part)]) + dot_nt(
            other_rows, wd_ref[:, side_cols(1 - side, part)]
        )

        small = 64
        floors = cols_ref[here, heads : 2 * heads]

        def tiles():
            for h in range(heads):
                for start in range(0, block, small):
                    yield h, start, pl.ds(start, small), pl.ds(h * head_dim, head_dim)

        stats = {}
        for h, start, rows, lanes in tiles():
            denominator = den_ref[rows, h * 128 : h * 128 + 1]
            floor = floors[start : start + small, h : h + 1]
            inverse = 1.0 / jnp.maximum(jnp.abs(denominator), floor)
            hidden = num_ref[rows, lanes] * inverse
            num_ref[rows, lanes] = hidden
            stats[h, start] = [
                inverse,
                jnp.where(jnp.abs(denominator) >= floor, jnp.where(denominator >= 0.0, inverse, -inverse), 0.0),
                jnp.mean(hidden, axis=1, keepdims=True),
            ]
        for h, start, rows, lanes in tiles():
            centered = num_ref[rows, lanes] - stats[h, start][2]
            num_ref[rows, lanes] = centered
            stats[h, start].append(
                lax.rsqrt(jnp.mean(centered * centered, axis=1, keepdims=True) + eps_norm)
            )
        gain_sums = [jnp.zeros((8, head_dim), f32)] * heads
        skip_sums = [jnp.zeros((8, head_dim), f32)] * heads
        for h, start, rows, lanes in tiles():
            gain = params_ref[17:18, lanes].astype(f32)
            skip = params_ref[18:19, lanes].astype(f32)
            unit = num_ref[rows, lanes] * stats[h, start][3]
            num_ref[rows, lanes] = unit
            conv_out = conv_ref[pl.ds(span - block + start, small), lanes].astype(f32)
            inner = unit * gain + skip * conv_out
            upz = upz_ref[pl.ds(span - block + start, small), lanes].astype(f32)
            gate = sigmoid(upz)
            active = upz * gate
            gated_ref[rows, lanes] = (inner * active).astype(b16)
            grad_state = state_ref[rows, lanes]
            grad_inner = grad_state * active
            upz_grad_ref[pl.ds(span - block + start, small), lanes] = (
                grad_state * inner * (gate + active * (1.0 - gate))
            ).astype(b16)
            skip_grad_ref[pl.ds(span - block + start, small), lanes] = (grad_inner * skip).astype(b16)
            along = grad_inner * unit
            gain_sums[h] = gain_sums[h] + fold_rows(along)
            skip_sums[h] = skip_sums[h] + fold_rows(grad_inner * conv_out)
            grad_unit = grad_inner * gain
            state_ref[rows, lanes] = grad_unit
            stats[h, start] += [
                jnp.mean(grad_unit, axis=1, keepdims=True),
                jnp.mean(along * gain, axis=1, keepdims=True),
            ]
        for h, start, rows, lanes in tiles():
            inverse, signed, _, scale, mean, moment = stats[h, start]
            dnum_ref[pl.ds(span - block + start, small), lanes] = (
                (state_ref[rows, lanes] - mean - num_ref[rows, lanes] * moment) * (scale * inverse)
            ).astype(b16)
            slack = -signed * moment * (head_dim * eps_norm) * scale * scale
            slack_ref[rows, pl.ds(h * 128, 128)] = jnp.broadcast_to(slack, (small, 128))
        for h in range(heads):
            lanes = pl.ds(h * head_dim, head_dim)
            sums_ref[0:8, lanes] += gain_sums[h]
            sums_ref[8:16, lanes] += skip_sums[h]
        for h in range(heads):
            rows_ref[3 * heads + h : 3 * heads + h + 1, here] = slack_ref[:, pl.ds(h * 128, 128)].T[0:1]
        gated = gated_ref[...]
        keep_ref[here, :] = dot_nn(gated, wd_ref[:, side_cols(side, part)]).astype(b16)
        send_ref[here, :] = dot_nn(gated, wd_ref[:, side_cols(1 - side, part)]).astype(b16)
        seat_rows(gated.T, seats_ref, gated_t_ref.at[:, here])


    for count in range(begin + 1, end + 1):
        pl.when(side >= 0)(partial(attend, count))
    if not final:
        return
    gains_ref[0:1, :] = jnp.sum(sums_ref[0:8, :], axis=0, keepdims=True)
    gains_ref[1:2, :] = jnp.sum(sums_ref[8:16, :], axis=0, keepdims=True)
    gains_ref[2:8, :] = jnp.zeros((6, channels), f32)
    half = first_ref.shape[0]
    width = 2 * part
    for start in range(0, 2 * half, block):
        out_ref = (first_ref if start < half else second_ref).at[pl.ds(start % half, block), :]
        rows = pl.ds(start, block)
        turned = gated_t_ref[rows, :]
        out_ref[:, side_cols(side, part)] = dot_nn(turned, cot_own_ref[...]).astype(b16)
        out_ref[:, side_cols(1 - side, part)] = sum(
                dot_nn(gated_t_ref[rows, at : at + ref.shape[0]], ref[...])
                for at, ref in zip((0, cot_rows), cot_other_refs)
            ).astype(b16)
        out_ref[:, pl.ds(width, channels)] = dot_nn(
            flipped_ref[rows, :], upz_grad_ref[...]
        ).astype(b16)


def cell(
    side, seats, forget, gates_own, gates_other, q, k, v, conv, upz, flipped, cot_own, wd, params,
    cots_other, carried, head_dim, begin, end,
):
    length, channels = q.shape
    part = cot_own.shape[1]
    width = wd.shape[1]
    heads = channels // head_dim
    half = shape_of((length, part), b16)
    full = shape_of((length, channels), b16)
    shapes = [shape_of((8, length), f32), shape_of((length, 8), f32), half, half, full, full, full]
    shapes += [shape_of((channels, length), b16), shape_of((16, channels), f32)]
    aliases = {14 + len(cots_other) + at: at for at in range(len(carried))}
    if end == length // block:
        shapes += [shape_of((channels // 2, width + channels), b16)] * 2
        shapes += [shape_of((8, channels), f32)]
    return pl.pallas_call(
        partial(cell_kernel, head_dim, begin, end),
        in_specs=[smem()] * 3 + [vmem()] * (11 + len(cots_other) + len(carried)),
        out_specs=[vmem()] * len(shapes),
        out_shape=shapes,
        input_output_aliases=aliases,
        scratch_shapes=[
            pltpu.VMEM((2, block, channels), f32),
            pltpu.VMEM((2, block, channels), b16),
            pltpu.VMEM((2, block, channels), f32),
            pltpu.VMEM((2, block, heads * 128), f32),
            pltpu.VMEM((2, block, heads * 128), f32),
        ],
        compiler_params=roomy(16),
        cost_estimate=cost(10),
        name="cell",
    )(side, seats, forget, gates_own, gates_other, q, k, v, conv, upz, flipped, cot_own, wd, params,
      *cots_other, *carried)


def cell_back_kernel(
    h, heads, q_ref, k_ref, v_ref, dnum_ref, rows_ref, prior_ref, dq_ref, dk_ref, dv_ref, gates_ref,
    grads_ref, pair_ref,
):
    length, head_dim = dq_ref.shape
    lanes = pl.ds(h * head_dim, head_dim)
    gates_ref[...] = prior_ref[...]
    ahead = rows_ref[...].T[:, h : h + 1]
    row_ids = lax.broadcasted_iota(jnp.int32, (block, block), 0)
    col_ids = lax.broadcasted_iota(jnp.int32, (block, block), 1)
    blocks = length // block
    for s in range(blocks):
        there = pl.ds(s * block, block)
        span = length - s * block
        after = pl.ds(s * block, span)
        keys = k_ref[there, lanes]
        scores = dot_nt(keys, q_ref[after, lanes])
        grads = dot_nt(v_ref[there, lanes], dnum_ref[after, lanes])
        scored, graded = [], []
        for t in range(s, blocks):
            here = pl.ds(t * block, block)
            at = slice((t - s) * block, (t - s + 1) * block)
            exponent = ahead[s * block : (s + 1) * block] - rows_ref[heads + h : heads + h + 1, here]
            if s == t:
                exponent = jnp.where(row_ids <= col_ids, exponent, -jnp.inf)
            weight = jnp.exp(exponent)
            slack = rows_ref[3 * heads + h : 3 * heads + h + 1, here]
            scored.append((scores[:, at] * weight).astype(b16))
            graded.append(((grads[:, at] + slack) * weight).astype(b16))
            grads_ref[there, here] = graded[-1]
        dv_ref[there, :] = dot_nn(
            jnp.concatenate(scored, axis=1), dnum_ref[after, lanes]
        ).astype(b16)
        dk = dot_nn(jnp.concatenate(graded, axis=1), q_ref[after, lanes])
        dk_ref[there, :] = dk.astype(b16)
        pair_ref[there, 128:256] = jnp.broadcast_to(
            jnp.sum(dk * keys.astype(f32), axis=1, keepdims=True), (block, 128)
        )
    for t in range(blocks):
        here = pl.ds(t * block, block)
        before = pl.ds(0, (t + 1) * block)
        dq = dot_tn(grads_ref[before, here], k_ref[before, lanes])
        dq_ref[here, :] = dq.astype(b16)
        pair_ref[here, 0:128] = jnp.broadcast_to(
            jnp.sum(dq * q_ref[here, lanes].astype(f32), axis=1, keepdims=True), (block, 128)
        )
    outward = pair_ref[:, 0:128].T[0:1]
    inward = pair_ref[:, 128:256].T[0:1]
    forget = rows_ref[2 * heads + h : 2 * heads + h + 1, :]
    grad_log = scan_lanes(jnp.broadcast_to(outward - inward, (8, length)), jnp.add, 0.0, True)[0:1]
    gates_ref[h : h + 1, :] = inward
    gates_ref[heads + h : heads + h + 1, :] = grad_log * sigmoid(-forget)


def cell_back(q, k, v, dnum, rows, prior, h, head_dim):
    length, channels = q.shape
    heads = channels // head_dim
    full = shape_of((length, head_dim), b16)
    return pl.pallas_call(
        partial(cell_back_kernel, h, heads),
        in_specs=[vmem()] * 6,
        out_specs=[vmem()] * 4,
        out_shape=[full, full, full, shape_of((8, length), f32)],
        scratch_shapes=[pltpu.VMEM((length, length), b16), pltpu.VMEM((length, 256), f32)],
        compiler_params=roomy(16),
        cost_estimate=cost(7),
        name="cell_back",
    )(q, k, v, dnum, rows, prior)


def front_back_kernel(
    tap_count,
    heads,
    index,
    reseat,
    side_ref,
    table_ref,
    gates_own_ref,
    gates_other_ref,
    dq_ref,
    dk_ref,
    dv_ref,
    q_ref,
    k_ref,
    v_ref,
    conv_out_ref,
    slope_ref,
    upx_ref,
    skip_grad_ref,
    flipped_ref,
    params_ref,
    gate_ref,
    *refs,
):
    last = index == heads - 1
    if last:
        gains_ref, *refs = refs
        prior_refs, refs = refs[:index], refs[index:]
    upx_grad_ref, first_ref, second_ref, small_ref, padded_refs, turned_ref = refs
    side = side_ref[0]
    length, span = upx_grad_ref.shape
    own = gates_own_ref[...]
    other = gates_other_ref[...]
    gates = jnp.concatenate(
        [
            pick(side, own[:heads], other[:heads]),
            pick(side, other[:heads], own[:heads]),
            pick(side, own[heads : 2 * heads], other[heads : 2 * heads]),
            pick(side, other[heads : 2 * heads], own[heads : 2 * heads]),
        ],
        axis=0,
    )
    gates_t = gates.T.astype(b16)
    gates_b = gates.astype(b16)
    padded_refs[:, length : length + 8, :] = jnp.zeros((2, 8, group), f32)
    half = first_ref.shape[0]
    height = half // len(reseat)
    @pl.loop(0, span // group)
    def _(step):
        padded_ref = padded_refs.at[0]
        near = pl.ds(pl.multiple_of(step * group, group), group)
        lanes = pl.ds(pl.multiple_of(index * span + step * group, group), group)
        dq_b = (dq_ref[:, near].astype(f32) + dot_nn(gates_t, gate_ref[0, :, lanes])).astype(b16)
        dk_b = (dk_ref[:, near].astype(f32) + dot_nn(gates_t, gate_ref[1, :, lanes])).astype(b16)
        dv_b = (dv_ref[:, near].astype(f32) + dot_nn(gates_t, gate_ref[2, :, lanes])).astype(b16)
        conv_out = conv_out_ref[:, lanes]
        params = params_ref[:, lanes]
        upx_b = upx_ref[:, lanes]
        grad_conv = (
            skip_grad_ref[:, lanes].astype(f32)
            + dot_nt(dq_b, spread_taps(params[tap_count : 2 * tap_count]))
            + dot_nt(dk_b, spread_taps(params[2 * tap_count : 3 * tap_count]))
        )
        grad_pre = grad_conv * slope_ref[:, lanes].astype(f32)
        padded_ref[0:length, :] = grad_pre
        taps = params[0:tap_count].astype(f32)
        upx = upx_b.astype(f32)
        grad_upx = (
            dot_nt(dv_b, spread_taps(params[3 * tap_count : 4 * tap_count]))
            + taps[tap_count - 1 : tap_count] * grad_pre
        )
        tap_grads = [jnp.sum(upx * grad_pre, axis=0, keepdims=True)]
        for tap in range(tap_count - 2, -1, -1):
            moved = padded_ref[tap_count - 1 - tap : tap_count - 1 - tap + length, :]
            grad_upx = grad_upx + taps[tap : tap + 1] * moved
            tap_grads.insert(0, jnp.sum(upx * moved, axis=0, keepdims=True))
        grad_b = grad_upx.astype(b16)
        upx_grad_ref[:, near] = grad_b
        for start, out_ref in ((0, first_ref), (half, second_ref)):
            result = dot_nn(flipped_ref[start : start + half, :], grad_b).astype(b16)
            for seat, source in enumerate(reseat):
                out_ref[seat * height : (seat + 1) * height, near] = result[
                    source * height : (source + 1) * height
                ]
        small_ref[:, near] = jnp.concatenate(
            tap_grads
            + [
                gather_taps(dot_tn(conv_out, dq_b), tap_count),
                gather_taps(dot_tn(conv_out, dk_b), tap_count),
                gather_taps(dot_tn(upx_b, dv_b), tap_count),
                dot_nn(gates_b, q_ref[:, lanes]),
                dot_nn(gates_b, k_ref[:, lanes]),
                dot_nn(gates_b, v_ref[:, lanes]),
                jnp.broadcast_to(jnp.sum(gates, axis=1, keepdims=True), (gates.shape[0], group)),
                jnp.sum(grad_pre, axis=0, keepdims=True),
                jnp.zeros((7, group), f32),
            ],
            axis=0,
        )
    if last:
        small = jnp.concatenate([ref[...] for ref in (*prior_refs, small_ref)], axis=1)
        split = 4 * tap_count + 3 * gates.shape[0]
        stacked = jnp.concatenate(
            [
                small[:split],
                small[split + gates.shape[0] : split + gates.shape[0] + 1],
                gains_ref[0:2, :],
                jnp.zeros((128 - split - 3, small.shape[1]), f32),
            ],
            axis=0,
        )
        turned_ref[...] = stacked.T
        for seat in range(2 * len(reseat)):
            out_ref = first_ref if seat < len(reseat) else second_ref
            start = seat % len(reseat) * height
            out_ref[start : start + height, span : span + 128] = turned_ref[
                pl.ds(pl.multiple_of(table_ref[seat] * height, height), height), :
            ].astype(b16)


def front_back(
    side, table, gates_own, gates_other, dq, dk, dv, q, k, v, conv_out, slope, upx, skip_grad, flipped,
    params, gate, gains, priors, tap_count, heads, index, reseat,
):
    length, channels = q.shape
    width = flipped.shape[0]
    last = index == heads - 1
    span = channels // heads
    out_width = span + (128 if last else 0)
    extra = [gains, *priors] if last else []
    return pl.pallas_call(
        partial(front_back_kernel, tap_count, heads, index, reseat),
        in_specs=[smem(), smem()] + [vmem()] * (15 + len(extra)),
        out_specs=[vmem()] * 4,
        out_shape=[
            shape_of((length, span), b16),
            shape_of((width // 2, out_width), b16),
            shape_of((width // 2, out_width), b16),
            shape_of((56, span), f32),
        ],
        scratch_shapes=[
            pltpu.VMEM((2, length + 8, group), f32),
            pltpu.VMEM((channels, 128), f32),
        ],
        compiler_params=roomy(16),
        cost_estimate=cost(8),
        name="front_back",
    )(side, table, gates_own, gates_other, dq, dk, dv, q, k, v, conv_out, slope, upx, skip_grad,
      flipped, params, gate, *extra)


def norm_back_kernel(
    parts, side_ref, upz_grad_ref, wx_ref, wz_ref, unit_own_ref, unit_other_ref, gain_own_ref,
    gain_other_ref, *refs,
):
    upx_grad_refs = refs[:parts]
    keep_ref, send_ref, stats_ref = refs[parts:]
    side = side_ref[0]
    length, part = unit_own_ref.shape
    gain_sums = [jnp.zeros((8, part), f32)] * 2
    for start in range(0, length, block):
        here = pl.ds(start, block)
        sums = []
        for index, (unit_ref, place, gain_ref, out_ref) in enumerate(
            [
                (unit_own_ref, side, gain_own_ref, keep_ref),
                (unit_other_ref, 1 - side, gain_other_ref, send_ref),
            ]
        ):
            rows = side_cols(place, part)
            terms = dot_nt(upz_grad_ref[here, :], wz_ref[rows, :])
            for index_part, grad_ref in enumerate(upx_grad_refs):
                span = grad_ref.shape[1]
                lanes = pl.ds(index_part * span, span)
                terms = terms + dot_nt(grad_ref[here, :], wx_ref[rows, lanes])
            out_ref[here, :] = terms.astype(b16)
            along = terms * unit_ref[here, :].astype(f32)
            gain_sums[index] = gain_sums[index] + fold_rows(along)
            gain = gain_ref[...].astype(f32)
            sums.append(
                (
                    jnp.sum(terms * gain, axis=1, keepdims=True),
                    jnp.sum(along * gain, axis=1, keepdims=True),
                )
            )
        for row in range(2):
            stats_ref[row : row + 1, here] = jnp.broadcast_to(
                sums[0][row] + sums[1][row], (block, 128)
            ).T[0:1]
    stats_ref[2:8, :] = jnp.zeros((6, length), f32)
    for row, total in ((2, gain_sums[1]), (3, gain_sums[0])):
        stats_ref[row : row + 1, 0:part] = jnp.sum(total, axis=0, keepdims=True)


def norm_back(side, upx_grads, upz_grad, wx, wz, own, other, gain_own, gain_other):
    length, channels = upz_grad.shape
    parts = len(upx_grads)
    part = own.shape[1]
    return pl.pallas_call(
        partial(norm_back_kernel, parts),
        in_specs=[smem()] + [vmem()] * (7 + parts),
        out_specs=[vmem()] * 3,
        out_shape=[
            shape_of((length, part), b16),
            shape_of((length, part), b16),
            shape_of((8, max(length, part)), f32),
        ],
        compiler_params=roomy(16),
        cost_estimate=cost(9),
        name="norm_back",
    )(side, upz_grad, wx, wz, own, other, gain_own, gain_other, *upx_grads)


def seat_back(table_ref, near_ref, far_ref, out_ref):
    pieces = table_ref.shape[0]
    height = out_ref.shape[0] // pieces
    for seat in range(pieces):
        source = near_ref if seat < pieces // 2 else far_ref
        start = seat % (pieces // 2) * height
        out_ref[pl.ds(pl.multiple_of(table_ref[seat] * height, height), height), :] = source[
            start : start + height, :
        ].astype(f32)


def place_rows(table, pair):
    near, far = pair
    half, width = near.shape
    source = spec((half, group), lambda c: (0, c))
    return pl.pallas_call(
        seat_back,
        grid=(width // group,),
        in_specs=[smem(), source, source],
        out_specs=spec((2 * half, group), lambda c: (0, c)),
        out_shape=shape_of((2 * half, width), f32),
        compiler_params=settings(16),
        cost_estimate=cost(3),
        name="place_rows",
    )(table, near, far)


def place_last_kernel(
    taps, gate_count, mixed_ref, far_table_ref, near_ref, far_ref, near_two_ref, far_two_ref,
    near_small_ref, far_small_ref, out_ref, conv_ref, q_ref, k_ref, v_ref, bias_ref, gain_ref,
    skip_ref, gate_ref, turned_ref,
):
    step = pl.program_id(0)
    middle = pl.num_programs(0) // 2

    @pl.when(step == 0)
    def _():
        seat_back(far_table_ref, near_small_ref, far_small_ref, turned_ref)
        flat = turned_ref[...].T
        for at, ref in enumerate((conv_ref, q_ref, k_ref, v_ref)):
            ref[...] = flat[at * taps : (at + 1) * taps]
        start = 4 * taps
        for part in range(3):
            gate_ref[part, :, :] = flat[start + part * gate_count : start + (part + 1) * gate_count]
        start += 3 * gate_count
        for at, ref in enumerate((bias_ref, gain_ref, skip_ref)):
            ref[...] = flat[start + at : start + at + 1]

    @pl.when(step < middle)
    def _():
        seat_back(mixed_ref, near_ref, far_ref, out_ref)

    @pl.when(step >= middle)
    def _():
        seat_back(far_table_ref, near_two_ref, far_two_ref, out_ref)


def place_last(mixed_table, far_table, pair, pair_two, taps, gate_count):
    half, width = pair[0].shape
    steps = width // group
    channels = 2 * half

    def source(first):
        return spec((half, group), lambda c: (0, jnp.clip(c - first, 0, steps - 1)))

    small = spec((half, 128), lambda c: (0, width // 128))
    row = shape_of((1, channels), f32)
    tap_rows = shape_of((taps, channels), f32)
    shapes = [tap_rows] * 4 + [row] * 3 + [shape_of((3, gate_count, channels), f32)]
    return pl.pallas_call(
        partial(place_last_kernel, taps, gate_count),
        grid=(2 * steps,),
        in_specs=[smem(), smem(), source(0), source(0), source(steps), source(steps), small, small],
        out_specs=[spec((2 * half, group), lambda c: (0, c))] + [whole(v.shape) for v in shapes],
        out_shape=[shape_of((2 * half, 2 * width), f32)] + shapes,
        scratch_shapes=[pltpu.VMEM((channels, 128), f32)],
        compiler_params=settings(16),
        cost_estimate=cost(5),
        name="place_last",
    )(mixed_table, far_table, *pair, *pair_two, *pair_two)


def finish_kernel(
    unit_ref, scales_ref, gain_ref, keep_ref, recv_ref, recv_two_ref, stats_own_ref, stats_other_ref,
    cot_ref, out_ref,
):
    length, part = unit_ref.shape
    width = 2 * part
    gain = gain_ref[...].astype(f32)
    for start in range(0, length, block):
        here = pl.ds(start, block)
        unit = unit_ref[here, :].astype(f32)
        scale = scales_ref[:, here].T[:, 0:1]
        stats = (stats_own_ref[:, here] + stats_other_ref[:, here]).T
        half = recv_ref.shape[0]
        got_ref, at = (recv_ref, start) if start < half else (recv_two_ref, start - half)
        terms = keep_ref[here, :].astype(f32) + got_ref[at : at + block, :].astype(f32)
        pulled = terms * gain - (stats[:, 0:1] + unit * stats[:, 1:2]) / width
        out_ref[here, :] = cot_ref[here, :].astype(f32) + pulled * scale


def finish(unit, scales, gain, keep, recv, recv_two, stats_own, stats_other, cot):
    return pl.pallas_call(
        finish_kernel,
        in_specs=[vmem()] * 9,
        out_specs=vmem(),
        out_shape=shape_of(unit.shape, f32),
        compiler_params=roomy(16),
        cost_estimate=cost(4),
        name="finish",
    )(unit, scales, gain, keep, recv, recv_two, stats_own, stats_other, cot)


def swap(values):
    return lax.ppermute(values, "head", [(0, 1), (1, 0)])


def across(values, bit, count):
    return lax.ppermute(values, "dp", [(i, i ^ (1 << bit)) for i in range(count)])


def add_halves(first, second):
    return (first.astype(f32) + second.astype(f32)).astype(first.dtype)


class Reduction:
    def __init__(self, keep, out, order, bits, count, step=0):
        self.keep, self.out, self.count = keep, out, count
        self.plan = (
            [("half", bit) for bit in order]
            + [("full", bit) for bit in range(len(order), bits)]
            + [("copy", bit) for bit in reversed(order)]
        )
        self.step = step
        self.result = None

    def send(self):
        if not self.more():
            return None
        self.got = across(self.keep if self.out is None else self.out, self.plan[self.step][1], self.count)
        return self.got

    def take(self, got=None):
        if not self.more():
            return
        got = self.got if got is None else got
        kind, bit = self.plan[self.step]
        self.step += 1
        after = self.plan[self.step][0] if self.step < len(self.plan) else "end"
        if kind == "copy":
            if after == "end":
                self.result = (self.keep, got)
            else:
                self.keep = jnp.concatenate([self.keep, got], axis=0)
                self.out = None
        elif after == "half":
            half = self.keep.shape[0] // 2
            self.out = add_halves(self.keep[half:], got[half:])
            self.keep = add_halves(self.keep[:half], got[:half])
        else:
            self.keep = add_halves(self.keep, got)
            self.out = None

    def more(self):
        return self.step < len(self.plan)


def arrange(order, place):
    levels = len(order)
    return sum((((place >> bit) & 1) << (levels - 1 - at)) for at, bit in enumerate(order))


def settle(value, *flows):
    flows = [flow for flow in flows if flow.more()]
    value, gots = lax.optimization_barrier((value, [flow.got for flow in flows]))
    for flow, got in zip(flows, gots):
        flow.take(got)
    held = [(flow.keep, flow.out, flow.result) for flow in flows]
    value, held = lax.optimization_barrier((value, held))
    for flow, (keep, out, result) in zip(flows, held):
        flow.keep, flow.out, flow.result = keep, out, result
    return value


def send_all(flows):
    for flow in flows:
        flow.send()


def on_device(
    layer_input,
    ln_gain,
    up_x_weight,
    up_z_weight,
    conv_weight,
    conv_bias,
    query_weight,
    key_weight,
    value_weight,
    gate_weight,
    forget_bias,
    norm_gain,
    skip_gain,
    down_weight,
    cotangent,
):
    head_index = lax.axis_index("head")
    place = lax.axis_index("dp")
    count = lax.axis_size("dp")
    side = head_index.astype(jnp.int32).reshape(1)
    length, part = layer_input.shape
    channels = up_x_weight.shape[1]
    all_heads = gate_weight.shape[2] // 2
    heads = all_heads // lax.axis_size("head")
    head_dim = channels // heads
    taps = conv_weight.shape[0]
    bits = count.bit_length() - 1
    levels = min(bits, 4)
    near_order = list(range(levels))
    far_order = near_order[:1] + near_order[2:3] + near_order[1:2] + near_order[3:]
    pieces = 2**levels
    turned = [0] * pieces
    for relative in range(pieces):
        turned[arrange(near_order, relative)] = arrange(far_order, relative)
    seats = jnp.arange(pieces, dtype=jnp.int32)
    near_table = (seats ^ arrange(near_order, place)).astype(jnp.int32)
    far_table = (seats ^ arrange(far_order, place)).astype(jnp.int32)
    mixed_table = (jnp.array(turned, jnp.int32) ^ arrange(far_order, place)).astype(jnp.int32)
    middle = max(pieces // 2, 1)
    straight = list(range(middle))
    mixed = [turned[seat] for seat in range(middle)]

    gain_own = ln_gain.reshape(1, part)
    gain_other = swap(gain_own)
    input_other = swap(layer_input)
    gate_t = gate_weight.transpose(0, 2, 1)
    input_v, wx_v, wz_v, wd_v, cot_v, params = stage(
        [layer_input, up_x_weight, up_z_weight, down_weight, cotangent],
        [conv_weight, query_weight, key_weight, value_weight]
        + [values.reshape(1, channels) for values in (conv_bias, norm_gain, skip_gain)],
    )
    blocks = length // block
    early_rows = (blocks - 1) * block if blocks > 1 else length
    cot_start, input_other, gain_other = lax.optimization_barrier(
        (cotangent[:early_rows], input_other, gain_other)
    )
    cots_other = [swap(cot_start)]
    normed, unit_own, unit_other, scales = norm(side, input_v, gain_own, gain_other, input_other)
    flipped, upx, upz, conv_out, slope, q, k, v, gates = front(
        side, far_table, normed, wx_v, wz_v, params, gate_t, taps
    )
    gates_other = swap(gates)
    cot_start, gates_own = lax.optimization_barrier((cotangent[early_rows:], gates))
    cot_late = swap(cot_start)
    carried = []
    for begin, end in ((0, blocks - 1), (blocks - 1, blocks)) if blocks > 1 else ((0, 1),):
        if begin:
            cots_other.append(cot_late)
        carried = cell(
            side, near_table, forget_bias.astype(f32), gates, gates_other, q, k, v, conv_out, upz,
            flipped, cot_v, wd_v, params, cots_other, carried, head_dim, begin, end,
        )
    rows, _, keep, send, dnum, skip_grad, upz_grad, _, _, early_keep, early_send, gains = carried
    width = down_weight.shape[1]
    done = dict(
        rows=rows, keep=keep, send=send, gains=gains, skip_grad=skip_grad, upz_grad=upz_grad
    )
    flows = {
        "a": Reduction(early_keep[:, :width], early_send[:, :width], near_order, bits, count),
        "b": Reduction(early_keep[:, width:], early_send[:, width:], far_order, bits, count),
    }
    grads, upx_grads, smalls = [], [], []

    def back_cell(index):
        prior = done["gate_grads"] if index else rows
        grads.append(cell_back(q, k, v, dnum, rows, prior, index, head_dim))
        done["gate_grads"] = grads[-1][3]
        return ["gate_grads"]

    def back_front(index, order, reseat):
        dq, dk, dv, _ = grads[index]
        upx_grad, late_keep, late_send, small = front_back(
            side, far_table, done["gate_grads"], done["gate_grads_other"], dq, dk, dv, q, k, v,
            conv_out, slope, upx, skip_grad, flipped, params, gate_t, gains, list(smalls), taps,
            heads, index, reseat,
        )
        smalls.append(small)
        flows["cd"[index]] = Reduction(late_keep, late_send, order, bits, count)
        done["upx_grad", index] = upx_grad
        return [("upx_grad", index)]

    def swap_gates():
        done["gate_grads_other"] = swap(done["gate_grads"])
        return ["gate_grads_other"]

    def add_output():
        done["layer_output"] = (
            layer_input.astype(f32) + keep.astype(f32) + done["down_other"].astype(f32)
        ).astype(b16)
        return ["layer_output"]

    def back_norm():
        done["terms"], done["terms_send"], done["stats"] = norm_back(
            side, [done["upx_grad", index] for index in range(heads)], upz_grad, up_x_weight,
            up_z_weight, unit_own, unit_other, gain_own, gain_other,
        )
        return ["terms", "terms_send", "stats"]

    def swap_stats():
        done["stats_other"] = swap(done["stats"])
        return ["stats_other"]

    def swap_terms(index):
        half = length // 2
        start = index * half
        done["terms_other", index] = swap(done["terms_send"][start : start + half])
        return [("terms_other", index)]

    def start_tiny():
        line = done["stats"][3, :part] + done["stats_other"][2, :part]
        tiny = jnp.concatenate([line, smalls[0][-12:-8, 0], jnp.zeros((124,), f32)])
        flows["t"] = Reduction(tiny.reshape(-1, 128), None, [], bits, count)
        return []

    def end_norm():
        done["input_grad"] = finish(
            unit_own, scales, gain_own, done["terms"], done["terms_other", 0],
            done["terms_other", 1], done["stats"], done["stats_other"], cotangent,
        )
        return ["input_grad"]

    def place_down():
        if flows["a"].result is not None:
            done["grad_down"] = place_rows(near_table, flows["a"].result)
            return ["grad_down"]
        return []

    def place_upz():
        if flows["b"].result is not None:
            done["grad_upz"] = place_rows(far_table, flows["b"].result)
            return ["grad_upz"]
        return []

    works = dict(
        cell0=partial(back_cell, 0),
        cell1=partial(back_cell, 1),
        gates=swap_gates,
        front0=partial(back_front, 0, near_order, mixed),
        front1=partial(back_front, 1, far_order, straight),
        output=add_output,
        norm=back_norm,
        stats=swap_stats,
        tiny=start_tiny,
        terms0=partial(swap_terms, 0),
        terms1=partial(swap_terms, 1),
        finish=end_norm,
        down=place_down,
        upz=place_upz,
        none=lambda: [],
    )
    plan = [
        ("ab", "cell0", "ab"),
        ("ab", "cell1", "ab"),
        ("", "gates", ""),
        ("ab", "front0+output", "ab"),
        ("abc", "front1", "c"),
        ("d", "none", "d"),
        ("cd", "norm", "abcd"),
        ("cdab", "stats", "cdab"),
        ("cdab", "terms0+tiny", "cdab"),
        ("cdabt", "terms1", "cdabt"),
        ("cdabt", "none", "cdabt"),
        ("cdabt", "finish+down+upz", "cdabt"),
    ]
    done["down_other"] = swap(send)
    sending = set()

    def run(sends, work, waits):
        for name in sends:
            if name in flows and flows[name].more() and name not in sending:
                flows[name].send()
                sending.add(name)
        names = []
        for one in work.split("+"):
            names += works[one]()
        ready = [name for name in waits if name in sending]
        held = settle([done[name] for name in names], *[flows[name] for name in ready])
        done.update(zip(names, held))
        sending.difference_update(ready)

    for step in plan:
        run(*step)
    while any(flow.more() for flow in flows.values()):
        run("cdabt", "none", "cdabt")
    for name, place_one in (("grad_down", place_down), ("grad_upz", place_upz)):
        if name not in done:
            place_one()
    grad_upx, conv_grad, q_grad, k_grad, v_grad, bias_grad, gain_grad, skip_sum, gate_grad = (
        place_last(
            mixed_table, far_table, flows["c"].result, flows["d"].result, taps, 2 * all_heads
        )
    )
    tiny = flows["t"].keep.reshape(-1)
    return (
        done["layer_output"],
        done["input_grad"],
        tiny[:part],
        grad_upx,
        done["grad_upz"],
        conv_grad,
        bias_grad.reshape(-1),
        q_grad,
        k_grad,
        v_grad,
        gate_grad.transpose(0, 2, 1),
        tiny[part : part + all_heads],
        gain_grad.reshape(-1),
        skip_sum.reshape(-1),
        done["grad_down"],
    )


def solution(mesh):
    in_specs = (
        P("dp", "head"),
        P("head"),
        P(None, "head"),
        P(None, "head"),
        P(None, "head"),
        P("head"),
        P(None, "head"),
        P(None, "head"),
        P(None, "head"),
        P(None, "head", None),
        P(),
        P("head"),
        P("head"),
        P("head", None),
        P("dp", "head"),
    )
    out_specs = (
        P("dp", "head"),
        P("dp", "head"),
        P("head"),
        P(None, "head"),
        P(None, "head"),
        P(None, "head"),
        P("head"),
        P(None, "head"),
        P(None, "head"),
        P(None, "head"),
        P(None, "head", None),
        P(),
        P("head"),
        P("head"),
        P("head", None),
    )
    return jax.shard_map(
        on_device, mesh=mesh, in_specs=in_specs, out_specs=out_specs, check_vma=False
    )
```

```python
from functools import partial

import jax
import jax.numpy as jnp
from jax import lax
from jax.experimental import pallas as pl
from jax.experimental.pallas import tpu as pltpu
from jax.sharding import PartitionSpec as P

eps_norm = 1e-05
group = 256
block = 256
b16 = jnp.bfloat16
f32 = jnp.float32


def dot_nn(first, second):
    return lax.dot_general(first, second, (((1,), (0,)), ((), ())), preferred_element_type=f32)


def dot_nt(first, second):
    return lax.dot_general(first, second, (((1,), (1,)), ((), ())), preferred_element_type=f32)


def dot_tn(first, second):
    return lax.dot_general(first, second, (((0,), (0,)), ((), ())), preferred_element_type=f32)


def sigmoid(values):
    return 0.5 * jnp.tanh(0.5 * values) + 0.5


def spec(shape, index_map):
    return pl.BlockSpec(shape, index_map)


def whole(shape):
    return pl.BlockSpec(shape, lambda *_: (0,) * len(shape))


def smem():
    return pl.BlockSpec(memory_space=pltpu.SMEM)


def shape_of(shape, dtype):
    return jax.ShapeDtypeStruct(shape, dtype)


def vmem():
    return pl.BlockSpec(memory_space=pltpu.VMEM)


def hbm():
    return pl.BlockSpec(memory_space=pltpu.HBM)


def roomy(mebibytes):
    return pltpu.CompilerParams(vmem_limit_bytes=mebibytes * 2**20)


def settings(mebibytes):
    return pltpu.CompilerParams(
        dimension_semantics=("arbitrary",), vmem_limit_bytes=mebibytes * 2**20
    )


def cost(micros):
    return pl.CostEstimate(
        flops=int(micros * 1.1e9), bytes_accessed=int(micros * 3.6e6), transcendentals=0
    )


def side_cols(side, width):
    return pl.ds(pl.multiple_of(side * width, width), width)


def spread_taps(taps):
    tap_count, width = taps.shape
    rows = lax.broadcasted_iota(jnp.int32, (width, width), 0) // tap_count
    cols = lax.broadcasted_iota(jnp.int32, (width, width), 1) // tap_count
    pair = jnp.concatenate([taps.astype(f32)] * (8 // tap_count), axis=0)
    full = jnp.concatenate([pair] * (width // 8), axis=0)
    return jnp.where(rows == cols, full, 0.0).astype(b16)


def gather_taps(dense, tap_count):
    width = dense.shape[0]
    rows = lax.broadcasted_iota(jnp.int32, (width, width), 0) // tap_count
    cols = lax.broadcasted_iota(jnp.int32, (width, width), 1) // tap_count
    kept = jnp.where(rows == cols, dense, 0.0)
    folded = jnp.sum(kept.reshape(width // 8, 8, width), axis=0)
    total = folded[:tap_count]
    for part in range(1, 8 // tap_count):
        total = total + folded[part * tap_count : (part + 1) * tap_count]
    return total


def row_stats(own, other):
    width = own.shape[1] + other.shape[1]
    total = jnp.sum(own, axis=1, keepdims=True) + jnp.sum(other, axis=1, keepdims=True)
    square = jnp.sum(own * own, axis=1, keepdims=True) + jnp.sum(
        other * other, axis=1, keepdims=True
    )
    center = total / width
    return center, lax.rsqrt(square / width - center * center + eps_norm)


def seat_rows(values, seats_ref, out_ref):
    seats = seats_ref.shape[0]
    height = values.shape[0] // seats
    for piece in range(seats):
        out_ref[pl.ds(pl.multiple_of(seats_ref[piece] * height, height), height), :] = values[
            piece * height : (piece + 1) * height
        ]


class Fetch:
    def __init__(self, sems):
        self.sems, self.copies = sems, []

    def __call__(self, source, target):
        copy = pltpu.make_async_copy(source, target, self.sems.at[len(self.copies)])
        copy.start()
        self.copies.append(copy)
        return copy


def buffers(*operands):
    return [pltpu.VMEM(value.shape, value.dtype) for value in operands]


def in_hbm(values):
    return pltpu.with_memory_space_constraint(values, pltpu.HBM)


def stage_kernel(count, taps_count, *refs):
    sources, smalls, targets = refs[:count], refs[count : count + 7], refs[count + 7 : 2 * count + 7]
    params_ref, sems = refs[2 * count + 7 :]
    fetch = Fetch(sems)
    for source, target in zip(sources, targets):
        fetch(source, target)
    rows = [ref[...].astype(f32) for ref in smalls]
    filled = sum(row.shape[0] for row in rows)
    rows.append(jnp.zeros((params_ref.shape[0] - filled, params_ref.shape[1]), f32))
    params_ref[...] = jnp.concatenate(rows, axis=0).astype(b16)
    for copy in fetch.copies:
        copy.wait()


def stage(arrays, smalls):
    count = len(arrays)
    params = shape_of((32, smalls[0].shape[1]), b16)
    return pl.pallas_call(
        partial(stage_kernel, count, smalls[0].shape[0]),
        in_specs=[hbm()] * count + [vmem()] * len(smalls),
        out_specs=[vmem()] * (count + 1),
        out_shape=[shape_of(value.shape, value.dtype) for value in arrays] + [params],
        scratch_shapes=[pltpu.SemaphoreType.DMA((count,))],
        compiler_params=roomy(16),
        cost_estimate=cost(4),
        name="stage",
    )(*[in_hbm(value) for value in arrays], *smalls)


def norm_kernel(
    side_ref, own_ref, gain_own_ref, gain_other_ref, other_ref, normed_ref, unit_own_ref,
    unit_other_ref, scales_ref,
):
    side = side_ref[0]
    length, part = own_ref.shape
    for start in range(0, length, block):
        rows = pl.ds(start, block)
        own = own_ref[rows, :].astype(f32)
        other = other_ref[rows, :].astype(f32)
        center, scale = row_stats(own, other)
        unit_own = (own - center) * scale
        unit_other = (other - center) * scale
        unit_own_ref[rows, :] = unit_own.astype(b16)
        unit_other_ref[rows, :] = unit_other.astype(b16)
        normed_ref[rows, side_cols(side, part)] = (
            unit_own * gain_own_ref[...].astype(f32)
        ).astype(b16)
        normed_ref[rows, side_cols(1 - side, part)] = (
            unit_other * gain_other_ref[...].astype(f32)
        ).astype(b16)
        scales_ref[:, rows] = jnp.broadcast_to(scale, (block, 128)).T[0:8]


def norm(side, own, gain_own, gain_other, other):
    length, part = own.shape
    half = shape_of((length, part), b16)
    return pl.pallas_call(
        norm_kernel,
        in_specs=[smem()] + [vmem()] * 4,
        out_specs=[vmem()] * 4,
        out_shape=[shape_of((length, 2 * part), b16), half, half, shape_of((8, length), f32)],
        compiler_params=roomy(16),
        cost_estimate=cost(4),
        name="norm",
    )(side, own, gain_own, gain_other, other)


def front_kernel(
    taps_count,
    side_ref,
    seats_ref,
    normed_ref,
    wx_ref,
    wz_ref,
    params_ref,
    gate_ref,
    flipped_ref,
    upx_ref,
    upz_ref,
    conv_out_ref,
    slope_ref,
    q_ref,
    k_ref,
    v_ref,
    gates_ref,
    padded_ref,
):
    side = side_ref[0]
    length = normed_ref.shape[0]
    channels = wx_ref.shape[1]
    tap_count = taps_count
    steps = channels // group
    padded_ref[0:8, :] = jnp.zeros((8, group), f32)
    flip_rows = length // steps
    gates_ref[...] = jnp.zeros_like(gates_ref)

    @pl.loop(0, steps)
    def _(step):
        lanes = pl.ds(pl.multiple_of(step * group, group), group)
        upx = dot_nn(normed_ref[...], wx_ref[:, lanes])
        upx_b = upx.astype(b16)
        upx_ref[:, lanes] = upx_b
        padded_ref[pl.ds(8, length), :] = upx
        upz_ref[:, lanes] = dot_nn(normed_ref[...], wz_ref[:, lanes]).astype(b16)
        params = params_ref[:, lanes]
        taps = params[0:tap_count].astype(f32)
        bias = params[4 * tap_count : 4 * tap_count + 1].astype(f32)
        pre = bias + taps[tap_count - 1 : tap_count] * upx
        for tap in range(tap_count - 1):
            pre = pre + taps[tap : tap + 1] * padded_ref[pl.ds(8 - (tap_count - 1 - tap), length), :]
        gate = sigmoid(pre)
        conv_out = pre * gate
        conv_b = conv_out.astype(b16)
        conv_out_ref[:, lanes] = conv_b
        slope_ref[:, lanes] = (gate + conv_out * (1.0 - gate)).astype(b16)
        conv_low = (conv_out - conv_b.astype(f32)).astype(b16)
        upx_low = (upx - upx_b.astype(f32)).astype(b16)
        qd, kd, vd = (
            spread_taps(params[at * tap_count : (at + 1) * tap_count]) for at in range(1, 4)
        )
        q_b = (dot_nn(conv_b, qd) + dot_nn(conv_low, qd)).astype(b16)
        k_b = (dot_nn(conv_b, kd) + dot_nn(conv_low, kd)).astype(b16)
        v_b = (dot_nn(upx_b, vd) + dot_nn(upx_low, vd)).astype(b16)
        q_ref[:, lanes] = q_b
        k_ref[:, lanes] = k_b
        v_ref[:, lanes] = v_b
        gates_ref[...] += (
            dot_nt(gate_ref[0, :, lanes], q_b)
            + dot_nt(gate_ref[1, :, lanes], k_b)
            + dot_nt(gate_ref[2, :, lanes], v_b)
        )
        rows = pl.ds(pl.multiple_of(step * flip_rows, flip_rows), flip_rows)
        seat_rows(normed_ref[rows, :].T, seats_ref, flipped_ref.at[:, rows])


def front(side, seats, normed, wx, wz, params, gate, taps_count):
    length = normed.shape[0]
    width, channels = wx.shape
    full = shape_of((length, channels), b16)
    return pl.pallas_call(
        partial(front_kernel, taps_count),
        in_specs=[smem(), smem()] + [vmem()] * 5,
        out_specs=[vmem()] * 9,
        out_shape=[shape_of((width, length), b16)]
        + [full] * 7
        + [shape_of((gate.shape[1], length), f32)],
        scratch_shapes=[pltpu.VMEM((length + 8, group), f32)],
        compiler_params=roomy(16),
        cost_estimate=cost(14),
        name="front",
    )(side, seats, normed, wx, wz, params, gate)


def scan_lanes(values, combine, empty, reverse=False):
    length = values.shape[1]
    lane = lax.broadcasted_iota(jnp.int32, values.shape, 1)
    distance = 1
    while distance < length:
        if reverse:
            moved = pltpu.roll(values, length - distance, 1)
            inside = lane < length - distance
        else:
            moved = pltpu.roll(values, distance, 1)
            inside = lane >= distance
        values = combine(values, jnp.where(inside, moved, empty))
        distance *= 2
    return values


def pick(side, first, second):
    return jnp.where(side == 0, first, second)


def fold_rows(values):
    rows, lanes = values.shape
    return jnp.sum(values.reshape(rows // 8, 8, lanes), axis=0)


def cell_kernel(
    head_dim,
    begin,
    end,
    side_ref,
    seats_ref,
    forget_ref,
    gates_own_ref,
    gates_other_ref,
    q_ref,
    k_ref,
    v_ref,
    conv_ref,
    upz_ref,
    flipped_ref,
    cot_own_ref,
    wd_ref,
    params_ref,
    *refs,
):
    length = q_ref.shape[0]
    final = end == length // block
    shares = 2 if begin else 1
    cot_other_refs, refs = refs[:shares], refs[shares:]
    if begin:
        refs = refs[9:]
    rows_ref, cols_ref, keep_ref, send_ref, dnum_ref, skip_grad_ref = refs[:6]
    upz_grad_ref, gated_t_ref, sums_ref, *refs = refs[6:]
    if final:
        first_ref, second_ref, gains_ref, *refs = refs
    states_ref, gateds_ref, nums_ref, dens_ref, slacks_ref = refs
    side = side_ref[0]
    length, channels = q_ref.shape
    heads = channels // head_dim
    gate_count = gates_own_ref.shape[0]
    all_heads = gate_count // 2
    part = cot_own_ref.shape[1]
    cot_rows = cot_other_refs[0].shape[0]
    if begin == 0:
        gates = gates_own_ref[...] + gates_other_ref[...]
        inlet = pick(side, gates[:heads], gates[heads : 2 * heads])
        forget = pick(
            side, gates[all_heads : all_heads + heads], gates[all_heads + heads : gate_count]
        )
        forget = forget + jnp.concatenate(
            [jnp.full((1, length), forget_ref[side * heads + h], f32) for h in range(heads)], axis=0
        )
        log_forget = jnp.minimum(forget, 0.0) - jnp.log1p(jnp.exp(-jnp.abs(forget)))
        total = scan_lanes(log_forget, jnp.add, 0.0)
        ahead = inlet - total
        top = scan_lanes(jnp.maximum(ahead, 0.0), jnp.maximum, 0.0)
        floor = jnp.exp(-(total + top))
        rows_ref[...] = jnp.concatenate(
            [ahead + jnp.log(f32(head_dim**-0.5)), top, forget, jnp.zeros_like(top)], axis=0
        )
        cols_ref[...] = jnp.concatenate([top, floor, top, floor], axis=0).T
        sums_ref[...] = jnp.zeros_like(sums_ref)

    ones = jnp.ones((length, 128), b16)

    def attend(count):
        span = count * block
        here = pl.ds(span - block, block)
        slot = count % 2
        start = span - block
        if start < cot_rows:
            other_rows = cot_other_refs[0][start : start + block, :]
        else:
            other_rows = cot_other_refs[1][start - cot_rows : start - cot_rows + block, :]
        num_ref, den_ref, state_ref, gated_ref, slack_ref = (
            ref.at[slot] for ref in (nums_ref, dens_ref, states_ref, gateds_ref, slacks_ref)
        )
        pieces = []
        for h in range(heads):
            lanes = pl.ds(h * head_dim, head_dim)
            start = span - block
            top = cols_ref[pl.ds(start, block), h : h + 1]
            scores = dot_nt(q_ref[pl.ds(start, block), lanes], k_ref[pl.ds(0, span), lanes])
            done = []
            for piece in range(count):
                there = slice(piece * block, (piece + 1) * block)
                exponent = rows_ref[h : h + 1, there] - top
                if piece == count - 1:
                    row_ids = lax.broadcasted_iota(jnp.int32, (block, block), 0)
                    col_ids = lax.broadcasted_iota(jnp.int32, (block, block), 1)
                    exponent = jnp.where(row_ids >= col_ids, exponent, -jnp.inf)
                done.append((scores[:, there] * jnp.exp(exponent)).astype(b16))
            pieces.append(jnp.concatenate(done, axis=1))
        for h in range(heads):
            lanes = pl.ds(h * head_dim, head_dim)
            num_ref[:, lanes] = dot_nn(pieces[h], v_ref[pl.ds(0, span), lanes])
            den_ref[:, pl.ds(h * 128, 128)] = dot_nn(pieces[h], ones[:span])
        state_ref[...] = dot_nt(cot_own_ref[here, :], wd_ref[:, side_cols(side, part)]) + dot_nt(
            other_rows, wd_ref[:, side_cols(1 - side, part)]
        )

        small = 64
        floors = cols_ref[here, heads : 2 * heads]

        def tiles():
            for h in range(heads):
                for start in range(0, block, small):
                    yield h, start, pl.ds(start, small), pl.ds(h * head_dim, head_dim)

        stats = {}
        for h, start, rows, lanes in tiles():
            denominator = den_ref[rows, h * 128 : h * 128 + 1]
            floor = floors[start : start + small, h : h + 1]
            inverse = 1.0 / jnp.maximum(jnp.abs(denominator), floor)
            hidden = num_ref[rows, lanes] * inverse
            num_ref[rows, lanes] = hidden
            stats[h, start] = [
                inverse,
                jnp.where(jnp.abs(denominator) >= floor, jnp.where(denominator >= 0.0, inverse, -inverse), 0.0),
                jnp.mean(hidden, axis=1, keepdims=True),
            ]
        for h, start, rows, lanes in tiles():
            centered = num_ref[rows, lanes] - stats[h, start][2]
            num_ref[rows, lanes] = centered
            stats[h, start].append(
                lax.rsqrt(jnp.mean(centered * centered, axis=1, keepdims=True) + eps_norm)
            )
        gain_sums = [jnp.zeros((8, head_dim), f32)] * heads
        skip_sums = [jnp.zeros((8, head_dim), f32)] * heads
        for h, start, rows, lanes in tiles():
            gain = params_ref[17:18, lanes].astype(f32)
            skip = params_ref[18:19, lanes].astype(f32)
            unit = num_ref[rows, lanes] * stats[h, start][3]
            num_ref[rows, lanes] = unit
            conv_out = conv_ref[pl.ds(span - block + start, small), lanes].astype(f32)
            inner = unit * gain + skip * conv_out
            upz = upz_ref[pl.ds(span - block + start, small), lanes].astype(f32)
            gate = sigmoid(upz)
            active = upz * gate
            gated_ref[rows, lanes] = (inner * active).astype(b16)
            grad_state = state_ref[rows, lanes]
            grad_inner = grad_state * active
            upz_grad_ref[pl.ds(span - block + start, small), lanes] = (
                grad_state * inner * (gate + active * (1.0 - gate))
            ).astype(b16)
            skip_grad_ref[pl.ds(span - block + start, small), lanes] = (grad_inner * skip).astype(b16)
            along = grad_inner * unit
            gain_sums[h] = gain_sums[h] + fold_rows(along)
            skip_sums[h] = skip_sums[h] + fold_rows(grad_inner * conv_out)
            grad_unit = grad_inner * gain
            state_ref[rows, lanes] = grad_unit
            stats[h, start] += [
                jnp.mean(grad_unit, axis=1, keepdims=True),
                jnp.mean(along * gain, axis=1, keepdims=True),
            ]
        for h, start, rows, lanes in tiles():
            inverse, signed, _, scale, mean, moment = stats[h, start]
            dnum_ref[pl.ds(span - block + start, small), lanes] = (
                (state_ref[rows, lanes] - mean - num_ref[rows, lanes] * moment) * (scale * inverse)
            ).astype(b16)
            slack = -signed * moment * (head_dim * eps_norm) * scale * scale
            slack_ref[rows, pl.ds(h * 128, 128)] = jnp.broadcast_to(slack, (small, 128))
        for h in range(heads):
            lanes = pl.ds(h * head_dim, head_dim)
            sums_ref[0:8, lanes] += gain_sums[h]
            sums_ref[8:16, lanes] += skip_sums[h]
        for h in range(heads):
            rows_ref[3 * heads + h : 3 * heads + h + 1, here] = slack_ref[:, pl.ds(h * 128, 128)].T[0:1]
        gated = gated_ref[...]
        keep_ref[here, :] = dot_nn(gated, wd_ref[:, side_cols(side, part)]).astype(b16)
        send_ref[here, :] = dot_nn(gated, wd_ref[:, side_cols(1 - side, part)]).astype(b16)
        seat_rows(gated.T, seats_ref, gated_t_ref.at[:, here])


    for count in range(begin + 1, end + 1):
        pl.when(side >= 0)(partial(attend, count))
    if not final:
        return
    gains_ref[0:1, :] = jnp.sum(sums_ref[0:8, :], axis=0, keepdims=True)
    gains_ref[1:2, :] = jnp.sum(sums_ref[8:16, :], axis=0, keepdims=True)
    gains_ref[2:8, :] = jnp.zeros((6, channels), f32)
    half = first_ref.shape[0]
    width = 2 * part
    for start in range(0, 2 * half, block):
        out_ref = (first_ref if start < half else second_ref).at[pl.ds(start % half, block), :]
        rows = pl.ds(start, block)
        turned = gated_t_ref[rows, :]
        out_ref[:, side_cols(side, part)] = dot_nn(turned, cot_own_ref[...]).astype(b16)
        out_ref[:, side_cols(1 - side, part)] = sum(
                dot_nn(gated_t_ref[rows, at : at + ref.shape[0]], ref[...])
                for at, ref in zip((0, cot_rows), cot_other_refs)
            ).astype(b16)
        out_ref[:, pl.ds(width, channels)] = dot_nn(
            flipped_ref[rows, :], upz_grad_ref[...]
        ).astype(b16)


def cell(
    side, seats, forget, gates_own, gates_other, q, k, v, conv, upz, flipped, cot_own, wd, params,
    cots_other, carried, head_dim, begin, end,
):
    length, channels = q.shape
    part = cot_own.shape[1]
    width = wd.shape[1]
    heads = channels // head_dim
    half = shape_of((length, part), b16)
    full = shape_of((length, channels), b16)
    shapes = [shape_of((8, length), f32), shape_of((length, 8), f32), half, half, full, full, full]
    shapes += [shape_of((channels, length), b16), shape_of((16, channels), f32)]
    aliases = {14 + len(cots_other) + at: at for at in range(len(carried))}
    if end == length // block:
        shapes += [shape_of((channels // 2, width + channels), b16)] * 2
        shapes += [shape_of((8, channels), f32)]
    return pl.pallas_call(
        partial(cell_kernel, head_dim, begin, end),
        in_specs=[smem()] * 3 + [vmem()] * (11 + len(cots_other) + len(carried)),
        out_specs=[vmem()] * len(shapes),
        out_shape=shapes,
        input_output_aliases=aliases,
        scratch_shapes=[
            pltpu.VMEM((2, block, channels), f32),
            pltpu.VMEM((2, block, channels), b16),
            pltpu.VMEM((2, block, channels), f32),
            pltpu.VMEM((2, block, heads * 128), f32),
            pltpu.VMEM((2, block, heads * 128), f32),
        ],
        compiler_params=roomy(16),
        cost_estimate=cost(10),
        name="cell",
    )(side, seats, forget, gates_own, gates_other, q, k, v, conv, upz, flipped, cot_own, wd, params,
      *cots_other, *carried)


def cell_back_kernel(
    h, heads, q_ref, k_ref, v_ref, dnum_ref, rows_ref, prior_ref, dq_ref, dk_ref, dv_ref, gates_ref,
    grads_ref, pair_ref,
):
    length, head_dim = dq_ref.shape
    lanes = pl.ds(h * head_dim, head_dim)
    gates_ref[...] = prior_ref[...]
    ahead = rows_ref[...].T[:, h : h + 1]
    row_ids = lax.broadcasted_iota(jnp.int32, (block, block), 0)
    col_ids = lax.broadcasted_iota(jnp.int32, (block, block), 1)
    blocks = length // block
    for s in range(blocks):
        there = pl.ds(s * block, block)
        span = length - s * block
        after = pl.ds(s * block, span)
        keys = k_ref[there, lanes]
        scores = dot_nt(keys, q_ref[after, lanes])
        grads = dot_nt(v_ref[there, lanes], dnum_ref[after, lanes])
        scored, graded = [], []
        for t in range(s, blocks):
            here = pl.ds(t * block, block)
            at = slice((t - s) * block, (t - s + 1) * block)
            exponent = ahead[s * block : (s + 1) * block] - rows_ref[heads + h : heads + h + 1, here]
            if s == t:
                exponent = jnp.where(row_ids <= col_ids, exponent, -jnp.inf)
            weight = jnp.exp(exponent)
            slack = rows_ref[3 * heads + h : 3 * heads + h + 1, here]
            scored.append((scores[:, at] * weight).astype(b16))
            graded.append(((grads[:, at] + slack) * weight).astype(b16))
            grads_ref[there, here] = graded[-1]
        dv_ref[there, :] = dot_nn(
            jnp.concatenate(scored, axis=1), dnum_ref[after, lanes]
        ).astype(b16)
        dk = dot_nn(jnp.concatenate(graded, axis=1), q_ref[after, lanes])
        dk_ref[there, :] = dk.astype(b16)
        pair_ref[there, 128:256] = jnp.broadcast_to(
            jnp.sum(dk * keys.astype(f32), axis=1, keepdims=True), (block, 128)
        )
    for t in range(blocks):
        here = pl.ds(t * block, block)
        before = pl.ds(0, (t + 1) * block)
        dq = dot_tn(grads_ref[before, here], k_ref[before, lanes])
        dq_ref[here, :] = dq.astype(b16)
        pair_ref[here, 0:128] = jnp.broadcast_to(
            jnp.sum(dq * q_ref[here, lanes].astype(f32), axis=1, keepdims=True), (block, 128)
        )
    outward = pair_ref[:, 0:128].T[0:1]
    inward = pair_ref[:, 128:256].T[0:1]
    forget = rows_ref[2 * heads + h : 2 * heads + h + 1, :]
    grad_log = scan_lanes(jnp.broadcast_to(outward - inward, (8, length)), jnp.add, 0.0, True)[0:1]
    gates_ref[h : h + 1, :] = inward
    gates_ref[heads + h : heads + h + 1, :] = grad_log * sigmoid(-forget)


def cell_back(q, k, v, dnum, rows, prior, h, head_dim):
    length, channels = q.shape
    heads = channels // head_dim
    full = shape_of((length, head_dim), b16)
    return pl.pallas_call(
        partial(cell_back_kernel, h, heads),
        in_specs=[vmem()] * 6,
        out_specs=[vmem()] * 4,
        out_shape=[full, full, full, shape_of((8, length), f32)],
        scratch_shapes=[pltpu.VMEM((length, length), b16), pltpu.VMEM((length, 256), f32)],
        compiler_params=roomy(16),
        cost_estimate=cost(7),
        name="cell_back",
    )(q, k, v, dnum, rows, prior)


def front_back_kernel(
    tap_count,
    heads,
    index,
    reseat,
    side_ref,
    table_ref,
    gates_own_ref,
    gates_other_ref,
    dq_ref,
    dk_ref,
    dv_ref,
    q_ref,
    k_ref,
    v_ref,
    conv_out_ref,
    slope_ref,
    upx_ref,
    skip_grad_ref,
    flipped_ref,
    params_ref,
    gate_ref,
    *refs,
):
    last = index == heads - 1
    if last:
        gains_ref, *refs = refs
        prior_refs, refs = refs[:index], refs[index:]
    upx_grad_ref, first_ref, second_ref, small_ref, padded_refs, turned_ref = refs
    side = side_ref[0]
    length, span = upx_grad_ref.shape
    own = gates_own_ref[...]
    other = gates_other_ref[...]
    gates = jnp.concatenate(
        [
            pick(side, own[:heads], other[:heads]),
            pick(side, other[:heads], own[:heads]),
            pick(side, own[heads : 2 * heads], other[heads : 2 * heads]),
            pick(side, other[heads : 2 * heads], own[heads : 2 * heads]),
        ],
        axis=0,
    )
    gates_t = gates.T.astype(b16)
    gates_b = gates.astype(b16)
    padded_refs[:, length : length + 8, :] = jnp.zeros((2, 8, group), f32)
    half = first_ref.shape[0]
    height = half // len(reseat)
    @pl.loop(0, span // group)
    def _(step):
        padded_ref = padded_refs.at[0]
        near = pl.ds(pl.multiple_of(step * group, group), group)
        lanes = pl.ds(pl.multiple_of(index * span + step * group, group), group)
        dq_b = (dq_ref[:, near].astype(f32) + dot_nn(gates_t, gate_ref[0, :, lanes])).astype(b16)
        dk_b = (dk_ref[:, near].astype(f32) + dot_nn(gates_t, gate_ref[1, :, lanes])).astype(b16)
        dv_b = (dv_ref[:, near].astype(f32) + dot_nn(gates_t, gate_ref[2, :, lanes])).astype(b16)
        conv_out = conv_out_ref[:, lanes]
        params = params_ref[:, lanes]
        upx_b = upx_ref[:, lanes]
        grad_conv = (
            skip_grad_ref[:, lanes].astype(f32)
            + dot_nt(dq_b, spread_taps(params[tap_count : 2 * tap_count]))
            + dot_nt(dk_b, spread_taps(params[2 * tap_count : 3 * tap_count]))
        )
        grad_pre = grad_conv * slope_ref[:, lanes].astype(f32)
        padded_ref[0:length, :] = grad_pre
        taps = params[0:tap_count].astype(f32)
        upx = upx_b.astype(f32)
        grad_upx = (
            dot_nt(dv_b, spread_taps(params[3 * tap_count : 4 * tap_count]))
            + taps[tap_count - 1 : tap_count] * grad_pre
        )
        tap_grads = [jnp.sum(upx * grad_pre, axis=0, keepdims=True)]
        for tap in range(tap_count - 2, -1, -1):
            moved = padded_ref[tap_count - 1 - tap : tap_count - 1 - tap + length, :]
            grad_upx = grad_upx + taps[tap : tap + 1] * moved
            tap_grads.insert(0, jnp.sum(upx * moved, axis=0, keepdims=True))
        grad_b = grad_upx.astype(b16)
        upx_grad_ref[:, near] = grad_b
        for start, out_ref in ((0, first_ref), (half, second_ref)):
            result = dot_nn(flipped_ref[start : start + half, :], grad_b).astype(b16)
            for seat, source in enumerate(reseat):
                out_ref[seat * height : (seat + 1) * height, near] = result[
                    source * height : (source + 1) * height
                ]
        small_ref[:, near] = jnp.concatenate(
            tap_grads
            + [
                gather_taps(dot_tn(conv_out, dq_b), tap_count),
                gather_taps(dot_tn(conv_out, dk_b), tap_count),
                gather_taps(dot_tn(upx_b, dv_b), tap_count),
                dot_nn(gates_b, q_ref[:, lanes]),
                dot_nn(gates_b, k_ref[:, lanes]),
                dot_nn(gates_b, v_ref[:, lanes]),
                jnp.broadcast_to(jnp.sum(gates, axis=1, keepdims=True), (gates.shape[0], group)),
                jnp.sum(grad_pre, axis=0, keepdims=True),
                jnp.zeros((7, group), f32),
            ],
            axis=0,
        )
    if last:
        small = jnp.concatenate([ref[...] for ref in (*prior_refs, small_ref)], axis=1)
        split = 4 * tap_count + 3 * gates.shape[0]
        stacked = jnp.concatenate(
            [
                small[:split],
                small[split + gates.shape[0] : split + gates.shape[0] + 1],
                gains_ref[0:2, :],
                jnp.zeros((128 - split - 3, small.shape[1]), f32),
            ],
            axis=0,
        )
        turned_ref[...] = stacked.T
        for seat in range(2 * len(reseat)):
            out_ref = first_ref if seat < len(reseat) else second_ref
            start = seat % len(reseat) * height
            out_ref[start : start + height, span : span + 128] = turned_ref[
                pl.ds(pl.multiple_of(table_ref[seat] * height, height), height), :
            ].astype(b16)


def front_back(
    side, table, gates_own, gates_other, dq, dk, dv, q, k, v, conv_out, slope, upx, skip_grad, flipped,
    params, gate, gains, priors, tap_count, heads, index, reseat,
):
    length, channels = q.shape
    width = flipped.shape[0]
    last = index == heads - 1
    span = channels // heads
    out_width = span + (128 if last else 0)
    extra = [gains, *priors] if last else []
    return pl.pallas_call(
        partial(front_back_kernel, tap_count, heads, index, reseat),
        in_specs=[smem(), smem()] + [vmem()] * (15 + len(extra)),
        out_specs=[vmem()] * 4,
        out_shape=[
            shape_of((length, span), b16),
            shape_of((width // 2, out_width), b16),
            shape_of((width // 2, out_width), b16),
            shape_of((56, span), f32),
        ],
        scratch_shapes=[
            pltpu.VMEM((2, length + 8, group), f32),
            pltpu.VMEM((channels, 128), f32),
        ],
        compiler_params=roomy(16),
        cost_estimate=cost(8),
        name="front_back",
    )(side, table, gates_own, gates_other, dq, dk, dv, q, k, v, conv_out, slope, upx, skip_grad,
      flipped, params, gate, *extra)


def norm_back_kernel(
    parts, side_ref, upz_grad_ref, wx_ref, wz_ref, unit_own_ref, unit_other_ref, gain_own_ref,
    gain_other_ref, *refs,
):
    upx_grad_refs = refs[:parts]
    keep_ref, send_ref, stats_ref = refs[parts:]
    side = side_ref[0]
    length, part = unit_own_ref.shape
    gain_sums = [jnp.zeros((8, part), f32)] * 2
    for start in range(0, length, block):
        here = pl.ds(start, block)
        sums = []
        for index, (unit_ref, place, gain_ref, out_ref) in enumerate(
            [
                (unit_own_ref, side, gain_own_ref, keep_ref),
                (unit_other_ref, 1 - side, gain_other_ref, send_ref),
            ]
        ):
            rows = side_cols(place, part)
            terms = dot_nt(upz_grad_ref[here, :], wz_ref[rows, :])
            for index_part, grad_ref in enumerate(upx_grad_refs):
                span = grad_ref.shape[1]
                lanes = pl.ds(index_part * span, span)
                terms = terms + dot_nt(grad_ref[here, :], wx_ref[rows, lanes])
            out_ref[here, :] = terms.astype(b16)
            along = terms * unit_ref[here, :].astype(f32)
            gain_sums[index] = gain_sums[index] + fold_rows(along)
            gain = gain_ref[...].astype(f32)
            sums.append(
                (
                    jnp.sum(terms * gain, axis=1, keepdims=True),
                    jnp.sum(along * gain, axis=1, keepdims=True),
                )
            )
        for row in range(2):
            stats_ref[row : row + 1, here] = jnp.broadcast_to(
                sums[0][row] + sums[1][row], (block, 128)
            ).T[0:1]
    stats_ref[2:8, :] = jnp.zeros((6, length), f32)
    for row, total in ((2, gain_sums[1]), (3, gain_sums[0])):
        stats_ref[row : row + 1, 0:part] = jnp.sum(total, axis=0, keepdims=True)


def norm_back(side, upx_grads, upz_grad, wx, wz, own, other, gain_own, gain_other):
    length, channels = upz_grad.shape
    parts = len(upx_grads)
    part = own.shape[1]
    return pl.pallas_call(
        partial(norm_back_kernel, parts),
        in_specs=[smem()] + [vmem()] * (7 + parts),
        out_specs=[vmem()] * 3,
        out_shape=[
            shape_of((length, part), b16),
            shape_of((length, part), b16),
            shape_of((8, max(length, part)), f32),
        ],
        compiler_params=roomy(16),
        cost_estimate=cost(9),
        name="norm_back",
    )(side, upz_grad, wx, wz, own, other, gain_own, gain_other, *upx_grads)


def seat_back(table_ref, near_ref, far_ref, out_ref):
    pieces = table_ref.shape[0]
    height = out_ref.shape[0] // pieces
    for seat in range(pieces):
        source = near_ref if seat < pieces // 2 else far_ref
        start = seat % (pieces // 2) * height
        out_ref[pl.ds(pl.multiple_of(table_ref[seat] * height, height), height), :] = source[
            start : start + height, :
        ].astype(f32)


def place_rows(table, pair):
    near, far = pair
    half, width = near.shape
    source = spec((half, group), lambda c: (0, c))
    return pl.pallas_call(
        seat_back,
        grid=(width // group,),
        in_specs=[smem(), source, source],
        out_specs=spec((2 * half, group), lambda c: (0, c)),
        out_shape=shape_of((2 * half, width), f32),
        compiler_params=settings(16),
        cost_estimate=cost(3),
        name="place_rows",
    )(table, near, far)


def place_last_kernel(
    taps, gate_count, mixed_ref, far_table_ref, near_ref, far_ref, near_two_ref, far_two_ref,
    near_small_ref, far_small_ref, out_ref, conv_ref, q_ref, k_ref, v_ref, bias_ref, gain_ref,
    skip_ref, gate_ref, turned_ref,
):
    step = pl.program_id(0)
    middle = pl.num_programs(0) // 2

    @pl.when(step == 1)
    def _():
        seat_back(far_table_ref, near_small_ref, far_small_ref, turned_ref)
        flat = turned_ref[...].T
        for at, ref in enumerate((conv_ref, q_ref, k_ref, v_ref)):
            ref[...] = flat[at * taps : (at + 1) * taps]
        start = 4 * taps
        for part in range(3):
            gate_ref[part, :, :] = flat[start + part * gate_count : start + (part + 1) * gate_count]
        start += 3 * gate_count
        for at, ref in enumerate((bias_ref, gain_ref, skip_ref)):
            ref[...] = flat[start + at : start + at + 1]

    @pl.when(step < middle)
    def _():
        seat_back(mixed_ref, near_ref, far_ref, out_ref)

    @pl.when(step >= middle)
    def _():
        seat_back(far_table_ref, near_two_ref, far_two_ref, out_ref)


def place_last(mixed_table, far_table, pair, pair_two, taps, gate_count):
    half, width = pair[0].shape
    steps = width // group
    channels = 2 * half

    def source(first):
        return spec((half, group), lambda c: (0, jnp.clip(c - first, 0, steps - 1)))

    small = spec((half, 128), lambda c: (0, width // 128))
    row = shape_of((1, channels), f32)
    tap_rows = shape_of((taps, channels), f32)
    shapes = [tap_rows] * 4 + [row] * 3 + [shape_of((3, gate_count, channels), f32)]
    return pl.pallas_call(
        partial(place_last_kernel, taps, gate_count),
        grid=(2 * steps,),
        in_specs=[smem(), smem(), source(0), source(0), source(steps), source(steps), small, small],
        out_specs=[spec((2 * half, group), lambda c: (0, c))] + [whole(v.shape) for v in shapes],
        out_shape=[shape_of((2 * half, 2 * width), f32)] + shapes,
        scratch_shapes=[pltpu.VMEM((channels, 128), f32)],
        compiler_params=settings(16),
        cost_estimate=cost(5),
        name="place_last",
    )(mixed_table, far_table, *pair, *pair_two, *pair_two)


def finish_kernel(
    unit_ref, scales_ref, gain_ref, keep_ref, recv_ref, recv_two_ref, stats_own_ref, stats_other_ref,
    cot_ref, out_ref,
):
    length, part = unit_ref.shape
    width = 2 * part
    gain = gain_ref[...].astype(f32)
    for start in range(0, length, block):
        here = pl.ds(start, block)
        unit = unit_ref[here, :].astype(f32)
        scale = scales_ref[:, here].T[:, 0:1]
        stats = (stats_own_ref[:, here] + stats_other_ref[:, here]).T
        half = recv_ref.shape[0]
        got_ref, at = (recv_ref, start) if start < half else (recv_two_ref, start - half)
        terms = keep_ref[here, :].astype(f32) + got_ref[at : at + block, :].astype(f32)
        pulled = terms * gain - (stats[:, 0:1] + unit * stats[:, 1:2]) / width
        out_ref[here, :] = cot_ref[here, :].astype(f32) + pulled * scale


def finish(unit, scales, gain, keep, recv, recv_two, stats_own, stats_other, cot):
    return pl.pallas_call(
        finish_kernel,
        in_specs=[vmem()] * 9,
        out_specs=vmem(),
        out_shape=shape_of(unit.shape, f32),
        compiler_params=roomy(16),
        cost_estimate=cost(4),
        name="finish",
    )(unit, scales, gain, keep, recv, recv_two, stats_own, stats_other, cot)


def swap(values):
    return lax.ppermute(values, "head", [(0, 1), (1, 0)])


def across(values, bit, count):
    return lax.ppermute(values, "dp", [(i, i ^ (1 << bit)) for i in range(count)])


def add_halves(first, second):
    return (first.astype(f32) + second.astype(f32)).astype(first.dtype)


class Reduction:
    def __init__(self, keep, out, order, bits, count, step=0):
        self.keep, self.out, self.count = keep, out, count
        self.plan = (
            [("half", bit) for bit in order]
            + [("full", bit) for bit in range(len(order), bits)]
            + [("copy", bit) for bit in reversed(order)]
        )
        self.step = step
        self.result = None

    def send(self):
        if not self.more():
            return None
        self.got = across(self.keep if self.out is None else self.out, self.plan[self.step][1], self.count)
        return self.got

    def take(self, got=None):
        if not self.more():
            return
        got = self.got if got is None else got
        kind, bit = self.plan[self.step]
        self.step += 1
        after = self.plan[self.step][0] if self.step < len(self.plan) else "end"
        if kind == "copy":
            if after == "end":
                self.result = (self.keep, got)
            else:
                self.keep = jnp.concatenate([self.keep, got], axis=0)
                self.out = None
        elif after == "half":
            half = self.keep.shape[0] // 2
            self.out = add_halves(self.keep[half:], got[half:])
            self.keep = add_halves(self.keep[:half], got[:half])
        else:
            self.keep = add_halves(self.keep, got)
            self.out = None

    def more(self):
        return self.step < len(self.plan)


def arrange(order, place):
    levels = len(order)
    return sum((((place >> bit) & 1) << (levels - 1 - at)) for at, bit in enumerate(order))


def settle(value, *flows):
    flows = [flow for flow in flows if flow.more()]
    value, gots = lax.optimization_barrier((value, [flow.got for flow in flows]))
    for flow, got in zip(flows, gots):
        flow.take(got)
    held = [(flow.keep, flow.out, flow.result) for flow in flows]
    value, held = lax.optimization_barrier((value, held))
    for flow, (keep, out, result) in zip(flows, held):
        flow.keep, flow.out, flow.result = keep, out, result
    return value


def send_all(flows):
    for flow in flows:
        flow.send()


def on_device(
    layer_input,
    ln_gain,
    up_x_weight,
    up_z_weight,
    conv_weight,
    conv_bias,
    query_weight,
    key_weight,
    value_weight,
    gate_weight,
    forget_bias,
    norm_gain,
    skip_gain,
    down_weight,
    cotangent,
):
    head_index = lax.axis_index("head")
    place = lax.axis_index("dp")
    count = lax.axis_size("dp")
    side = head_index.astype(jnp.int32).reshape(1)
    length, part = layer_input.shape
    channels = up_x_weight.shape[1]
    all_heads = gate_weight.shape[2] // 2
    heads = all_heads // lax.axis_size("head")
    head_dim = channels // heads
    taps = conv_weight.shape[0]
    bits = count.bit_length() - 1
    levels = min(bits, 4)
    near_order = list(range(levels))
    far_order = near_order[:1] + near_order[2:3] + near_order[1:2] + near_order[3:]
    pieces = 2**levels
    turned = [0] * pieces
    for relative in range(pieces):
        turned[arrange(near_order, relative)] = arrange(far_order, relative)
    seats = jnp.arange(pieces, dtype=jnp.int32)
    near_table = (seats ^ arrange(near_order, place)).astype(jnp.int32)
    far_table = (seats ^ arrange(far_order, place)).astype(jnp.int32)
    mixed_table = (jnp.array(turned, jnp.int32) ^ arrange(far_order, place)).astype(jnp.int32)
    middle = max(pieces // 2, 1)
    straight = list(range(middle))
    mixed = [turned[seat] for seat in range(middle)]

    gain_own = ln_gain.reshape(1, part)
    gain_other = swap(gain_own)
    input_other = swap(layer_input)
    gate_t = gate_weight.transpose(0, 2, 1)
    input_v, wx_v, wz_v, wd_v, cot_v, params = stage(
        [layer_input, up_x_weight, up_z_weight, down_weight, cotangent],
        [conv_weight, query_weight, key_weight, value_weight]
        + [values.reshape(1, channels) for values in (conv_bias, norm_gain, skip_gain)],
    )
    blocks = length // block
    early_rows = (blocks - 1) * block if blocks > 1 else length
    cot_start, input_other, gain_other = lax.optimization_barrier(
        (cotangent[:early_rows], input_other, gain_other)
    )
    cots_other = [swap(cot_start)]
    normed, unit_own, unit_other, scales = norm(side, input_v, gain_own, gain_other, input_other)
    flipped, upx, upz, conv_out, slope, q, k, v, gates = front(
        side, far_table, normed, wx_v, wz_v, params, gate_t, taps
    )
    gates_other = swap(gates)
    cot_start, gates_own = lax.optimization_barrier((cotangent[early_rows:], gates))
    cot_late = swap(cot_start)
    carried = []
    for begin, end in ((0, blocks - 1), (blocks - 1, blocks)) if blocks > 1 else ((0, 1),):
        if begin:
            cots_other.append(cot_late)
        carried = cell(
            side, near_table, forget_bias.astype(f32), gates, gates_other, q, k, v, conv_out, upz,
            flipped, cot_v, wd_v, params, cots_other, carried, head_dim, begin, end,
        )
    rows, _, keep, send, dnum, skip_grad, upz_grad, _, _, early_keep, early_send, gains = carried
    width = down_weight.shape[1]
    done = dict(
        rows=rows, keep=keep, send=send, gains=gains, skip_grad=skip_grad, upz_grad=upz_grad
    )
    flows = {
        "a": Reduction(early_keep[:, :width], early_send[:, :width], near_order, bits, count),
        "b": Reduction(early_keep[:, width:], early_send[:, width:], far_order, bits, count),
    }
    grads, upx_grads, smalls = [], [], []

    def back_cell(index):
        prior = done["gate_grads"] if index else rows
        grads.append(cell_back(q, k, v, dnum, rows, prior, index, head_dim))
        done["gate_grads"] = grads[-1][3]
        return ["gate_grads"]

    def back_front(index, order, reseat):
        dq, dk, dv, _ = grads[index]
        upx_grad, late_keep, late_send, small = front_back(
            side, far_table, done["gate_grads"], done["gate_grads_other"], dq, dk, dv, q, k, v,
            conv_out, slope, upx, skip_grad, flipped, params, gate_t, gains, list(smalls), taps,
            heads, index, reseat,
        )
        smalls.append(small)
        flows["cd"[index]] = Reduction(late_keep, late_send, order, bits, count)
        done["upx_grad", index] = upx_grad
        return [("upx_grad", index)]

    def swap_gates():
        done["gate_grads_other"] = swap(done["gate_grads"])
        return ["gate_grads_other"]

    def add_output():
        done["layer_output"] = (
            layer_input.astype(f32) + keep.astype(f32) + done["down_other"].astype(f32)
        ).astype(b16)
        return ["layer_output"]

    def back_norm():
        done["terms"], done["terms_send"], done["stats"] = norm_back(
            side, [done["upx_grad", index] for index in range(heads)], upz_grad, up_x_weight,
            up_z_weight, unit_own, unit_other, gain_own, gain_other,
        )
        return ["terms", "terms_send", "stats"]

    def swap_stats():
        done["stats_other"] = swap(done["stats"])
        return ["stats_other"]

    def swap_terms(index):
        half = length // 2
        start = index * half
        done["terms_other", index] = swap(done["terms_send"][start : start + half])
        return [("terms_other", index)]

    def start_tiny():
        line = done["stats"][3, :part] + done["stats_other"][2, :part]
        tiny = jnp.concatenate([line, smalls[0][-12:-8, 0], jnp.zeros((124,), f32)])
        flows["t"] = Reduction(tiny.reshape(-1, 128), None, [], bits, count)
        return []

    def end_norm():
        done["input_grad"] = finish(
            unit_own, scales, gain_own, done["terms"], done["terms_other", 0],
            done["terms_other", 1], done["stats"], done["stats_other"], cotangent,
        )
        return ["input_grad"]

    def place_down():
        if flows["a"].result is not None:
            done["grad_down"] = place_rows(near_table, flows["a"].result)
            return ["grad_down"]
        return []

    def place_upz():
        if flows["b"].result is not None:
            done["grad_upz"] = place_rows(far_table, flows["b"].result)
            return ["grad_upz"]
        return []

    works = dict(
        cell0=partial(back_cell, 0),
        cell1=partial(back_cell, 1),
        gates=swap_gates,
        front0=partial(back_front, 0, near_order, mixed),
        front1=partial(back_front, 1, far_order, straight),
        output=add_output,
        norm=back_norm,
        stats=swap_stats,
        tiny=start_tiny,
        terms0=partial(swap_terms, 0),
        terms1=partial(swap_terms, 1),
        finish=end_norm,
        down=place_down,
        upz=place_upz,
        none=lambda: [],
    )
    plan = [
        ("ab", "cell0", "ab"),
        ("ab", "cell1", "ab"),
        ("", "gates", ""),
        ("ab", "front0", "ab"),
        ("abc", "front1", "c"),
        ("d", "output", "d"),
        ("cd", "norm", "abcd"),
        ("cdab", "stats", "cdab"),
        ("cdab", "terms0+tiny", "cdab"),
        ("cdabt", "terms1", "cdabt"),
        ("cdabt", "none", "cdabt"),
        ("cdabt", "finish+down+upz", "cdabt"),
    ]
    done["down_other"] = swap(send)
    sending = set()

    def run(sends, work, waits):
        for name in sends:
            if name in flows and flows[name].more() and name not in sending:
                flows[name].send()
                sending.add(name)
        names = []
        for one in work.split("+"):
            names += works[one]()
        ready = [name for name in waits if name in sending]
        held = settle([done[name] for name in names], *[flows[name] for name in ready])
        done.update(zip(names, held))
        sending.difference_update(ready)

    for step in plan:
        run(*step)
    while any(flow.more() for flow in flows.values()):
        run("cdabt", "none", "cdabt")
    for name, place_one in (("grad_down", place_down), ("grad_upz", place_upz)):
        if name not in done:
            place_one()
    grad_upx, conv_grad, q_grad, k_grad, v_grad, bias_grad, gain_grad, skip_sum, gate_grad = (
        place_last(
            mixed_table, far_table, flows["c"].result, flows["d"].result, taps, 2 * all_heads
        )
    )
    tiny = flows["t"].keep.reshape(-1)
    return (
        done["layer_output"],
        done["input_grad"],
        tiny[:part],
        grad_upx,
        done["grad_upz"],
        conv_grad,
        bias_grad.reshape(-1),
        q_grad,
        k_grad,
        v_grad,
        gate_grad.transpose(0, 2, 1),
        tiny[part : part + all_heads],
        gain_grad.reshape(-1),
        skip_sum.reshape(-1),
        done["grad_down"],
    )


def solution(mesh):
    in_specs = (
        P("dp", "head"),
        P("head"),
        P(None, "head"),
        P(None, "head"),
        P(None, "head"),
        P("head"),
        P(None, "head"),
        P(None, "head"),
        P(None, "head"),
        P(None, "head", None),
        P(),
        P("head"),
        P("head"),
        P("head", None),
        P("dp", "head"),
    )
    out_specs = (
        P("dp", "head"),
        P("dp", "head"),
        P("head"),
        P(None, "head"),
        P(None, "head"),
        P(None, "head"),
        P("head"),
        P(None, "head"),
        P(None, "head"),
        P(None, "head"),
        P(None, "head", None),
        P(),
        P("head"),
        P("head"),
        P("head", None),
    )
    return jax.shard_map(
        on_device, mesh=mesh, in_specs=in_specs, out_specs=out_specs, check_vma=False
    )
```
